32 devices in a mesh: group: 4 (over x, core), expert: 8 (over z, y).
Axes of the slice: x: 2, y: 2, z: 4, core: 2. Of those that a mesh axis runs over, the one named last changes fastest.
Arguments:
- out_grad: bfloat16 [8192, 3584], P(('group', 'expert')), may hold values from -6 to 6
- gates: float32 [8192, 8], P(('group', 'expert')), may hold values from 0.05 to 0.6
- routes: int32 [8192, 8], P(('group', 'expert')), may hold values from 0 to 23, all different within a row
- copy_pick: int32 [8192, 8], P(('group', 'expert')), may hold values from 0 to 839
- replica_plan: int32 [8], replicated, may hold values from 0 to 5, as said below
- down_weight: bfloat16 [8, 1024, 3584], P('expert'), as said below
- saved_hidden: bfloat16 [4, 8, 8, 80, 1024], P('group', 'expert'), may hold values from -0.75 to 0.75
Outputs:
- route_grad: float32 [8192, 8], P(('group', 'expert'))
- hidden_grad: bfloat16 [4, 8, 8, 80, 1024], P('group', 'expert')
- copy_grad: bfloat16 [8, 1024, 3584], P('expert', 'group')
The draws below stay inside these ranges and needn't reach their ends.
Inputs may be any that keep to these rules, and one draw needn't show every extreme that they name: `replica_plan`: every expert 0 to 5 is served by at least one slot; exactly 2 experts are served by more than one slot. `down_weight`: slots that serve the same expert hold equal weights.
All inputs are finite; a program needn't handle non-finite values.
Results may differ from the reference program's by a relative error of at most 0.019.
Values may be sent and summed in bfloat16 or wider, within the bound.
No kernel may reach another device: no remote copies, remote signals or barrier semaphores. Data moves between devices by JAX's collectives and lax.ppermute only.
A program may use at most 128 MiB of HBM per device.

```python
import jax
import jax.numpy as jnp
from jax import lax

D = 3584
F = 1024
K = 8
HOT = 2
TOK_DEV = 256
GROUPS = 4
SLOTS = 8
EXPERTS = 6
ALL_EXPERTS = 24
TOKENS = 8192
CAP = 80


def plan_table(key):
    extra_slots = SLOTS - EXPERTS
    key_hot, key_more, key_order = jax.random.split(jax.random.fold_in(key, 11), 3)
    hot_experts = jax.random.permutation(key_hot, EXPERTS)[:HOT].astype(jnp.int32)
    more_copies = jax.random.randint(key_more, (extra_slots - HOT,), 0, HOT)
    extras = jnp.concatenate([hot_experts, hot_experts[more_copies]])
    all_slots = jnp.concatenate([jnp.arange(EXPERTS, dtype=jnp.int32), extras])
    return jax.random.permutation(key_order, all_slots).astype(jnp.int32)


def draw_replica_plan(key, part):
    return plan_table(key)


def draw_down_weight(key, part):
    slot_plan = plan_table(key)
    weight_key = jax.random.fold_in(key, 23)
    logical = jnp.clip(jax.random.normal(weight_key, (EXPERTS, F, D), jnp.float32), -4.0, 4.0)
    logical = logical * D ** (-0.5)
    return logical[slot_plan].astype(jnp.bfloat16)


def with_ends(drawn, stream_key, least, high):
    longest = drawn.shape.index(max(drawn.shape))
    spots = []
    for shift in (0, 1):
        where = [jax.random.randint(jax.random.fold_in(stream_key, axis), (), 0, length) for axis, length in enumerate(drawn.shape)]
        where[longest] = (where[longest] + shift) % drawn.shape[longest]
        spots.append(tuple(where))
    return drawn.at[spots[0]].set(least).at[spots[1]].set(high)


def steps_of(rng, shape, cuts, least, largest):
    def one(axis_at, parts):
        draws = jax.random.uniform(jax.random.fold_in(jax.random.fold_in(rng, 6), axis_at), (parts,), jnp.float32, least / len(cuts), largest / len(cuts))
        return jnp.repeat(jnp.exp(draws), shape[axis_at] // parts).reshape((-1,) + (1,) * (len(shape) - axis_at - 1))

    gain = one(*cuts[0])
    for cut in cuts[1:]:
        gain = gain * one(*cut)
    return gain


def picks_of(stream_key, rows, count, top, lift):
    sequence = jax.random.permutation(jax.random.fold_in(stream_key, 1), count)
    favour = sequence
    for power in range(3):
        favour = favour * favour // count
    favour = favour * lift // count
    chance = jax.random.randint(jax.random.fold_in(stream_key, 2), (rows, count), 0, 4096) + favour
    holders = jax.random.permutation(jax.random.fold_in(stream_key, 3), rows)[jnp.arange(count) % rows]
    chance = jnp.where(jnp.arange(rows)[:, None] == holders[None, :], 1 << 14, chance)
    priority = chance * count + jnp.arange(count)
    return lax.top_k(priority.astype(jnp.int32), top)[1].astype(jnp.int32)


def normal_values(own_key, dims, deviation, most, shards=(), held_as=jnp.bfloat16):
    drawn = jax.random.normal(own_key, dims, jnp.float32) * deviation
    if len(shards) > 0:
        drawn = steps_of(own_key, dims, shards, -0.22, 0.18) * drawn
    return jnp.clip(drawn, min=-most, max=most).astype(held_as)


def setup_inputs(seed: int = 0) -> dict:
    seeds = jax.random.split(jax.random.key(seed), 8)
    out_grad = normal_values(seeds[0], (TOKENS, D), 1.0, 6.0, ((0, 32),))
    gates = jnp.clip(0.05 + 0.55 * jax.random.uniform(seeds[1], (TOKENS, K), jnp.float32) ** steps_of(seeds[1], (TOKENS, K), ((0, 32),), -0.2, 0.2), 0.05, 0.6)
    routes = picks_of(seeds[2], TOKENS, ALL_EXPERTS, K, 5461)
    copy_pick = with_ends(jax.random.randint(seeds[3], (TOKENS, K), 0, 840), jax.random.fold_in(seeds[3], 1), 0, 839).astype(jnp.int32)
    replica_plan = draw_replica_plan(jax.random.fold_in(seeds[7], 71), 0)
    down_weight = draw_down_weight(jax.random.fold_in(seeds[7], 71), 0)
    saved_hidden = normal_values(seeds[6], (GROUPS, SLOTS, SLOTS, CAP, F), 0.125, 0.75, ((0, 4), (1, 8)))
    return {"out_grad": out_grad, "gates": gates, "routes": routes, "copy_pick": copy_pick, "replica_plan": replica_plan, "down_weight": down_weight, "saved_hidden": saved_hidden}


def slot_layout(replica_plan):
    slot_count = replica_plan.shape[0]
    slot_ids = jnp.arange(slot_count, dtype=jnp.int32)
    same_expert = replica_plan[:, None] == replica_plan[None, :]
    earlier_slot = slot_ids[None, :] < slot_ids[:, None]
    ordinal = jnp.sum(same_expert & earlier_slot, axis=1).astype(jnp.int32)
    return slot_ids, same_expert, ordinal


def route_slots(routes, copy_pick, replica_plan, expert_count):
    slot_ids, same_expert, ordinal = slot_layout(replica_plan)
    serves = replica_plan == routes[..., None]
    copies = jnp.sum(serves, axis=-1).astype(jnp.int32)
    inside = routes < expert_count
    chosen = copy_pick % jnp.maximum(copies, 1)
    slot_match = serves & (ordinal == chosen[..., None]) & inside[..., None]
    slot_of = jnp.sum(jnp.where(slot_match, slot_ids, 0), axis=-1).astype(jnp.int32)
    return slot_match, slot_of, inside


def route_ranks(slot_match):
    onehot = slot_match.astype(jnp.int32)
    earlier = jnp.cumsum(onehot, axis=-2) - onehot
    return jnp.sum(earlier * onehot, axis=-1).astype(jnp.int32)


def reference(out_grad, gates, routes, copy_pick, replica_plan, down_weight, saved_hidden):
    slot_count = SLOTS
    per_group = slot_count * TOK_DEV * K
    held_count = slot_count * slot_count * CAP
    slot_match, slot_of, inside = route_slots(routes, copy_pick, replica_plan, EXPERTS)
    match_dev = slot_match.reshape(GROUPS * slot_count, TOK_DEV * K, slot_count)
    route_rank = route_ranks(match_dev).reshape(GROUPS, per_group)
    slot_group = slot_of.reshape(GROUPS, per_group)
    kept_route = inside.reshape(GROUPS, per_group) & (route_rank < CAP)
    route_ids = jnp.arange(per_group, dtype=jnp.int32)
    source_dev = route_ids // (TOK_DEV * K)
    position = (slot_group * slot_count + source_dev[None, :]) * CAP + route_rank
    position = jnp.where(kept_route, position, held_count).astype(jnp.int32)
    grad_groups = out_grad.reshape(GROUPS, slot_count * TOK_DEV, D)
    gate_groups = gates.reshape(GROUPS, per_group)
    hidden_groups = saved_hidden.reshape(GROUPS, slot_count, slot_count * CAP, F)
    _, same_expert, _ = slot_layout(replica_plan)

    def one_group(grad_total, group_items):
        grad_rows, gate_rows, place, kept, held_hidden = group_items
        source_route = jnp.full((held_count,), per_group, jnp.int32).at[place].set(route_ids, mode="drop")
        occupied = source_route < per_group
        safe_route = jnp.where(occupied, source_route, 0)
        grad_held = jnp.where(occupied[:, None], grad_rows[safe_route // K], 0).astype(jnp.bfloat16)
        gate_held = jnp.where(occupied, gate_rows[safe_route], 0.0).astype(jnp.bfloat16)
        grad_held = grad_held.reshape(slot_count, slot_count * CAP, D)
        gate_held = gate_held.reshape(slot_count, slot_count * CAP)

        def one_slot(inputs):
            slot_rows, slot_gate, slot_hidden, weight_mat = inputs
            projected = lax.dot_general(slot_rows, weight_mat, (((1,), (1,)), ((), ())), preferred_element_type=jnp.float32)
            gate_f = slot_gate.astype(jnp.float32)[:, None]
            slot_grad = (gate_f * projected).astype(jnp.bfloat16)
            route_score = jnp.sum(projected * slot_hidden.astype(jnp.float32), axis=1)
            scaled = (gate_f * slot_rows.astype(jnp.float32)).astype(jnp.bfloat16)
            partial_sum = lax.dot_general(slot_hidden, scaled, (((0,), (0,)), ((), ())), preferred_element_type=jnp.float32)
            return slot_grad, route_score, partial_sum.astype(jnp.bfloat16)

        slot_grad, route_score, partial_sum = lax.map(one_slot, (grad_held, gate_held, held_hidden, down_weight))
        score_flat = jnp.concatenate([route_score.reshape(-1), jnp.zeros((1,), jnp.float32)])
        group_grad = jnp.where(kept, score_flat[place], 0.0)
        grad_total = grad_total + lax.optimization_barrier(partial_sum).astype(jnp.float32)
        return grad_total, (slot_grad, group_grad)

    start_total = jnp.zeros((slot_count, F, D), jnp.float32)
    grad_total, outputs = lax.scan(one_group, start_total, (grad_groups, gate_groups, position, kept_route, hidden_groups))
    slot_grads, group_grads = outputs
    group_sum = lax.optimization_barrier(grad_total.astype(jnp.bfloat16)).astype(jnp.float32)
    copy_grad = jnp.einsum("st,tfd->sfd", same_expert.astype(jnp.float32), group_sum, precision=lax.Precision.HIGHEST).astype(jnp.bfloat16)
    route_grad = group_grads.reshape(TOKENS, K)
    hidden_grad = slot_grads.reshape(GROUPS, slot_count, slot_count, CAP, F)
    return route_grad, hidden_grad, copy_grad
```

```python
import functools
import itertools

import jax
import jax.numpy as jnp
import numpy as np
from jax import lax
from jax.experimental import pallas as pl
from jax.experimental.pallas import tpu as pltpu
from jax.sharding import PartitionSpec as P

HOT = 2
CHUNKS = (1024, 1024, 1024, 512)


def slot_layout(replica_plan):
    slot_count = replica_plan.shape[0]
    slot_ids = jnp.arange(slot_count, dtype=jnp.int32)
    same_expert = replica_plan[:, None] == replica_plan[None, :]
    earlier_slot = slot_ids[None, :] < slot_ids[:, None]
    ordinal = jnp.sum(same_expert & earlier_slot, axis=1)
    return (slot_ids, same_expert, ordinal)


def route_kernel(expert_count, cap_rows, plan_col, plan_row, routes, picks, gates, spread, rank_out, slot_out):
    slot_count = plan_col.shape[0]
    top_count, tokens = routes.shape
    plan = plan_col[...]
    same = plan == plan_row[...]
    slot_r = lax.broadcasted_iota(jnp.int32, (slot_count, slot_count), 0)
    slot_c = lax.broadcasted_iota(jnp.int32, (slot_count, slot_count), 1)
    copies = jnp.sum(jnp.where(same, 1.0, 0.0), axis=1, keepdims=True)
    ordinal = jnp.sum(jnp.where(same & (slot_c < slot_r), 1.0, 0.0), axis=1, keepdims=True)
    slot_ids = lax.broadcasted_iota(jnp.int32, (slot_count, tokens), 0)
    reach = jnp.zeros((slot_count, tokens), jnp.float32)
    gate_of = jnp.zeros((slot_count, tokens), jnp.float32)
    matches = []
    for k in range(top_count):
        route = routes[k : k + 1, :]
        pick = picks[k : k + 1, :].astype(jnp.float32)
        chosen = pick - copies * jnp.floor((pick + 0.5) / copies)
        match = (route == plan) & (chosen == ordinal) & (route < expert_count)
        matches.append(match)
        reach = jnp.where(match, 1.0, reach)
        gate_of = jnp.where(match, gates[k : k + 1, :], gate_of)
    before = lax.broadcasted_iota(jnp.int32, (tokens, tokens), 0) < lax.broadcasted_iota(
        jnp.int32, (tokens, tokens), 1
    )
    rank = lax.dot_general(
        reach.astype(jnp.bfloat16),
        jnp.where(before, 1.0, 0.0).astype(jnp.bfloat16),
        (((1,), (0,)), ((), ())),
        preferred_element_type=jnp.float32,
    ).astype(jnp.int32)
    kept = (reach > 0.0) & (rank < cap_rows)
    rank_out[...] = jnp.where(kept, rank, -1)
    for k in range(top_count):
        slot_out[k : k + 1, :] = (
            jnp.sum(jnp.where(matches[k] & kept, slot_ids + 1, 0), axis=0, keepdims=True) - 1
        )
    place = jnp.where(kept, slot_ids * cap_rows + rank, -1)
    held = slot_count * cap_rows
    block = 80 if held % 80 == 0 else held
    for start in range(0, held, block):
        row_ids = lax.broadcasted_iota(jnp.int32, (block, tokens), 0) + start
        total = jnp.zeros((block, tokens), jnp.float32)
        for s in range(start // cap_rows, -(-(start + block) // cap_rows)):
            total = jnp.where(row_ids == place[s : s + 1, :], gate_of[s : s + 1, :], total)
        spread[start : start + block, :] = total.astype(jnp.bfloat16)


def place_routes(routes, picks, gates, replica_plan, expert_count, cap_rows):
    slot_count = replica_plan.shape[0]
    top_count, tokens = routes.shape
    return pl.pallas_call(
        functools.partial(route_kernel, expert_count, cap_rows),
        out_shape=(
            jax.ShapeDtypeStruct((slot_count * cap_rows, tokens), jnp.bfloat16),
            jax.ShapeDtypeStruct((slot_count, tokens), jnp.int32),
            jax.ShapeDtypeStruct((top_count, tokens), jnp.int32),
        ),
    )(replica_plan.reshape(slot_count, 1), replica_plan.reshape(1, slot_count), routes, picks, gates)


def return_kernel(score, rank, slot_of, gates, out):
    slot_count, cap_rows = score.shape
    top_count, tokens = slot_of.shape
    row_ids = lax.broadcasted_iota(jnp.int32, (cap_rows, tokens), 0)
    total = jnp.zeros((top_count, tokens), jnp.float32)
    for s in range(slot_count):
        onehot = jnp.where(row_ids == rank[s : s + 1, :], 1.0, 0.0)
        value = lax.dot_general(
            score[s : s + 1, :],
            onehot,
            (((1,), (0,)), ((), ())),
            precision=lax.Precision.HIGHEST,
            preferred_element_type=jnp.float32,
        )
        total = jnp.where(slot_of[...] == s, value, total)
    held_gate = gates[...].astype(jnp.bfloat16).astype(jnp.float32)
    out[...] = jnp.where(slot_of[...] >= 0, total / held_gate, 0.0)


def matchings(slot_count):
    first = np.zeros((1 << slot_count,), np.int32)
    perms = []
    for four in itertools.combinations(range(slot_count), 4):
        first[sum(1 << s for s in four)] = len(perms)
        for other in range(3):
            rest = [four[1 + i] for i in range(3) if i != other]
            pairs = ((four[0], four[1 + other]), tuple(rest))
            perms.append([(a, b) for a, b in pairs] + [(b, a) for a, b in pairs])
    return first, perms


def matching_index(replica_plan, first):
    slot_ids, same_expert, ordinal = slot_layout(replica_plan)
    hot = jnp.sum(same_expert, axis=1) > 1
    mask = jnp.sum(jnp.where(hot, 1 << slot_ids, 0))
    least = jnp.min(jnp.where(hot, slot_ids, slot_ids.shape[0]))
    expert = jnp.sum(jnp.where(slot_ids == least, replica_plan, 0))
    partner = jnp.max(jnp.where(replica_plan == expert, slot_ids, 0))
    between = jnp.sum(hot & (slot_ids > least) & (slot_ids < partner))
    base = jnp.sum(jnp.where(jnp.arange(first.shape[0]) == mask, jnp.asarray(first), 0))
    return base + between


def sum_copies_any(group_sum, replica_plan):
    slot_ids, same_expert, ordinal = slot_layout(replica_plan)
    copies = jnp.sum(same_expert, axis=1)
    hot_first = (copies > 1) & (ordinal == 0)
    hot_rank = jnp.sum(hot_first[None, :] & (replica_plan[None, :] < replica_plan[:, None]), axis=1)
    my_slot = slot_ids == lax.axis_index("expert")
    my_rank = jnp.sum(jnp.where(my_slot, hot_rank, 0))
    my_hot = jnp.any(my_slot & (copies > 1))
    place_hot = (jnp.arange(HOT, dtype=jnp.int32) == my_rank) & my_hot
    group_f = group_sum.astype(jnp.float32)
    table = jnp.where(place_hot[:, None, None], group_f[None], 0.0)
    summed = lax.psum(table.astype(jnp.bfloat16), "expert").astype(jnp.float32)
    picked = jnp.sum(jnp.where(place_hot[:, None, None], summed, 0.0), axis=0)
    return jnp.where(my_hot, picked, group_f).astype(jnp.bfloat16)


def local(out_grad, gates, routes, copy_pick, replica_plan, down_weight, saved_hidden):
    slot_count = replica_plan.shape[0]
    cap_rows = saved_hidden.shape[3]
    expert_count = slot_count - slot_count // 4
    model_width = out_grad.shape[1]
    hidden_units = down_weight.shape[1]
    held_count = slot_count * cap_rows
    group_size = lax.axis_size("group")
    chips = group_size // 2
    shard_rows = hidden_units // group_size
    me = lax.axis_index("group")
    chip, core = me // 2, me % 2

    spread, rank, slot_of = place_routes(
        routes.T, copy_pick.T, gates.T, replica_plan, expert_count, cap_rows
    )
    edges = np.cumsum((0,) + CHUNKS)
    spans = [(int(a), int(b)) for a, b in zip(edges[:-1], edges[1:])]
    arrived = []
    for a, b in spans:
        rows = jnp.dot(spread, out_grad[:, a:b], preferred_element_type=jnp.float32).astype(jnp.bfloat16)
        got = lax.all_to_all(
            rows.reshape(slot_count, cap_rows, b - a), "expert", split_axis=0, concat_axis=0, tiled=True
        )
        arrived.append(got.reshape(held_count, b - a))

    held_hidden = saved_hidden.reshape(held_count, hidden_units)
    by_owner = held_hidden.T.reshape(chips, 2, shard_rows, held_count)
    by_owner = jnp.stack([by_owner[chip ^ d] for d in range(chips)])
    stay = lax.optimization_barrier(by_owner[:, core].reshape(-1, held_count))
    leave = lax.optimization_barrier(by_owner[:, 1 - core].reshape(-1, held_count))

    projected = jnp.zeros((held_count, hidden_units), jnp.float32)
    group_sum = []
    for (a, b), rows in zip(spans, arrived):
        away = jnp.dot(leave, rows, preferred_element_type=jnp.float32).astype(jnp.bfloat16)
        near = lax.ppermute(away, "group", [(i, i ^ 1) for i in range(group_size)])
        total = jnp.dot(stay, rows, preferred_element_type=jnp.float32) + near.astype(jnp.float32)
        total = total.reshape(chips, shard_rows, b - a)
        mine = total[0]
        for d in range(1, chips):
            far = lax.ppermute(
                total[d].astype(jnp.bfloat16), "group", [(i, i ^ (2 * d)) for i in range(group_size)]
            )
            mine = mine + far.astype(jnp.float32)
        group_sum.append(mine.astype(jnp.bfloat16))
        projected = projected + lax.dot_general(
            rows, down_weight[0, :, a:b], (((1,), (1,)), ((), ())), preferred_element_type=jnp.float32
        )

    hidden_grad = projected.astype(jnp.bfloat16)
    route_score = jnp.sum(projected * held_hidden.astype(jnp.float32), axis=1)
    returned = lax.all_to_all(
        route_score.reshape(slot_count, cap_rows), "expert", split_axis=0, concat_axis=0, tiled=True
    )
    route_grad = pl.pallas_call(
        return_kernel, out_shape=jax.ShapeDtypeStruct(gates.T.shape, jnp.float32)
    )(returned, rank, slot_of, gates.T).T

    group_sum = jnp.concatenate(group_sum, axis=1)
    if slot_count - expert_count == HOT:
        first, perms = matchings(slot_count)
        other = lax.switch(
            matching_index(replica_plan, first),
            [functools.partial(lax.ppermute, axis_name="expert", perm=perm) for perm in perms],
            group_sum,
        )
        copy_grad = (group_sum.astype(jnp.float32) + other.astype(jnp.float32)).astype(jnp.bfloat16)
    else:
        copy_grad = sum_copies_any(group_sum, replica_plan)
    hidden_out = hidden_grad.reshape(1, 1, slot_count, cap_rows, hidden_units)
    return (route_grad, hidden_out, copy_grad.reshape(1, shard_rows, model_width))


def solution(mesh):
    placed = (
        P(("group", "expert"), None),
        P(("group", "expert"), None),
        P(("group", "expert"), None),
        P(("group", "expert"), None),
        P(),
        P("expert", None, None),
        P("group", "expert", None, None, None),
    )
    return jax.shard_map(
        local,
        mesh=mesh,
        in_specs=placed,
        out_specs=(
            P(("group", "expert"), None),
            P("group", "expert", None, None, None),
            P("expert", "group", None),
        ),
        check_vma=False,
    )
```

```python
import functools
import itertools

import jax
import jax.numpy as jnp
import numpy as np
from jax import lax
from jax.experimental import pallas as pl
from jax.experimental.pallas import tpu as pltpu
from jax.sharding import PartitionSpec as P

HOT = 2
CHUNKS = (1024, 1024, 1024, 512)


def slot_layout(replica_plan):
    slot_count = replica_plan.shape[0]
    slot_ids = jnp.arange(slot_count, dtype=jnp.int32)
    same_expert = replica_plan[:, None] == replica_plan[None, :]
    earlier_slot = slot_ids[None, :] < slot_ids[:, None]
    ordinal = jnp.sum(same_expert & earlier_slot, axis=1)
    return (slot_ids, same_expert, ordinal)


def route_kernel(
    expert_count, cap_rows, plan_col, plan_row, id_col, id_row, routes, picks, gates, spread, rank_out, slot_out
):
    slot_count = plan_col.shape[0]
    top_count, tokens = routes.shape
    plan = plan_col[...]
    same = plan == plan_row[...]
    copies = jnp.sum(jnp.where(same, 1.0, 0.0), axis=1, keepdims=True)
    ordinal = jnp.sum(jnp.where(same & (id_row[...] < id_col[...]), 1.0, 0.0), axis=1, keepdims=True)
    slot_ids = lax.broadcasted_iota(jnp.int32, (slot_count, tokens), 0)
    reach = jnp.zeros((slot_count, tokens), jnp.float32)
    gate_of = jnp.zeros((slot_count, tokens), jnp.float32)
    matches = []
    for k in range(top_count):
        route = routes[k : k + 1, :]
        pick = picks[k : k + 1, :].astype(jnp.float32)
        chosen = pick - copies * jnp.floor((pick + 0.5) / copies)
        match = (route == plan) & (chosen == ordinal) & (route < expert_count)
        matches.append(match)
        reach = jnp.where(match, 1.0, reach)
        gate_of = jnp.where(match, gates[k : k + 1, :], gate_of)
    before = lax.broadcasted_iota(jnp.int32, (tokens, tokens), 0) < lax.broadcasted_iota(
        jnp.int32, (tokens, tokens), 1
    )
    rank = lax.dot_general(
        reach.astype(jnp.bfloat16),
        jnp.where(before, 1.0, 0.0).astype(jnp.bfloat16),
        (((1,), (0,)), ((), ())),
        preferred_element_type=jnp.float32,
    ).astype(jnp.int32)
    kept = (reach > 0.0) & (rank < cap_rows)
    rank_out[...] = jnp.where(kept, rank, -1)
    for k in range(top_count):
        slot_out[k : k + 1, :] = (
            jnp.sum(jnp.where(matches[k] & kept, slot_ids + 1, 0), axis=0, keepdims=True) - 1
        )
    place = jnp.where(kept, slot_ids * cap_rows + rank, -1)
    held = slot_count * cap_rows
    block = 80 if held % 80 == 0 else held
    for start in range(0, held, block):
        row_ids = lax.broadcasted_iota(jnp.int32, (block, tokens), 0) + start
        total = jnp.zeros((block, tokens), jnp.float32)
        for s in range(start // cap_rows, -(-(start + block) // cap_rows)):
            total = jnp.where(row_ids == place[s : s + 1, :], gate_of[s : s + 1, :], total)
        spread[start : start + block, :] = total.astype(jnp.bfloat16)


def place_routes(routes, picks, gates, replica_plan, slot_order, expert_count, cap_rows):
    slot_count = replica_plan.shape[0]
    top_count, tokens = routes.shape
    return pl.pallas_call(
        functools.partial(route_kernel, expert_count, cap_rows),
        out_shape=(
            jax.ShapeDtypeStruct((slot_count * cap_rows, tokens), jnp.bfloat16),
            jax.ShapeDtypeStruct((slot_count, tokens), jnp.int32),
            jax.ShapeDtypeStruct((top_count, tokens), jnp.int32),
        ),
    )(
        replica_plan.reshape(slot_count, 1),
        replica_plan.reshape(1, slot_count),
        slot_order.reshape(slot_count, 1),
        slot_order.reshape(1, slot_count),
        routes,
        picks,
        gates,
    )


def return_kernel(score, rank, slot_of, gates, out):
    slot_count, cap_rows = score.shape
    top_count, tokens = slot_of.shape
    row_ids = lax.broadcasted_iota(jnp.int32, (cap_rows, tokens), 0)
    total = jnp.zeros((top_count, tokens), jnp.float32)
    for s in range(slot_count):
        onehot = jnp.where(row_ids == rank[s : s + 1, :], 1.0, 0.0)
        value = lax.dot_general(
            score[s : s + 1, :],
            onehot,
            (((1,), (0,)), ((), ())),
            precision=lax.Precision.HIGHEST,
            preferred_element_type=jnp.float32,
        )
        total = jnp.where(slot_of[...] == s, value, total)
    held_gate = gates[...].astype(jnp.bfloat16).astype(jnp.float32)
    out[...] = jnp.where(slot_of[...] >= 0, total / held_gate, 0.0)


def matchings(slot_count):
    first = np.zeros((1 << slot_count,), np.int32)
    perms = []
    for four in itertools.combinations(range(slot_count), 4):
        first[sum(1 << s for s in four)] = len(perms)
        for other in range(3):
            rest = [four[1 + i] for i in range(3) if i != other]
            pairs = ((four[0], four[1 + other]), tuple(rest))
            perms.append([(a, b) for a, b in pairs] + [(b, a) for a, b in pairs])
    return first, perms


def matching_index(replica_plan, first):
    slot_ids, same_expert, ordinal = slot_layout(replica_plan)
    hot = jnp.sum(same_expert, axis=1) > 1
    mask = jnp.sum(jnp.where(hot, 1 << slot_ids, 0))
    least = jnp.min(jnp.where(hot, slot_ids, slot_ids.shape[0]))
    expert = jnp.sum(jnp.where(slot_ids == least, replica_plan, 0))
    partner = jnp.max(jnp.where(replica_plan == expert, slot_ids, 0))
    between = jnp.sum(hot & (slot_ids > least) & (slot_ids < partner))
    base = jnp.sum(jnp.where(jnp.arange(first.shape[0]) == mask, jnp.asarray(first), 0))
    return base + between


def sum_copies_any(group_sum, replica_plan):
    slot_ids, same_expert, ordinal = slot_layout(replica_plan)
    copies = jnp.sum(same_expert, axis=1)
    hot_first = (copies > 1) & (ordinal == 0)
    hot_rank = jnp.sum(hot_first[None, :] & (replica_plan[None, :] < replica_plan[:, None]), axis=1)
    my_slot = slot_ids == lax.axis_index("expert")
    my_rank = jnp.sum(jnp.where(my_slot, hot_rank, 0))
    my_hot = jnp.any(my_slot & (copies > 1))
    place_hot = (jnp.arange(HOT, dtype=jnp.int32) == my_rank) & my_hot
    group_f = group_sum.astype(jnp.float32)
    table = jnp.where(place_hot[:, None, None], group_f[None], 0.0)
    summed = lax.psum(table.astype(jnp.bfloat16), "expert").astype(jnp.float32)
    picked = jnp.sum(jnp.where(place_hot[:, None, None], summed, 0.0), axis=0)
    return jnp.where(my_hot, picked, group_f).astype(jnp.bfloat16)


def local(out_grad, gates, routes, copy_pick, replica_plan, down_weight, saved_hidden):
    slot_count = replica_plan.shape[0]
    cap_rows = saved_hidden.shape[3]
    expert_count = slot_count - slot_count // 4
    model_width = out_grad.shape[1]
    hidden_units = down_weight.shape[1]
    held_count = slot_count * cap_rows
    group_size = lax.axis_size("group")
    chips = group_size // 2
    shard_rows = hidden_units // group_size
    me = lax.axis_index("group")
    chip, core = me // 2, me % 2

    seat = lax.axis_index("expert")
    slot_order = jnp.arange(slot_count, dtype=jnp.int32) ^ seat

    spread, rank, slot_of = place_routes(
        routes.T, copy_pick.T, gates.T, replica_plan[slot_order], slot_order, expert_count, cap_rows
    )
    edges = np.cumsum((0,) + CHUNKS)
    spans = [(int(a), int(b)) for a, b in zip(edges[:-1], edges[1:])]
    arrived = []
    for a, b in spans:
        got = []
        for d in reversed(range(slot_count)):
            rows = jnp.dot(
                spread[d * cap_rows : (d + 1) * cap_rows],
                out_grad[:, a:b],
                preferred_element_type=jnp.float32,
            ).astype(jnp.bfloat16)
            got.append(lax.ppermute(rows, "expert", [(i, i ^ d) for i in range(slot_count)]) if d else rows)
        arrived.append(jnp.concatenate(got[::-1], axis=0))

    held_hidden = saved_hidden[0, 0][slot_order].reshape(held_count, hidden_units)
    by_owner = held_hidden.T.reshape(chips, 2, shard_rows, held_count)
    by_owner = jnp.stack([by_owner[chip ^ d] for d in range(chips)])
    stay = lax.optimization_barrier(by_owner[:, core].reshape(-1, held_count))
    leave = lax.optimization_barrier(by_owner[:, 1 - core].reshape(-1, held_count))

    projected = jnp.zeros((held_count, hidden_units), jnp.float32)
    group_sum = []
    for (a, b), rows in zip(spans, arrived):
        away = jnp.dot(leave, rows, preferred_element_type=jnp.float32).astype(jnp.bfloat16)
        near = lax.ppermute(away, "group", [(i, i ^ 1) for i in range(group_size)])
        total = jnp.dot(stay, rows, preferred_element_type=jnp.float32) + near.astype(jnp.float32)
        total = total.reshape(chips, shard_rows, b - a)
        mine = total[0]
        for d in range(1, chips):
            far = lax.ppermute(
                total[d].astype(jnp.bfloat16), "group", [(i, i ^ (2 * d)) for i in range(group_size)]
            )
            mine = mine + far.astype(jnp.float32)
        group_sum.append(mine.astype(jnp.bfloat16))
        projected = projected + lax.dot_general(
            rows, down_weight[0, :, a:b], (((1,), (1,)), ((), ())), preferred_element_type=jnp.float32
        )

    hidden_grad = projected.astype(jnp.bfloat16).reshape(slot_count, cap_rows, hidden_units)[slot_order]
    route_score = jnp.sum(projected * held_hidden.astype(jnp.float32), axis=1)
    returned = lax.all_to_all(
        route_score.reshape(slot_count, cap_rows)[slot_order],
        "expert",
        split_axis=0,
        concat_axis=0,
        tiled=True,
    )
    route_grad = pl.pallas_call(
        return_kernel, out_shape=jax.ShapeDtypeStruct(gates.T.shape, jnp.float32)
    )(returned[slot_order], rank, slot_of, gates.T).T

    group_sum = jnp.concatenate(group_sum, axis=1)
    if slot_count - expert_count == HOT:
        first, perms = matchings(slot_count)
        other = lax.switch(
            matching_index(replica_plan, first),
            [functools.partial(lax.ppermute, axis_name="expert", perm=perm) for perm in perms],
            group_sum,
        )
        copy_grad = (group_sum.astype(jnp.float32) + other.astype(jnp.float32)).astype(jnp.bfloat16)
    else:
        copy_grad = sum_copies_any(group_sum, replica_plan)
    hidden_out = hidden_grad.reshape(1, 1, slot_count, cap_rows, hidden_units)
    return (route_grad, hidden_out, copy_grad.reshape(1, shard_rows, model_width))


def solution(mesh):
    placed = (
        P(("group", "expert"), None),
        P(("group", "expert"), None),
        P(("group", "expert"), None),
        P(("group", "expert"), None),
        P(),
        P("expert", None, None),
        P("group", "expert", None, None, None),
    )
    return jax.shard_map(
        local,
        mesh=mesh,
        in_specs=placed,
        out_specs=(
            P(("group", "expert"), None),
            P("group", "expert", None, None, None),
            P("expert", "group", None),
        ),
        check_vma=False,
    )
```

```python
import functools
import itertools

import jax
import jax.numpy as jnp
import numpy as np
from jax import lax
from jax.experimental import pallas as pl
from jax.experimental.pallas import tpu as pltpu
from jax.sharding import PartitionSpec as P

HOT = 2
TILE = 512
CHUNKS = (2048, 1024, 512)
WINDOW = 4


def slot_layout(replica_plan):
    slot_count = replica_plan.shape[0]
    slot_ids = jnp.arange(slot_count, dtype=jnp.int32)
    same_expert = replica_plan[:, None] == replica_plan[None, :]
    earlier_slot = slot_ids[None, :] < slot_ids[:, None]
    ordinal = jnp.sum(same_expert & earlier_slot, axis=1)
    return (slot_ids, same_expert, ordinal)


def route_kernel(
    expert_count, cap_rows, seat, plan_col, plan_row, routes, picks, gates, spread, rank_out, slot_out
):
    slot_count = plan_col.shape[0]
    top_count, tokens = routes.shape
    plan = plan_col[...]
    same = plan == plan_row[...]
    slot_r = lax.broadcasted_iota(jnp.int32, (slot_count, slot_count), 0)
    slot_c = lax.broadcasted_iota(jnp.int32, (slot_count, slot_count), 1)
    copies = jnp.sum(jnp.where(same, 1.0, 0.0), axis=1, keepdims=True)
    ordinal = jnp.sum(jnp.where(same & (slot_c < slot_r), 1.0, 0.0), axis=1, keepdims=True)
    slot_ids = lax.broadcasted_iota(jnp.int32, (slot_count, tokens), 0)
    reach = jnp.zeros((slot_count, tokens), jnp.float32)
    gate_of = jnp.zeros((slot_count, tokens), jnp.float32)
    matches = []
    for k in range(top_count):
        route = routes[k : k + 1, :]
        pick = picks[k : k + 1, :].astype(jnp.float32)
        chosen = pick - copies * jnp.floor((pick + 0.5) / copies)
        match = (route == plan) & (chosen == ordinal) & (route < expert_count)
        matches.append(match)
        reach = jnp.where(match, 1.0, reach)
        gate_of = jnp.where(match, gates[k : k + 1, :], gate_of)
    before = lax.broadcasted_iota(jnp.int32, (tokens, tokens), 0) < lax.broadcasted_iota(
        jnp.int32, (tokens, tokens), 1
    )
    rank = lax.dot_general(
        reach.astype(jnp.bfloat16),
        jnp.where(before, 1.0, 0.0).astype(jnp.bfloat16),
        (((1,), (0,)), ((), ())),
        preferred_element_type=jnp.float32,
    ).astype(jnp.int32)
    kept = (reach > 0.0) & (rank < cap_rows)
    rank = jnp.where(kept, rank, -1)
    rank_out[...] = rank
    for k in range(top_count):
        slot_out[k : k + 1, :] = (
            jnp.sum(jnp.where(matches[k] & kept, slot_ids + 1, 0), axis=0, keepdims=True) - 1
        )
    row_ids = lax.broadcasted_iota(jnp.int32, spread.shape[1:], 0)
    for s in range(slot_count):
        placed = jnp.where(row_ids == rank[s : s + 1, :], gate_of[s : s + 1, :], 0.0)
        spread[seat[0] ^ s] = placed.astype(jnp.bfloat16)


def place_routes(routes, picks, gates, replica_plan, seat, expert_count, cap_rows, held_rows):
    slot_count = replica_plan.shape[0]
    top_count, tokens = routes.shape
    vmem = pl.BlockSpec(memory_space=pltpu.VMEM)
    return pl.pallas_call(
        functools.partial(route_kernel, expert_count, cap_rows),
        out_shape=(
            jax.ShapeDtypeStruct((slot_count, held_rows, tokens), jnp.bfloat16),
            jax.ShapeDtypeStruct((slot_count, tokens), jnp.int32),
            jax.ShapeDtypeStruct((top_count, tokens), jnp.int32),
        ),
        in_specs=[pl.BlockSpec(memory_space=pltpu.SMEM)] + [vmem] * 5,
        out_specs=(vmem, vmem, vmem),
    )(seat, replica_plan.reshape(slot_count, 1), replica_plan.reshape(1, slot_count), routes, picks, gates)


def send_kernel(spread, rows, *rest):
    out = rest[-1]
    out[...] = jnp.dot(spread[0], rows[...], preferred_element_type=jnp.float32).astype(jnp.bfloat16)


def rows_to_send(spread, out_grad, d, span, after):
    _, held_rows, tokens = spread.shape
    start, stop = span
    return pl.pallas_call(
        send_kernel,
        grid=((stop - start) // TILE,),
        in_specs=[
            pl.BlockSpec((1, held_rows, tokens), lambda j: (d, 0, 0)),
            pl.BlockSpec((tokens, TILE), lambda j: (0, start // TILE + j)),
        ]
        + [pl.BlockSpec(memory_space=pl.ANY)] * len(after),
        out_specs=pl.BlockSpec((held_rows, TILE), lambda j: (0, j)),
        out_shape=jax.ShapeDtypeStruct((held_rows, stop - start), jnp.bfloat16),
        cost_estimate=pl.CostEstimate(
            flops=2 * held_rows * tokens * (stop - start),
            bytes_accessed=2 * (held_rows + tokens) * (stop - start),
            transcendentals=0,
        ),
    )(spread, out_grad, *after)


def away_kernel(seat, leave, *refs):
    blocks, (rows, away) = refs[:-2], refs[-2:]
    for d, block in enumerate(blocks):
        rows[seat[0] ^ d] = block[...]
    flat = rows[...].reshape(-1, rows.shape[-1])
    away[...] = jnp.dot(leave[...], flat, preferred_element_type=jnp.float32).astype(jnp.bfloat16)


def gather_rows(blocks, seat, leave):
    held_rows, width = blocks[0].shape
    units, held = leave.shape
    return pl.pallas_call(
        away_kernel,
        grid=(width // TILE,),
        in_specs=[pl.BlockSpec(memory_space=pltpu.SMEM), pl.BlockSpec((units, held), lambda j: (0, 0))]
        + [pl.BlockSpec((held_rows, TILE), lambda j: (0, j))] * len(blocks),
        out_specs=(
            pl.BlockSpec((len(blocks), held_rows, TILE), lambda j: (0, 0, j)),
            pl.BlockSpec((units, TILE), lambda j: (0, j)),
        ),
        out_shape=(
            jax.ShapeDtypeStruct((len(blocks), held_rows, width), jnp.bfloat16),
            jax.ShapeDtypeStruct((units, width), jnp.bfloat16),
        ),
        cost_estimate=pl.CostEstimate(
            flops=2 * units * held * width, bytes_accessed=2 * (2 * held + units) * width, transcendentals=0
        ),
    )(seat, leave, *blocks)


def near_kernel(stay, rows, near, mine, *others):
    flat = rows[...].reshape(-1, rows.shape[-1])
    shard = mine.shape[0]
    total = jnp.dot(stay[...], flat, preferred_element_type=jnp.float32) + near[...].astype(jnp.float32)
    mine[...] = total[:shard]
    for d, other in enumerate(others):
        other[...] = total[(d + 1) * shard : (d + 2) * shard].astype(jnp.bfloat16)


def add_near(stay, rows, near, chips):
    units, held = stay.shape
    width = rows.shape[-1]
    shard = units // chips
    return pl.pallas_call(
        near_kernel,
        grid=(width // TILE,),
        in_specs=[
            pl.BlockSpec((units, held), lambda j: (0, 0)),
            pl.BlockSpec(rows.shape[:2] + (TILE,), lambda j: (0, 0, j)),
            pl.BlockSpec((units, TILE), lambda j: (0, j)),
        ],
        out_specs=(pl.BlockSpec((shard, TILE), lambda j: (0, j)),) * chips,
        out_shape=(jax.ShapeDtypeStruct((shard, width), jnp.float32),)
        + (jax.ShapeDtypeStruct((shard, width), jnp.bfloat16),) * (chips - 1),
        cost_estimate=pl.CostEstimate(
            flops=2 * units * held * width, bytes_accessed=2 * (held + 3 * units) * width, transcendentals=0
        ),
    )(stay, rows, near)


def return_kernel(score, rank, slot_of, gates, out):
    slot_count, cap_rows = score.shape
    top_count, tokens = slot_of.shape
    row_ids = lax.broadcasted_iota(jnp.int32, (cap_rows, tokens), 0)
    total = jnp.zeros((top_count, tokens), jnp.float32)
    for s in range(slot_count):
        onehot = jnp.where(row_ids == rank[s : s + 1, :], 1.0, 0.0)
        value = lax.dot_general(
            score[s : s + 1, :],
            onehot,
            (((1,), (0,)), ((), ())),
            precision=lax.Precision.HIGHEST,
            preferred_element_type=jnp.float32,
        )
        total = jnp.where(slot_of[...] == s, value, total)
    held_gate = gates[...].astype(jnp.bfloat16).astype(jnp.float32)
    out[...] = jnp.where(slot_of[...] >= 0, total / held_gate, 0.0)


def matchings(slot_count):
    first = np.zeros((1 << slot_count,), np.int32)
    perms = []
    for four in itertools.combinations(range(slot_count), 4):
        first[sum(1 << s for s in four)] = len(perms)
        for other in range(3):
            rest = [four[1 + i] for i in range(3) if i != other]
            pairs = ((four[0], four[1 + other]), tuple(rest))
            perms.append([(a, b) for a, b in pairs] + [(b, a) for a, b in pairs])
    return first, perms


def matching_index(replica_plan, first):
    slot_ids, same_expert, ordinal = slot_layout(replica_plan)
    hot = jnp.sum(same_expert, axis=1) > 1
    mask = jnp.sum(jnp.where(hot, 1 << slot_ids, 0))
    least = jnp.min(jnp.where(hot, slot_ids, slot_ids.shape[0]))
    expert = jnp.sum(jnp.where(slot_ids == least, replica_plan, 0))
    partner = jnp.max(jnp.where(replica_plan == expert, slot_ids, 0))
    between = jnp.sum(hot & (slot_ids > least) & (slot_ids < partner))
    base = jnp.sum(jnp.where(jnp.arange(first.shape[0]) == mask, jnp.asarray(first), 0))
    return base + between


def sum_copies_any(group_sum, replica_plan):
    slot_ids, same_expert, ordinal = slot_layout(replica_plan)
    copies = jnp.sum(same_expert, axis=1)
    hot_first = (copies > 1) & (ordinal == 0)
    hot_rank = jnp.sum(hot_first[None, :] & (replica_plan[None, :] < replica_plan[:, None]), axis=1)
    my_slot = slot_ids == lax.axis_index("expert")
    my_rank = jnp.sum(jnp.where(my_slot, hot_rank, 0))
    my_hot = jnp.any(my_slot & (copies > 1))
    place_hot = (jnp.arange(HOT, dtype=jnp.int32) == my_rank) & my_hot
    group_f = group_sum.astype(jnp.float32)
    table = jnp.where(place_hot[:, None, None], group_f[None], 0.0)
    summed = lax.psum(table.astype(jnp.bfloat16), "expert").astype(jnp.float32)
    picked = jnp.sum(jnp.where(place_hot[:, None, None], summed, 0.0), axis=0)
    return jnp.where(my_hot, picked, group_f).astype(jnp.bfloat16)


def local(out_grad, gates, routes, copy_pick, replica_plan, down_weight, saved_hidden):
    slot_count = replica_plan.shape[0]
    cap_rows = saved_hidden.shape[3]
    expert_count = slot_count - slot_count // 4
    model_width = out_grad.shape[1]
    hidden_units = down_weight.shape[1]
    group_size = lax.axis_size("group")
    chips = group_size // 2
    shard_rows = hidden_units // group_size
    me = lax.axis_index("group")
    chip, core = me // 2, me % 2

    seat = lax.axis_index("expert").astype(jnp.int32).reshape(1)
    held_rows = -(-cap_rows // 16) * 16
    pad = ((0, 0), (0, held_rows - cap_rows), (0, 0))
    held_hidden = jnp.pad(saved_hidden[0, 0], pad).reshape(slot_count * held_rows, hidden_units)

    spread, rank, slot_of = place_routes(
        routes.T, copy_pick.T, gates.T, replica_plan, seat, expert_count, cap_rows, held_rows
    )

    by_owner = held_hidden.T.reshape(chips, 2, shard_rows, -1)
    by_owner = jnp.stack([by_owner[chip ^ d] for d in range(chips)])
    stay = by_owner[:, core].reshape(hidden_units // 2, -1)
    leave = by_owner[:, 1 - core].reshape(hidden_units // 2, -1)

    edges = np.cumsum((0,) + CHUNKS)
    spans = [(int(a), int(b)) for a, b in zip(edges[:-1], edges[1:])]
    far_first = [d for pair in zip(range(slot_count - 1, 0, -1), range(1, slot_count)) for d in pair]
    far_first = list(dict.fromkeys(far_first))
    sent = []
    projected = jnp.zeros((slot_count * held_rows, hidden_units), jnp.float32)
    group_sum = []
    pending = {}
    for span in spans:
        blocks = {0: rows_to_send(spread, out_grad, 0, span, sent[-1:])}
        for place, d in enumerate(far_first):
            after = sent[-WINDOW:][:1] if len(sent) >= WINDOW else []
            after = after + pending.pop(place, [])
            rows = rows_to_send(spread, out_grad, d, span, after)
            blocks[d] = lax.ppermute(rows, "expert", [(i, i ^ d) for i in range(slot_count)])
            sent.append(blocks[d])
        rows, away = gather_rows([blocks[d] for d in range(slot_count)], seat, leave)
        near = lax.ppermute(away, "group", [(i, i ^ 1) for i in range(group_size)])
        mine, *others = add_near(stay, rows, near, chips)
        for d, other in enumerate(others):
            far = lax.ppermute(other, "group", [(i, i ^ (2 * d + 2)) for i in range(group_size)])
            mine = mine + far.astype(jnp.float32)
        group_sum.append(mine.astype(jnp.bfloat16))
        pending = {WINDOW: [away], WINDOW + 1: [others[0]]}
        projected = projected + lax.dot_general(
            rows.reshape(slot_count * held_rows, -1),
            down_weight[0, :, span[0] : span[1]],
            (((1,), (1,)), ((), ())),
            preferred_element_type=jnp.float32,
        )

    route_score = jnp.sum(projected * held_hidden.astype(jnp.float32), axis=1)
    returned = lax.all_to_all(
        route_score.reshape(slot_count, held_rows), "expert", split_axis=0, concat_axis=0, tiled=True
    )
    route_grad = pl.pallas_call(
        return_kernel, out_shape=jax.ShapeDtypeStruct(gates.T.shape, jnp.float32)
    )(returned, rank, slot_of, gates.T).T
    hidden_grad = projected.astype(jnp.bfloat16).reshape(slot_count, held_rows, hidden_units)[:, :cap_rows]

    group_sum = jnp.concatenate(group_sum, axis=1)
    if slot_count - expert_count == HOT:
        first, perms = matchings(slot_count)
        other = lax.switch(
            matching_index(replica_plan, first),
            [functools.partial(lax.ppermute, axis_name="expert", perm=perm) for perm in perms],
            group_sum,
        )
        copy_grad = (group_sum.astype(jnp.float32) + other.astype(jnp.float32)).astype(jnp.bfloat16)
    else:
        copy_grad = sum_copies_any(group_sum, replica_plan)
    return (route_grad, hidden_grad[None, None], copy_grad.reshape(1, shard_rows, model_width))


def solution(mesh):
    placed = (
        P(("group", "expert"), None),
        P(("group", "expert"), None),
        P(("group", "expert"), None),
        P(("group", "expert"), None),
        P(),
        P("expert", None, None),
        P("group", "expert", None, None, None),
    )
    return jax.shard_map(
        local,
        mesh=mesh,
        in_specs=placed,
        out_specs=(
            P(("group", "expert"), None),
            P("group", "expert", None, None, None),
            P("expert", "group", None),
        ),
        check_vma=False,
    )
```

```python
import functools
import itertools

import jax
import jax.numpy as jnp
import numpy as np
from jax import lax
from jax.experimental import pallas as pl
from jax.experimental.pallas import tpu as pltpu
from jax.sharding import PartitionSpec as P

HOT = 2
TILE = 512
LITTLE = pl.CostEstimate(flops=1, bytes_accessed=1, transcendentals=0)
CHUNKS = (1536, 1536, 512)


def slot_layout(replica_plan):
    slot_count = replica_plan.shape[0]
    slot_ids = jnp.arange(slot_count, dtype=jnp.int32)
    same_expert = replica_plan[:, None] == replica_plan[None, :]
    earlier_slot = slot_ids[None, :] < slot_ids[:, None]
    ordinal = jnp.sum(same_expert & earlier_slot, axis=1)
    return (slot_ids, same_expert, ordinal)


def route_kernel(
    expert_count, cap_rows, seat, plan_col, plan_row, routes, picks, gates, spread, rank_out, slot_out
):
    slot_count = plan_col.shape[0]
    top_count, tokens = routes.shape
    plan = plan_col[...]
    same = plan == plan_row[...]
    slot_r = lax.broadcasted_iota(jnp.int32, (slot_count, slot_count), 0)
    slot_c = lax.broadcasted_iota(jnp.int32, (slot_count, slot_count), 1)
    copies = jnp.sum(jnp.where(same, 1.0, 0.0), axis=1, keepdims=True)
    ordinal = jnp.sum(jnp.where(same & (slot_c < slot_r), 1.0, 0.0), axis=1, keepdims=True)
    slot_ids = lax.broadcasted_iota(jnp.int32, (slot_count, tokens), 0)
    reach = jnp.zeros((slot_count, tokens), jnp.float32)
    gate_of = jnp.zeros((slot_count, tokens), jnp.float32)
    matches = []
    for k in range(top_count):
        route = routes[k : k + 1, :]
        pick = picks[k : k + 1, :].astype(jnp.float32)
        chosen = pick - copies * jnp.floor((pick + 0.5) / copies)
        match = (route == plan) & (chosen == ordinal) & (route < expert_count)
        matches.append(match)
        reach = jnp.where(match, 1.0, reach)
        gate_of = jnp.where(match, gates[k : k + 1, :], gate_of)
    before = lax.broadcasted_iota(jnp.int32, (tokens, tokens), 0) < lax.broadcasted_iota(
        jnp.int32, (tokens, tokens), 1
    )
    rank = lax.dot_general(
        reach.astype(jnp.bfloat16),
        jnp.where(before, 1.0, 0.0).astype(jnp.bfloat16),
        (((1,), (0,)), ((), ())),
        preferred_element_type=jnp.float32,
    ).astype(jnp.int32)
    kept = (reach > 0.0) & (rank < cap_rows)
    rank = jnp.where(kept, rank, -1)
    rank_out[...] = rank
    for k in range(top_count):
        slot_out[k : k + 1, :] = (
            jnp.sum(jnp.where(matches[k] & kept, slot_ids + 1, 0), axis=0, keepdims=True) - 1
        )
    row_ids = lax.broadcasted_iota(jnp.int32, spread.shape[1:], 0)
    for s in range(slot_count):
        placed = jnp.where(row_ids == rank[s : s + 1, :], gate_of[s : s + 1, :], 0.0)
        spread[seat[0] ^ s] = placed.astype(jnp.bfloat16)


def place_routes(routes, picks, gates, replica_plan, seat, expert_count, cap_rows, held_rows):
    slot_count = replica_plan.shape[0]
    top_count, tokens = routes.shape
    vmem = pl.BlockSpec(memory_space=pltpu.VMEM)
    return pl.pallas_call(
        functools.partial(route_kernel, expert_count, cap_rows),
        out_shape=(
            jax.ShapeDtypeStruct((slot_count, held_rows, tokens), jnp.bfloat16),
            jax.ShapeDtypeStruct((slot_count, tokens), jnp.int32),
            jax.ShapeDtypeStruct((top_count, tokens), jnp.int32),
        ),
        in_specs=[pl.BlockSpec(memory_space=pltpu.SMEM)] + [vmem] * 5,
        out_specs=(vmem, vmem, vmem),
    )(seat, replica_plan.reshape(slot_count, 1), replica_plan.reshape(1, slot_count), routes, picks, gates)


def send_kernel(spread, rows, *rest):
    held_rows, tokens = spread.shape[1:]
    blocks = rest[-spread.shape[0] :]
    total = jnp.dot(spread[...].reshape(-1, tokens), rows[...], preferred_element_type=jnp.float32)
    for i, block in enumerate(blocks):
        block[...] = total[i * held_rows : (i + 1) * held_rows].astype(jnp.bfloat16)


def rows_to_send(spread, out_grad, half, span, after):
    slot_count, held_rows, tokens = spread.shape
    blocks = slot_count // 2
    start, stop = span
    return pl.pallas_call(
        send_kernel,
        grid=((stop - start) // TILE,),
        in_specs=[
            pl.BlockSpec((blocks, held_rows, tokens), lambda j: (half, 0, 0)),
            pl.BlockSpec((tokens, TILE), lambda j: (0, start // TILE + j)),
        ]
        + [pl.BlockSpec(memory_space=pl.ANY)] * len(after),
        out_specs=(pl.BlockSpec((held_rows, TILE), lambda j: (0, j)),) * blocks,
        out_shape=(jax.ShapeDtypeStruct((held_rows, stop - start), jnp.bfloat16),) * blocks,
        cost_estimate=LITTLE,
    )(spread, out_grad, *after)


def send_all_kernel(seat, spread, rows, *rest):
    out = rest[-1]
    held_rows, tokens = spread.shape[1:]
    total = jnp.dot(spread[...].reshape(-1, tokens), rows[...], preferred_element_type=jnp.float32)
    for d in range(spread.shape[0]):
        out[seat[0] ^ d] = total[d * held_rows : (d + 1) * held_rows].astype(jnp.bfloat16)


def all_rows_to_send(spread, out_grad, seat, span, after):
    slot_count, held_rows, tokens = spread.shape
    start, stop = span
    return pl.pallas_call(
        send_all_kernel,
        grid=((stop - start) // TILE,),
        in_specs=[
            pl.BlockSpec(memory_space=pltpu.SMEM),
            pl.BlockSpec((slot_count, held_rows, tokens), lambda j: (0, 0, 0)),
            pl.BlockSpec((tokens, TILE), lambda j: (0, start // TILE + j)),
        ]
        + [pl.BlockSpec(memory_space=pl.ANY)] * len(after),
        out_specs=pl.BlockSpec((slot_count, held_rows, TILE), lambda j: (0, 0, j)),
        out_shape=jax.ShapeDtypeStruct((slot_count, held_rows, stop - start), jnp.bfloat16),
        cost_estimate=LITTLE,
    )(seat, spread, out_grad, *after)


def part_kernel(leave, rows, *rest):
    flat = rows[...].reshape(-1, rows.shape[-1])
    rest[-1][...] = jnp.dot(leave[...], flat, preferred_element_type=jnp.float32).astype(jnp.bfloat16)


def other_core_part(rows, leave, after):
    slot_count, held_rows, width = rows.shape
    units, held = leave.shape
    return pl.pallas_call(
        part_kernel,
        grid=(width // TILE,),
        in_specs=[
            pl.BlockSpec((units, held), lambda j: (0, 0)),
            pl.BlockSpec((slot_count, held_rows, TILE), lambda j: (0, 0, j)),
        ]
        + [pl.BlockSpec(memory_space=pl.ANY)] * len(after),
        out_specs=pl.BlockSpec((units, TILE), lambda j: (0, j)),
        out_shape=jax.ShapeDtypeStruct((units, width), jnp.bfloat16),
        cost_estimate=LITTLE,
    )(leave, rows, *after)


def away_kernel(slot_count, seat, leave, *refs):
    rows, away = refs[-2:]
    for d, block in enumerate(refs[:slot_count]):
        rows[seat[0] ^ d] = block[...]
    flat = rows[...].reshape(-1, rows.shape[-1])
    away[...] = jnp.dot(leave[...], flat, preferred_element_type=jnp.float32).astype(jnp.bfloat16)


def gather_rows(blocks, seat, leave, after):
    held_rows, width = blocks[0].shape
    units, held = leave.shape
    return pl.pallas_call(
        functools.partial(away_kernel, len(blocks)),
        grid=(width // TILE,),
        in_specs=[pl.BlockSpec(memory_space=pltpu.SMEM), pl.BlockSpec((units, held), lambda j: (0, 0))]
        + [pl.BlockSpec((held_rows, TILE), lambda j: (0, j))] * len(blocks)
        + [pl.BlockSpec(memory_space=pl.ANY)] * len(after),
        out_specs=(
            pl.BlockSpec((len(blocks), held_rows, TILE), lambda j: (0, 0, j)),
            pl.BlockSpec((units, TILE), lambda j: (0, j)),
        ),
        out_shape=(
            jax.ShapeDtypeStruct((len(blocks), held_rows, width), jnp.bfloat16),
            jax.ShapeDtypeStruct((units, width), jnp.bfloat16),
        ),
        cost_estimate=LITTLE,
    )(seat, leave, *blocks, *after)


def near_kernel(stay, rows, near, mine, *others):
    flat = rows[...].reshape(-1, rows.shape[-1])
    shard = mine.shape[0]
    total = jnp.dot(stay[...], flat, preferred_element_type=jnp.float32) + near[...].astype(jnp.float32)
    mine[...] = total[:shard]
    for d, other in enumerate(others):
        other[...] = total[(d + 1) * shard : (d + 2) * shard].astype(jnp.bfloat16)


def add_near(stay, rows, near, chips):
    units, held = stay.shape
    width = rows.shape[-1]
    shard = units // chips
    return pl.pallas_call(
        near_kernel,
        grid=(width // TILE,),
        in_specs=[
            pl.BlockSpec((units, held), lambda j: (0, 0)),
            pl.BlockSpec(rows.shape[:2] + (TILE,), lambda j: (0, 0, j)),
            pl.BlockSpec((units, TILE), lambda j: (0, j)),
        ],
        out_specs=(pl.BlockSpec((shard, TILE), lambda j: (0, j)),) * chips,
        out_shape=(jax.ShapeDtypeStruct((shard, width), jnp.float32),)
        + (jax.ShapeDtypeStruct((shard, width), jnp.bfloat16),) * (chips - 1),
        cost_estimate=LITTLE,
    )(stay, rows, near)


def return_kernel(score, rank, slot_of, gates, out):
    slot_count, cap_rows = score.shape
    top_count, tokens = slot_of.shape
    row_ids = lax.broadcasted_iota(jnp.int32, (cap_rows, tokens), 0)
    total = jnp.zeros((top_count, tokens), jnp.float32)
    for s in range(slot_count):
        onehot = jnp.where(row_ids == rank[s : s + 1, :], 1.0, 0.0)
        value = lax.dot_general(
            score[s : s + 1, :],
            onehot,
            (((1,), (0,)), ((), ())),
            precision=lax.Precision.HIGHEST,
            preferred_element_type=jnp.float32,
        )
        total = jnp.where(slot_of[...] == s, value, total)
    held_gate = gates[...].astype(jnp.bfloat16).astype(jnp.float32)
    out[...] = jnp.where(slot_of[...] >= 0, total / held_gate, 0.0)


def matchings(slot_count):
    first = np.zeros((1 << slot_count,), np.int32)
    perms = []
    for four in itertools.combinations(range(slot_count), 4):
        first[sum(1 << s for s in four)] = len(perms)
        for other in range(3):
            rest = [four[1 + i] for i in range(3) if i != other]
            pairs = ((four[0], four[1 + other]), tuple(rest))
            perms.append([(a, b) for a, b in pairs] + [(b, a) for a, b in pairs])
    return first, perms


def matching_index(replica_plan, first):
    slot_ids, same_expert, ordinal = slot_layout(replica_plan)
    hot = jnp.sum(same_expert, axis=1) > 1
    mask = jnp.sum(jnp.where(hot, 1 << slot_ids, 0))
    least = jnp.min(jnp.where(hot, slot_ids, slot_ids.shape[0]))
    expert = jnp.sum(jnp.where(slot_ids == least, replica_plan, 0))
    partner = jnp.max(jnp.where(replica_plan == expert, slot_ids, 0))
    between = jnp.sum(hot & (slot_ids > least) & (slot_ids < partner))
    base = jnp.sum(jnp.where(jnp.arange(first.shape[0]) == mask, jnp.asarray(first), 0))
    return base + between


def sum_copies_any(group_sum, replica_plan):
    slot_ids, same_expert, ordinal = slot_layout(replica_plan)
    copies = jnp.sum(same_expert, axis=1)
    hot_first = (copies > 1) & (ordinal == 0)
    hot_rank = jnp.sum(hot_first[None, :] & (replica_plan[None, :] < replica_plan[:, None]), axis=1)
    my_slot = slot_ids == lax.axis_index("expert")
    my_rank = jnp.sum(jnp.where(my_slot, hot_rank, 0))
    my_hot = jnp.any(my_slot & (copies > 1))
    place_hot = (jnp.arange(HOT, dtype=jnp.int32) == my_rank) & my_hot
    group_f = group_sum.astype(jnp.float32)
    table = jnp.where(place_hot[:, None, None], group_f[None], 0.0)
    summed = lax.psum(table.astype(jnp.bfloat16), "expert").astype(jnp.float32)
    picked = jnp.sum(jnp.where(place_hot[:, None, None], summed, 0.0), axis=0)
    return jnp.where(my_hot, picked, group_f).astype(jnp.bfloat16)


def local(out_grad, gates, routes, copy_pick, replica_plan, down_weight, saved_hidden):
    slot_count = replica_plan.shape[0]
    cap_rows = saved_hidden.shape[3]
    expert_count = slot_count - slot_count // 4
    model_width = out_grad.shape[1]
    hidden_units = down_weight.shape[1]
    group_size = lax.axis_size("group")
    chips = group_size // 2
    shard_rows = hidden_units // group_size
    me = lax.axis_index("group")
    chip, core = me // 2, me % 2

    seat = lax.axis_index("expert").astype(jnp.int32).reshape(1)
    held_rows = -(-cap_rows // 16) * 16
    pad = ((0, 0), (0, held_rows - cap_rows), (0, 0))
    held_hidden = jnp.pad(saved_hidden[0, 0], pad).reshape(slot_count * held_rows, hidden_units)

    spread, rank, slot_of = place_routes(
        routes.T, copy_pick.T, gates.T, replica_plan, seat, expert_count, cap_rows, held_rows
    )

    by_owner = held_hidden.T.reshape(chips, 2, shard_rows, -1)
    by_owner = jnp.stack([by_owner[chip ^ d] for d in range(chips)])
    stay = by_owner[:, core].reshape(hidden_units // 2, -1)
    leave = by_owner[:, 1 - core].reshape(hidden_units // 2, -1)

    edges = np.cumsum((0,) + CHUNKS)
    spans = [(int(a), int(b)) for a, b in zip(edges[:-1], edges[1:])]
    half = slot_count // 2

    def travel(ready, first):
        return [
            lax.ppermute(rows, "expert", [(i, i ^ d) for i in range(slot_count)]) if d else rows
            for d, rows in enumerate(ready, first)
        ]

    def by_permutes(span, after):
        far_ready = rows_to_send(spread, out_grad, 1, span, after)
        far_rows = travel(far_ready, half)
        return travel(rows_to_send(spread, out_grad, 0, span, far_ready[:1]), 0) + far_rows

    def to_owners(rows, away):
        near = lax.ppermute(away, "group", [(i, i ^ 1) for i in range(group_size)])
        mine, *others = add_near(stay, rows, near, chips)
        far = [
            lax.ppermute(other, "group", [(i, i ^ (2 * d + 2)) for i in range(group_size)])
            for d, other in enumerate(others)
        ]
        return mine, others, far

    first = by_permutes(spans[0], [])
    middle = lax.all_to_all(
        all_rows_to_send(spread, out_grad, seat, spans[1], first[half : half + 2]),
        "expert",
        split_axis=0,
        concat_axis=0,
        tiled=True,
    )
    first, away = gather_rows(first, seat, leave, [])
    sums = [to_owners(first, away)]
    last = by_permutes(spans[2], sums[0][2][:1])
    away = other_core_part(middle, leave, [])
    sums.append(to_owners(middle, away))
    last, away = gather_rows(last, seat, leave, sums[1][1][:1])
    sums.append(to_owners(last, away))

    projected = sum(
        lax.dot_general(
            rows.reshape(slot_count * held_rows, -1),
            down_weight[0, :, span[0] : span[1]],
            (((1,), (1,)), ((), ())),
            preferred_element_type=jnp.float32,
        )
        for span, rows in zip(spans, (first, middle, last))
    )
    group_sum = [
        sum((f.astype(jnp.float32) for f in far), mine).astype(jnp.bfloat16) for mine, _, far in sums
    ]

    route_score = jnp.sum(projected * held_hidden.astype(jnp.float32), axis=1)
    returned = lax.all_to_all(
        route_score.reshape(slot_count, held_rows), "expert", split_axis=0, concat_axis=0, tiled=True
    )
    route_grad = pl.pallas_call(
        return_kernel, out_shape=jax.ShapeDtypeStruct(gates.T.shape, jnp.float32)
    )(returned, rank, slot_of, gates.T).T
    hidden_grad = projected.astype(jnp.bfloat16).reshape(slot_count, held_rows, hidden_units)[:, :cap_rows]

    group_sum = jnp.concatenate(group_sum, axis=1)
    if slot_count - expert_count == HOT:
        first, perms = matchings(slot_count)
        other = lax.switch(
            matching_index(replica_plan, first),
            [functools.partial(lax.ppermute, axis_name="expert", perm=perm) for perm in perms],
            group_sum,
        )
        copy_grad = (group_sum.astype(jnp.float32) + other.astype(jnp.float32)).astype(jnp.bfloat16)
    else:
        copy_grad = sum_copies_any(group_sum, replica_plan)
    return (route_grad, hidden_grad[None, None], copy_grad.reshape(1, shard_rows, model_width))


def solution(mesh):
    placed = (
        P(("group", "expert"), None),
        P(("group", "expert"), None),
        P(("group", "expert"), None),
        P(("group", "expert"), None),
        P(),
        P("expert", None, None),
        P("group", "expert", None, None, None),
    )
    return jax.shard_map(
        local,
        mesh=mesh,
        in_specs=placed,
        out_specs=(
            P(("group", "expert"), None),
            P("group", "expert", None, None, None),
            P("expert", "group", None),
        ),
        check_vma=False,
    )
```

```python
import functools
import itertools

import jax
import jax.numpy as jnp
import numpy as np
from jax import lax
from jax.experimental import pallas as pl
from jax.experimental.pallas import tpu as pltpu
from jax.sharding import PartitionSpec as P

HOT = 2
TILE = 512
LITTLE = pl.CostEstimate(flops=1, bytes_accessed=1, transcendentals=0)
CHUNKS = (2048, 1024, 512)


def slot_layout(replica_plan):
    slot_count = replica_plan.shape[0]
    slot_ids = jnp.arange(slot_count, dtype=jnp.int32)
    same_expert = replica_plan[:, None] == replica_plan[None, :]
    earlier_slot = slot_ids[None, :] < slot_ids[:, None]
    ordinal = jnp.sum(same_expert & earlier_slot, axis=1)
    return (slot_ids, same_expert, ordinal)


def route_kernel(
    expert_count, cap_rows, seat, plan_col, plan_row, routes, picks, gates, spread, rank_out, slot_out
):
    slot_count = plan_col.shape[0]
    top_count, tokens = routes.shape
    plan = plan_col[...]
    same = plan == plan_row[...]
    slot_r = lax.broadcasted_iota(jnp.int32, (slot_count, slot_count), 0)
    slot_c = lax.broadcasted_iota(jnp.int32, (slot_count, slot_count), 1)
    copies = jnp.sum(jnp.where(same, 1.0, 0.0), axis=1, keepdims=True)
    ordinal = jnp.sum(jnp.where(same & (slot_c < slot_r), 1.0, 0.0), axis=1, keepdims=True)
    slot_ids = lax.broadcasted_iota(jnp.int32, (slot_count, tokens), 0)
    reach = jnp.zeros((slot_count, tokens), jnp.float32)
    gate_of = jnp.zeros((slot_count, tokens), jnp.float32)
    matches = []
    for k in range(top_count):
        route = routes[k : k + 1, :]
        pick = picks[k : k + 1, :].astype(jnp.float32)
        chosen = pick - copies * jnp.floor((pick + 0.5) / copies)
        match = (route == plan) & (chosen == ordinal) & (route < expert_count)
        matches.append(match)
        reach = jnp.where(match, 1.0, reach)
        gate_of = jnp.where(match, gates[k : k + 1, :], gate_of)
    before = lax.broadcasted_iota(jnp.int32, (tokens, tokens), 0) < lax.broadcasted_iota(
        jnp.int32, (tokens, tokens), 1
    )
    rank = lax.dot_general(
        reach.astype(jnp.bfloat16),
        jnp.where(before, 1.0, 0.0).astype(jnp.bfloat16),
        (((1,), (0,)), ((), ())),
        preferred_element_type=jnp.float32,
    ).astype(jnp.int32)
    kept = (reach > 0.0) & (rank < cap_rows)
    rank = jnp.where(kept, rank, -1)
    rank_out[...] = rank
    for k in range(top_count):
        slot_out[k : k + 1, :] = (
            jnp.sum(jnp.where(matches[k] & kept, slot_ids + 1, 0), axis=0, keepdims=True) - 1
        )
    row_ids = lax.broadcasted_iota(jnp.int32, spread.shape[1:], 0)
    for s in range(slot_count):
        placed = jnp.where(row_ids == rank[s : s + 1, :], gate_of[s : s + 1, :], 0.0)
        spread[seat[0] ^ s] = placed.astype(jnp.bfloat16)


def place_routes(routes, picks, gates, replica_plan, seat, expert_count, cap_rows, held_rows):
    slot_count = replica_plan.shape[0]
    top_count, tokens = routes.shape
    vmem = pl.BlockSpec(memory_space=pltpu.VMEM)
    return pl.pallas_call(
        functools.partial(route_kernel, expert_count, cap_rows),
        out_shape=(
            jax.ShapeDtypeStruct((slot_count, held_rows, tokens), jnp.bfloat16),
            jax.ShapeDtypeStruct((slot_count, tokens), jnp.int32),
            jax.ShapeDtypeStruct((top_count, tokens), jnp.int32),
        ),
        in_specs=[pl.BlockSpec(memory_space=pltpu.SMEM)] + [vmem] * 5,
        out_specs=(vmem, vmem, vmem),
    )(seat, replica_plan.reshape(slot_count, 1), replica_plan.reshape(1, slot_count), routes, picks, gates)


def send_all_kernel(seat, spread, rows, *rest):
    out = rest[-1]
    held_rows, tokens = spread.shape[1:]
    total = jnp.dot(spread[...].reshape(-1, tokens), rows[...], preferred_element_type=jnp.float32)
    for d in range(spread.shape[0]):
        out[seat[0] ^ d] = total[d * held_rows : (d + 1) * held_rows].astype(jnp.bfloat16)


def all_rows_to_send(spread, out_grad, seat, span, after):
    slot_count, held_rows, tokens = spread.shape
    start, stop = span
    return pl.pallas_call(
        send_all_kernel,
        grid=((stop - start) // TILE,),
        in_specs=[
            pl.BlockSpec(memory_space=pltpu.SMEM),
            pl.BlockSpec((slot_count, held_rows, tokens), lambda j: (0, 0, 0)),
            pl.BlockSpec((tokens, TILE), lambda j: (0, start // TILE + j)),
        ]
        + [pl.BlockSpec(memory_space=pl.ANY)] * len(after),
        out_specs=pl.BlockSpec((slot_count, held_rows, TILE), lambda j: (0, 0, j)),
        out_shape=jax.ShapeDtypeStruct((slot_count, held_rows, stop - start), jnp.bfloat16),
        cost_estimate=LITTLE,
    )(seat, spread, out_grad, *after)


def weight_kernel(units, rows, out):
    flat = rows[...].reshape(-1, rows.shape[-1])
    out[...] = jnp.dot(units[...], flat, preferred_element_type=jnp.float32).astype(jnp.bfloat16)


def weight_part(units, rows):
    slot_count, held_rows, width = rows.shape
    hidden, held = units.shape
    return pl.pallas_call(
        weight_kernel,
        grid=(width // TILE,),
        in_specs=[
            pl.BlockSpec((hidden, held), lambda j: (0, 0)),
            pl.BlockSpec((slot_count, held_rows, TILE), lambda j: (0, 0, j)),
        ],
        out_specs=pl.BlockSpec((hidden, TILE), lambda j: (0, j)),
        out_shape=jax.ShapeDtypeStruct((hidden, width), jnp.bfloat16),
        cost_estimate=LITTLE,
    )(units, rows)


def hold_kernel(*refs):
    pass


def hold(array, after):
    return pl.pallas_call(
        hold_kernel,
        in_specs=[pl.BlockSpec(memory_space=pl.ANY)] * 2,
        out_specs=pl.BlockSpec(memory_space=pl.ANY),
        out_shape=jax.ShapeDtypeStruct(array.shape, array.dtype),
        input_output_aliases={0: 0},
        cost_estimate=LITTLE,
    )(array, after)


def return_kernel(score, rank, slot_of, gates, out):
    slot_count, cap_rows = score.shape
    top_count, tokens = slot_of.shape
    row_ids = lax.broadcasted_iota(jnp.int32, (cap_rows, tokens), 0)
    total = jnp.zeros((top_count, tokens), jnp.float32)
    for s in range(slot_count):
        onehot = jnp.where(row_ids == rank[s : s + 1, :], 1.0, 0.0)
        value = lax.dot_general(
            score[s : s + 1, :],
            onehot,
            (((1,), (0,)), ((), ())),
            precision=lax.Precision.HIGHEST,
            preferred_element_type=jnp.float32,
        )
        total = jnp.where(slot_of[...] == s, value, total)
    held_gate = gates[...].astype(jnp.bfloat16).astype(jnp.float32)
    out[...] = jnp.where(slot_of[...] >= 0, total / held_gate, 0.0)


def matchings(slot_count):
    first = np.zeros((1 << slot_count,), np.int32)
    perms = []
    for four in itertools.combinations(range(slot_count), 4):
        first[sum(1 << s for s in four)] = len(perms)
        for other in range(3):
            rest = [four[1 + i] for i in range(3) if i != other]
            pairs = ((four[0], four[1 + other]), tuple(rest))
            perms.append([(a, b) for a, b in pairs] + [(b, a) for a, b in pairs])
    return first, perms


def matching_index(replica_plan, first):
    slot_ids, same_expert, ordinal = slot_layout(replica_plan)
    hot = jnp.sum(same_expert, axis=1) > 1
    mask = jnp.sum(jnp.where(hot, 1 << slot_ids, 0))
    least = jnp.min(jnp.where(hot, slot_ids, slot_ids.shape[0]))
    expert = jnp.sum(jnp.where(slot_ids == least, replica_plan, 0))
    partner = jnp.max(jnp.where(replica_plan == expert, slot_ids, 0))
    between = jnp.sum(hot & (slot_ids > least) & (slot_ids < partner))
    base = jnp.sum(jnp.where(jnp.arange(first.shape[0]) == mask, jnp.asarray(first), 0))
    return base + between


def sum_copies_any(group_sum, replica_plan):
    slot_ids, same_expert, ordinal = slot_layout(replica_plan)
    copies = jnp.sum(same_expert, axis=1)
    hot_first = (copies > 1) & (ordinal == 0)
    hot_rank = jnp.sum(hot_first[None, :] & (replica_plan[None, :] < replica_plan[:, None]), axis=1)
    my_slot = slot_ids == lax.axis_index("expert")
    my_rank = jnp.sum(jnp.where(my_slot, hot_rank, 0))
    my_hot = jnp.any(my_slot & (copies > 1))
    place_hot = (jnp.arange(HOT, dtype=jnp.int32) == my_rank) & my_hot
    group_f = group_sum.astype(jnp.float32)
    table = jnp.where(place_hot[:, None, None], group_f[None], 0.0)
    summed = lax.psum(table.astype(jnp.bfloat16), "expert").astype(jnp.float32)
    picked = jnp.sum(jnp.where(place_hot[:, None, None], summed, 0.0), axis=0)
    return jnp.where(my_hot, picked, group_f).astype(jnp.bfloat16)


def local(out_grad, gates, routes, copy_pick, replica_plan, down_weight, saved_hidden):
    slot_count = replica_plan.shape[0]
    cap_rows = saved_hidden.shape[3]
    expert_count = slot_count - slot_count // 4
    model_width = out_grad.shape[1]
    hidden_units = down_weight.shape[1]
    group_size = lax.axis_size("group")
    shard_rows = hidden_units // group_size

    seat = lax.axis_index("expert").astype(jnp.int32).reshape(1)
    held_rows = -(-cap_rows // 16) * 16
    pad = ((0, 0), (0, held_rows - cap_rows), (0, 0))
    held_hidden = jnp.pad(saved_hidden[0, 0], pad).reshape(slot_count * held_rows, hidden_units)

    spread, rank, slot_of = place_routes(
        routes.T, copy_pick.T, gates.T, replica_plan, seat, expert_count, cap_rows, held_rows
    )

    edges = np.cumsum((0,) + CHUNKS)
    spans = [(int(a), int(b)) for a, b in zip(edges[:-1], edges[1:])]
    ready = [all_rows_to_send(spread, out_grad, seat, span, []) for span in spans]
    units = held_hidden.T
    group_sum, projected, rows = [], [], None
    for span, sent in zip(spans, ready):
        sent = sent if rows is None else hold(sent, rows)
        rows = lax.all_to_all(sent, "expert", split_axis=0, concat_axis=0, tiled=True)
        flat = rows.reshape(slot_count * held_rows, -1)
        partial = weight_part(units, rows)
        group_sum.append(lax.psum_scatter(partial, "group", scatter_dimension=0, tiled=True))
        projected.append(
            lax.dot_general(
                flat,
                down_weight[0, :, span[0] : span[1]],
                (((1,), (1,)), ((), ())),
                preferred_element_type=jnp.float32,
            )
        )
    projected = sum(projected)

    route_score = jnp.sum(projected * held_hidden.astype(jnp.float32), axis=1)
    returned = lax.all_to_all(
        route_score.reshape(slot_count, held_rows), "expert", split_axis=0, concat_axis=0, tiled=True
    )
    route_grad = pl.pallas_call(
        return_kernel, out_shape=jax.ShapeDtypeStruct(gates.T.shape, jnp.float32)
    )(returned, rank, slot_of, gates.T).T
    hidden_grad = projected.astype(jnp.bfloat16).reshape(slot_count, held_rows, hidden_units)[:, :cap_rows]

    group_sum = jnp.concatenate(group_sum, axis=1)
    if slot_count - expert_count == HOT:
        first, perms = matchings(slot_count)
        other = lax.switch(
            matching_index(replica_plan, first),
            [functools.partial(lax.ppermute, axis_name="expert", perm=perm) for perm in perms],
            group_sum,
        )
        copy_grad = (group_sum.astype(jnp.float32) + other.astype(jnp.float32)).astype(jnp.bfloat16)
    else:
        copy_grad = sum_copies_any(group_sum, replica_plan)
    return (route_grad, hidden_grad[None, None], copy_grad.reshape(1, shard_rows, model_width))


def solution(mesh):
    placed = (
        P(("group", "expert"), None),
        P(("group", "expert"), None),
        P(("group", "expert"), None),
        P(("group", "expert"), None),
        P(),
        P("expert", None, None),
        P("group", "expert", None, None, None),
    )
    return jax.shard_map(
        local,
        mesh=mesh,
        in_specs=placed,
        out_specs=(
            P(("group", "expert"), None),
            P("group", "expert", None, None, None),
            P("expert", "group", None),
        ),
        check_vma=False,
    )
```

```python
import functools
import itertools

import jax
import jax.numpy as jnp
import numpy as np
from jax import lax
from jax.experimental import pallas as pl
from jax.experimental.pallas import tpu as pltpu
from jax.sharding import PartitionSpec as P

HOT = 2
TILE = 512


def cost(flops):
    return pl.CostEstimate(flops=flops, bytes_accessed=flops // 300, transcendentals=0)
CHUNKS = (2048, 1024, 512)


def slot_layout(replica_plan):
    slot_count = replica_plan.shape[0]
    slot_ids = jnp.arange(slot_count, dtype=jnp.int32)
    same_expert = replica_plan[:, None] == replica_plan[None, :]
    earlier_slot = slot_ids[None, :] < slot_ids[:, None]
    ordinal = jnp.sum(same_expert & earlier_slot, axis=1)
    return (slot_ids, same_expert, ordinal)


def route_kernel(
    expert_count, cap_rows, seat, plan_col, plan_row, routes, picks, gates, spread, rank_out, slot_out
):
    slot_count = plan_col.shape[0]
    top_count, tokens = routes.shape
    plan = plan_col[...]
    same = plan == plan_row[...]
    slot_r = lax.broadcasted_iota(jnp.int32, (slot_count, slot_count), 0)
    slot_c = lax.broadcasted_iota(jnp.int32, (slot_count, slot_count), 1)
    copies = jnp.sum(jnp.where(same, 1.0, 0.0), axis=1, keepdims=True)
    ordinal = jnp.sum(jnp.where(same & (slot_c < slot_r), 1.0, 0.0), axis=1, keepdims=True)
    slot_ids = lax.broadcasted_iota(jnp.int32, (slot_count, tokens), 0)
    reach = jnp.zeros((slot_count, tokens), jnp.float32)
    gate_of = jnp.zeros((slot_count, tokens), jnp.float32)
    matches = []
    for k in range(top_count):
        route = routes[k : k + 1, :]
        pick = picks[k : k + 1, :].astype(jnp.float32)
        chosen = pick - copies * jnp.floor((pick + 0.5) / copies)
        match = (route == plan) & (chosen == ordinal) & (route < expert_count)
        matches.append(match)
        reach = jnp.where(match, 1.0, reach)
        gate_of = jnp.where(match, gates[k : k + 1, :], gate_of)
    before = lax.broadcasted_iota(jnp.int32, (tokens, tokens), 0) < lax.broadcasted_iota(
        jnp.int32, (tokens, tokens), 1
    )
    rank = lax.dot_general(
        reach.astype(jnp.bfloat16),
        jnp.where(before, 1.0, 0.0).astype(jnp.bfloat16),
        (((1,), (0,)), ((), ())),
        preferred_element_type=jnp.float32,
    ).astype(jnp.int32)
    kept = (reach > 0.0) & (rank < cap_rows)
    rank = jnp.where(kept, rank, -1)
    rank_out[...] = rank
    for k in range(top_count):
        slot_out[k : k + 1, :] = (
            jnp.sum(jnp.where(matches[k] & kept, slot_ids + 1, 0), axis=0, keepdims=True) - 1
        )
    row_ids = lax.broadcasted_iota(jnp.int32, spread.shape[1:], 0)
    for s in range(slot_count):
        placed = jnp.where(row_ids == rank[s : s + 1, :], gate_of[s : s + 1, :], 0.0)
        spread[seat[0] ^ s] = placed.astype(jnp.bfloat16)


def place_routes(routes, picks, gates, replica_plan, seat, expert_count, cap_rows, held_rows):
    slot_count = replica_plan.shape[0]
    top_count, tokens = routes.shape
    vmem = pl.BlockSpec(memory_space=pltpu.VMEM)
    return pl.pallas_call(
        functools.partial(route_kernel, expert_count, cap_rows),
        out_shape=(
            jax.ShapeDtypeStruct((slot_count, held_rows, tokens), jnp.bfloat16),
            jax.ShapeDtypeStruct((slot_count, tokens), jnp.int32),
            jax.ShapeDtypeStruct((top_count, tokens), jnp.int32),
        ),
        in_specs=[pl.BlockSpec(memory_space=pltpu.SMEM)] + [vmem] * 5,
        out_specs=(vmem, vmem, vmem),
    )(seat, replica_plan.reshape(slot_count, 1), replica_plan.reshape(1, slot_count), routes, picks, gates)


def send_all_kernel(seat, spread, rows, *rest):
    out = rest[-1]
    held_rows, tokens = spread.shape[1:]
    total = jnp.dot(spread[...].reshape(-1, tokens), rows[...], preferred_element_type=jnp.float32)
    for d in range(spread.shape[0]):
        out[seat[0] ^ d] = total[d * held_rows : (d + 1) * held_rows].astype(jnp.bfloat16)


def all_rows_to_send(spread, out_grad, seat, span, after):
    slot_count, held_rows, tokens = spread.shape
    start, stop = span
    return pl.pallas_call(
        send_all_kernel,
        grid=((stop - start) // TILE,),
        in_specs=[
            pl.BlockSpec(memory_space=pltpu.SMEM),
            pl.BlockSpec((slot_count, held_rows, tokens), lambda j: (0, 0, 0)),
            pl.BlockSpec((tokens, TILE), lambda j: (0, start // TILE + j)),
        ]
        + [pl.BlockSpec(memory_space=pl.ANY)] * len(after),
        out_specs=pl.BlockSpec((slot_count, held_rows, TILE), lambda j: (0, 0, j)),
        out_shape=jax.ShapeDtypeStruct((slot_count, held_rows, stop - start), jnp.bfloat16),
        cost_estimate=cost(2 * slot_count * held_rows * tokens * (stop - start)),
    )(seat, spread, out_grad, *after)


def part_kernel(leave, rows, *rest):
    flat = rows[...].reshape(-1, rows.shape[-1])
    rest[-1][...] = jnp.dot(leave[...], flat, preferred_element_type=jnp.float32).astype(jnp.bfloat16)


def other_core_part(leave, rows, after):
    slot_count, held_rows, width = rows.shape
    units, held = leave.shape
    return pl.pallas_call(
        part_kernel,
        grid=(width // TILE,),
        in_specs=[
            pl.BlockSpec((units, held), lambda j: (0, 0)),
            pl.BlockSpec((slot_count, held_rows, TILE), lambda j: (0, 0, j)),
        ]
        + [pl.BlockSpec(memory_space=pl.ANY)] * len(after),
        out_specs=pl.BlockSpec((units, TILE), lambda j: (0, j)),
        out_shape=jax.ShapeDtypeStruct((units, width), jnp.bfloat16),
        cost_estimate=cost(2 * units * held * width),
    )(leave, rows, *after)


def near_kernel(chips, stay, rows, near, *rest):
    mine, *others = rest[-chips:]
    flat = rows[...].reshape(-1, rows.shape[-1])
    shard = mine.shape[0]
    total = jnp.dot(stay[...], flat, preferred_element_type=jnp.float32) + near[...].astype(jnp.float32)
    mine[...] = total[:shard]
    for d, other in enumerate(others):
        other[...] = total[(d + 1) * shard : (d + 2) * shard].astype(jnp.bfloat16)


def add_near(stay, rows, near, chips, after):
    units, held = stay.shape
    width = rows.shape[-1]
    shard = units // chips
    return pl.pallas_call(
        functools.partial(near_kernel, chips),
        grid=(width // TILE,),
        in_specs=[
            pl.BlockSpec((units, held), lambda j: (0, 0)),
            pl.BlockSpec(rows.shape[:2] + (TILE,), lambda j: (0, 0, j)),
            pl.BlockSpec((units, TILE), lambda j: (0, j)),
        ]
        + [pl.BlockSpec(memory_space=pl.ANY)] * len(after),
        out_specs=(pl.BlockSpec((shard, TILE), lambda j: (0, j)),) * chips,
        out_shape=(jax.ShapeDtypeStruct((shard, width), jnp.float32),)
        + (jax.ShapeDtypeStruct((shard, width), jnp.bfloat16),) * (chips - 1),
        cost_estimate=cost(2 * units * held * width),
    )(stay, rows, near, *after)


def hold_kernel(*refs):
    pass


def hold(array, after):
    return pl.pallas_call(
        hold_kernel,
        in_specs=[pl.BlockSpec(memory_space=pl.ANY)] * (1 + len(after)),
        out_specs=pl.BlockSpec(memory_space=pl.ANY),
        out_shape=jax.ShapeDtypeStruct(array.shape, array.dtype),
        input_output_aliases={0: 0},
        cost_estimate=cost(1),
    )(array, *after)


def return_kernel(score, rank, slot_of, gates, out):
    slot_count, cap_rows = score.shape
    top_count, tokens = slot_of.shape
    row_ids = lax.broadcasted_iota(jnp.int32, (cap_rows, tokens), 0)
    total = jnp.zeros((top_count, tokens), jnp.float32)
    for s in range(slot_count):
        onehot = jnp.where(row_ids == rank[s : s + 1, :], 1.0, 0.0)
        value = lax.dot_general(
            score[s : s + 1, :],
            onehot,
            (((1,), (0,)), ((), ())),
            precision=lax.Precision.HIGHEST,
            preferred_element_type=jnp.float32,
        )
        total = jnp.where(slot_of[...] == s, value, total)
    held_gate = gates[...].astype(jnp.bfloat16).astype(jnp.float32)
    out[...] = jnp.where(slot_of[...] >= 0, total / held_gate, 0.0)


def matchings(slot_count):
    first = np.zeros((1 << slot_count,), np.int32)
    perms = []
    for four in itertools.combinations(range(slot_count), 4):
        first[sum(1 << s for s in four)] = len(perms)
        for other in range(3):
            rest = [four[1 + i] for i in range(3) if i != other]
            pairs = ((four[0], four[1 + other]), tuple(rest))
            perms.append([(a, b) for a, b in pairs] + [(b, a) for a, b in pairs])
    return first, perms


def matching_index(replica_plan, first):
    slot_ids, same_expert, ordinal = slot_layout(replica_plan)
    hot = jnp.sum(same_expert, axis=1) > 1
    mask = jnp.sum(jnp.where(hot, 1 << slot_ids, 0))
    least = jnp.min(jnp.where(hot, slot_ids, slot_ids.shape[0]))
    expert = jnp.sum(jnp.where(slot_ids == least, replica_plan, 0))
    partner = jnp.max(jnp.where(replica_plan == expert, slot_ids, 0))
    between = jnp.sum(hot & (slot_ids > least) & (slot_ids < partner))
    base = jnp.sum(jnp.where(jnp.arange(first.shape[0]) == mask, jnp.asarray(first), 0))
    return base + between


def sum_copies_any(group_sum, replica_plan):
    slot_ids, same_expert, ordinal = slot_layout(replica_plan)
    copies = jnp.sum(same_expert, axis=1)
    hot_first = (copies > 1) & (ordinal == 0)
    hot_rank = jnp.sum(hot_first[None, :] & (replica_plan[None, :] < replica_plan[:, None]), axis=1)
    my_slot = slot_ids == lax.axis_index("expert")
    my_rank = jnp.sum(jnp.where(my_slot, hot_rank, 0))
    my_hot = jnp.any(my_slot & (copies > 1))
    place_hot = (jnp.arange(HOT, dtype=jnp.int32) == my_rank) & my_hot
    group_f = group_sum.astype(jnp.float32)
    table = jnp.where(place_hot[:, None, None], group_f[None], 0.0)
    summed = lax.psum(table.astype(jnp.bfloat16), "expert").astype(jnp.float32)
    picked = jnp.sum(jnp.where(place_hot[:, None, None], summed, 0.0), axis=0)
    return jnp.where(my_hot, picked, group_f).astype(jnp.bfloat16)


def local(out_grad, gates, routes, copy_pick, replica_plan, down_weight, saved_hidden):
    slot_count = replica_plan.shape[0]
    cap_rows = saved_hidden.shape[3]
    expert_count = slot_count - slot_count // 4
    model_width = out_grad.shape[1]
    hidden_units = down_weight.shape[1]
    group_size = lax.axis_size("group")
    chips = group_size // 2
    shard_rows = hidden_units // group_size
    me = lax.axis_index("group")
    chip, core = me // 2, me % 2

    seat = lax.axis_index("expert").astype(jnp.int32).reshape(1)
    held_rows = -(-cap_rows // 16) * 16
    pad = ((0, 0), (0, held_rows - cap_rows), (0, 0))
    held_hidden = jnp.pad(saved_hidden[0, 0], pad).reshape(slot_count * held_rows, hidden_units)

    spread, rank, slot_of = place_routes(
        routes.T, copy_pick.T, gates.T, replica_plan, seat, expert_count, cap_rows, held_rows
    )

    by_owner = held_hidden.T.reshape(chips, 2, shard_rows, -1)
    by_owner = jnp.stack([by_owner[chip ^ d] for d in range(chips)])
    stay = by_owner[:, core].reshape(hidden_units // 2, -1)
    leave = by_owner[:, 1 - core].reshape(hidden_units // 2, -1)

    edges = np.cumsum((0,) + CHUNKS)
    spans = [(int(a), int(b)) for a, b in zip(edges[:-1], edges[1:])]
    ready = [all_rows_to_send(spread, out_grad, seat, span, []) for span in spans]
    group_sum, projected = [], []
    rows, far, others, early = None, [], [], []
    for span, sent in zip(spans, ready):
        if rows is not None:
            sent = hold(sent, [rows] + early)
        early = others[:1]
        rows = lax.all_to_all(sent, "expert", split_axis=0, concat_axis=0, tiled=True)
        away = other_core_part(leave, rows, others[:1])
        near = lax.ppermute(away, "group", [(i, i ^ 1) for i in range(group_size)])
        mine, *others = add_near(stay, rows, near, chips, far[:1])
        far = [
            lax.ppermute(other, "group", [(i, i ^ (2 * d + 2)) for i in range(group_size)])
            for d, other in enumerate(others)
        ]
        group_sum.append(sum((f.astype(jnp.float32) for f in far), mine).astype(jnp.bfloat16))
        projected.append(
            lax.dot_general(
                rows.reshape(slot_count * held_rows, -1),
                down_weight[0, :, span[0] : span[1]],
                (((1,), (1,)), ((), ())),
                preferred_element_type=jnp.float32,
            )
        )
    projected = sum(projected)

    route_score = jnp.sum(projected * held_hidden.astype(jnp.float32), axis=1)
    returned = lax.all_to_all(
        route_score.reshape(slot_count, held_rows), "expert", split_axis=0, concat_axis=0, tiled=True
    )
    route_grad = pl.pallas_call(
        return_kernel, out_shape=jax.ShapeDtypeStruct(gates.T.shape, jnp.float32)
    )(returned, rank, slot_of, gates.T).T
    hidden_grad = projected.astype(jnp.bfloat16).reshape(slot_count, held_rows, hidden_units)[:, :cap_rows]

    group_sum = jnp.concatenate(group_sum, axis=1)
    if slot_count - expert_count == HOT:
        first, perms = matchings(slot_count)
        other = lax.switch(
            matching_index(replica_plan, first),
            [functools.partial(lax.ppermute, axis_name="expert", perm=perm) for perm in perms],
            group_sum,
        )
        copy_grad = (group_sum.astype(jnp.float32) + other.astype(jnp.float32)).astype(jnp.bfloat16)
    else:
        copy_grad = sum_copies_any(group_sum, replica_plan)
    return (route_grad, hidden_grad[None, None], copy_grad.reshape(1, shard_rows, model_width))


def solution(mesh):
    placed = (
        P(("group", "expert"), None),
        P(("group", "expert"), None),
        P(("group", "expert"), None),
        P(("group", "expert"), None),
        P(),
        P("expert", None, None),
        P("group", "expert", None, None, None),
    )
    return jax.shard_map(
        local,
        mesh=mesh,
        in_specs=placed,
        out_specs=(
            P(("group", "expert"), None),
            P("group", "expert", None, None, None),
            P("expert", "group", None),
        ),
        check_vma=False,
    )
```

```python
import functools
import itertools

import jax
import jax.numpy as jnp
import numpy as np
from jax import lax
from jax.experimental import pallas as pl
from jax.experimental.pallas import tpu as pltpu
from jax.sharding import PartitionSpec as P

HOT = 2
TILE = 512


def cost(flops):
    return pl.CostEstimate(flops=flops, bytes_accessed=flops // 300, transcendentals=0)
CHUNKS = (2048, 1024, 512)


def slot_layout(replica_plan):
    slot_count = replica_plan.shape[0]
    slot_ids = jnp.arange(slot_count, dtype=jnp.int32)
    same_expert = replica_plan[:, None] == replica_plan[None, :]
    earlier_slot = slot_ids[None, :] < slot_ids[:, None]
    ordinal = jnp.sum(same_expert & earlier_slot, axis=1)
    return (slot_ids, same_expert, ordinal)


def route_kernel(
    expert_count, cap_rows, seat, slot_plan, plan_row, routes, picks, gates, spread, rank_out, slot_out
):
    slot_count = plan_row.shape[1]
    top_count, tokens = routes.shape
    column = lax.broadcasted_iota(jnp.int32, (slot_count, 1), 0)
    plan = jnp.zeros((slot_count, 1), jnp.int32)
    for s in range(slot_count):
        plan = jnp.where(column == s, slot_plan[s], plan)
    same = plan == plan_row[...]
    slot_r = lax.broadcasted_iota(jnp.int32, (slot_count, slot_count), 0)
    slot_c = lax.broadcasted_iota(jnp.int32, (slot_count, slot_count), 1)
    copies = jnp.sum(jnp.where(same, 1.0, 0.0), axis=1, keepdims=True)
    ordinal = jnp.sum(jnp.where(same & (slot_c < slot_r), 1.0, 0.0), axis=1, keepdims=True)
    slot_ids = lax.broadcasted_iota(jnp.int32, (slot_count, tokens), 0)
    reach = jnp.zeros((slot_count, tokens), jnp.float32)
    gate_of = jnp.zeros((slot_count, tokens), jnp.float32)
    matches = []
    for k in range(top_count):
        route = routes[k : k + 1, :]
        pick = picks[k : k + 1, :].astype(jnp.float32)
        chosen = pick - copies * jnp.floor((pick + 0.5) / copies)
        match = (route == plan) & (chosen == ordinal) & (route < expert_count)
        matches.append(match)
        reach = jnp.where(match, 1.0, reach)
        gate_of = jnp.where(match, gates[k : k + 1, :], gate_of)
    before = lax.broadcasted_iota(jnp.int32, (tokens, tokens), 0) < lax.broadcasted_iota(
        jnp.int32, (tokens, tokens), 1
    )
    rank = lax.dot_general(
        reach.astype(jnp.bfloat16),
        jnp.where(before, 1.0, 0.0).astype(jnp.bfloat16),
        (((1,), (0,)), ((), ())),
        preferred_element_type=jnp.float32,
    ).astype(jnp.int32)
    kept = (reach > 0.0) & (rank < cap_rows)
    rank = jnp.where(kept, rank, -1)
    rank_out[...] = rank
    for k in range(top_count):
        slot_out[k : k + 1, :] = (
            jnp.sum(jnp.where(matches[k] & kept, slot_ids + 1, 0), axis=0, keepdims=True) - 1
        )
    row_ids = lax.broadcasted_iota(jnp.int32, spread.shape[1:], 0)
    for s in range(slot_count):
        placed = jnp.where(row_ids == rank[s : s + 1, :], gate_of[s : s + 1, :], 0.0)
        spread[seat[0] ^ s] = placed.astype(jnp.bfloat16)


def place_routes(routes, picks, gates, replica_plan, seat, expert_count, cap_rows, held_rows):
    slot_count = replica_plan.shape[0]
    top_count, tokens = routes.shape
    vmem = pl.BlockSpec(memory_space=pltpu.VMEM)
    return pl.pallas_call(
        functools.partial(route_kernel, expert_count, cap_rows),
        out_shape=(
            jax.ShapeDtypeStruct((slot_count, held_rows, tokens), jnp.bfloat16),
            jax.ShapeDtypeStruct((slot_count, tokens), jnp.int32),
            jax.ShapeDtypeStruct((top_count, tokens), jnp.int32),
        ),
        in_specs=[pl.BlockSpec(memory_space=pltpu.SMEM)] * 2 + [vmem] * 4,
        out_specs=(vmem, vmem, vmem),
    )(seat, replica_plan, replica_plan.reshape(1, slot_count), routes, picks, gates)


def send_all_kernel(seat, spread, rows, *rest):
    out = rest[-1]
    held_rows, tokens = spread.shape[1:]
    total = jnp.dot(spread[...].reshape(-1, tokens), rows[...], preferred_element_type=jnp.float32)
    for d in range(spread.shape[0]):
        out[seat[0] ^ d] = total[d * held_rows : (d + 1) * held_rows].astype(jnp.bfloat16)


def all_rows_to_send(spread, out_grad, seat, span, after):
    slot_count, held_rows, tokens = spread.shape
    start, stop = span
    return pl.pallas_call(
        send_all_kernel,
        grid=((stop - start) // TILE,),
        in_specs=[
            pl.BlockSpec(memory_space=pltpu.SMEM),
            pl.BlockSpec((slot_count, held_rows, tokens), lambda j: (0, 0, 0)),
            pl.BlockSpec((tokens, TILE), lambda j: (0, start // TILE + j)),
        ]
        + [pl.BlockSpec(memory_space=pl.ANY)] * len(after),
        out_specs=pl.BlockSpec((slot_count, held_rows, TILE), lambda j: (0, 0, j)),
        out_shape=jax.ShapeDtypeStruct((slot_count, held_rows, stop - start), jnp.bfloat16),
        cost_estimate=cost(2 * slot_count * held_rows * tokens * (stop - start)),
    )(seat, spread, out_grad, *after)


def part_kernel(leave, rows, *rest):
    flat = rows[...].reshape(-1, rows.shape[-1])
    rest[-1][...] = jnp.dot(leave[...], flat, preferred_element_type=jnp.float32).astype(jnp.bfloat16)


def other_core_part(leave, rows, after):
    slot_count, held_rows, width = rows.shape
    units, held = leave.shape
    return pl.pallas_call(
        part_kernel,
        grid=(width // TILE,),
        in_specs=[
            pl.BlockSpec((units, held), lambda j: (0, 0)),
            pl.BlockSpec((slot_count, held_rows, TILE), lambda j: (0, 0, j)),
        ]
        + [pl.BlockSpec(memory_space=pl.ANY)] * len(after),
        out_specs=pl.BlockSpec((units, TILE), lambda j: (0, j)),
        out_shape=jax.ShapeDtypeStruct((units, width), jnp.bfloat16),
        cost_estimate=cost(2 * units * held * width),
    )(leave, rows, *after)


def near_kernel(chips, stay, rows, near, *rest):
    mine, *others = rest[-chips:]
    flat = rows[...].reshape(-1, rows.shape[-1])
    shard = mine.shape[0]
    total = jnp.dot(stay[...], flat, preferred_element_type=jnp.float32) + near[...].astype(jnp.float32)
    mine[...] = total[:shard]
    for d, other in enumerate(others):
        other[...] = total[(d + 1) * shard : (d + 2) * shard].astype(jnp.bfloat16)


def add_near(stay, rows, near, chips, after):
    units, held = stay.shape
    width = rows.shape[-1]
    shard = units // chips
    return pl.pallas_call(
        functools.partial(near_kernel, chips),
        grid=(width // TILE,),
        in_specs=[
            pl.BlockSpec((units, held), lambda j: (0, 0)),
            pl.BlockSpec(rows.shape[:2] + (TILE,), lambda j: (0, 0, j)),
            pl.BlockSpec((units, TILE), lambda j: (0, j)),
        ]
        + [pl.BlockSpec(memory_space=pl.ANY)] * len(after),
        out_specs=(pl.BlockSpec((shard, TILE), lambda j: (0, j)),) * chips,
        out_shape=(jax.ShapeDtypeStruct((shard, width), jnp.float32),)
        + (jax.ShapeDtypeStruct((shard, width), jnp.bfloat16),) * (chips - 1),
        cost_estimate=cost(2 * units * held * width),
    )(stay, rows, near, *after)


def hold_kernel(*refs):
    pass


def hold(array, after):
    return pl.pallas_call(
        hold_kernel,
        in_specs=[pl.BlockSpec(memory_space=pl.ANY)] * (1 + len(after)),
        out_specs=pl.BlockSpec(memory_space=pl.ANY),
        out_shape=jax.ShapeDtypeStruct(array.shape, array.dtype),
        input_output_aliases={0: 0},
        cost_estimate=cost(1),
    )(array, *after)


def return_kernel(score, rank, slot_of, gates, out):
    slot_count, cap_rows = score.shape
    top_count, tokens = slot_of.shape
    row_ids = lax.broadcasted_iota(jnp.int32, (cap_rows, tokens), 0)
    total = jnp.zeros((top_count, tokens), jnp.float32)
    for s in range(slot_count):
        onehot = jnp.where(row_ids == rank[s : s + 1, :], 1.0, 0.0)
        value = lax.dot_general(
            score[s : s + 1, :],
            onehot,
            (((1,), (0,)), ((), ())),
            precision=lax.Precision.HIGHEST,
            preferred_element_type=jnp.float32,
        )
        total = jnp.where(slot_of[...] == s, value, total)
    held_gate = gates[...].astype(jnp.bfloat16).astype(jnp.float32)
    out[...] = jnp.where(slot_of[...] >= 0, total / held_gate, 0.0)


def matchings(slot_count):
    first = np.zeros((1 << slot_count,), np.int32)
    perms = []
    for four in itertools.combinations(range(slot_count), 4):
        first[sum(1 << s for s in four)] = len(perms)
        for other in range(3):
            rest = [four[1 + i] for i in range(3) if i != other]
            pairs = ((four[0], four[1 + other]), tuple(rest))
            perms.append([(a, b) for a, b in pairs] + [(b, a) for a, b in pairs])
    return first, perms


def matching_index(replica_plan, first):
    slot_ids, same_expert, ordinal = slot_layout(replica_plan)
    hot = jnp.sum(same_expert, axis=1) > 1
    mask = jnp.sum(jnp.where(hot, 1 << slot_ids, 0))
    least = jnp.min(jnp.where(hot, slot_ids, slot_ids.shape[0]))
    expert = jnp.sum(jnp.where(slot_ids == least, replica_plan, 0))
    partner = jnp.max(jnp.where(replica_plan == expert, slot_ids, 0))
    between = jnp.sum(hot & (slot_ids > least) & (slot_ids < partner))
    base = jnp.sum(jnp.where(jnp.arange(first.shape[0]) == mask, jnp.asarray(first), 0))
    return base + between


def sum_copies_any(group_sum, replica_plan):
    slot_ids, same_expert, ordinal = slot_layout(replica_plan)
    copies = jnp.sum(same_expert, axis=1)
    hot_first = (copies > 1) & (ordinal == 0)
    hot_rank = jnp.sum(hot_first[None, :] & (replica_plan[None, :] < replica_plan[:, None]), axis=1)
    my_slot = slot_ids == lax.axis_index("expert")
    my_rank = jnp.sum(jnp.where(my_slot, hot_rank, 0))
    my_hot = jnp.any(my_slot & (copies > 1))
    place_hot = (jnp.arange(HOT, dtype=jnp.int32) == my_rank) & my_hot
    group_f = group_sum.astype(jnp.float32)
    table = jnp.where(place_hot[:, None, None], group_f[None], 0.0)
    summed = lax.psum(table.astype(jnp.bfloat16), "expert").astype(jnp.float32)
    picked = jnp.sum(jnp.where(place_hot[:, None, None], summed, 0.0), axis=0)
    return jnp.where(my_hot, picked, group_f).astype(jnp.bfloat16)


def local(out_grad, gates, routes, copy_pick, replica_plan, down_weight, saved_hidden):
    slot_count = replica_plan.shape[0]
    cap_rows = saved_hidden.shape[3]
    expert_count = slot_count - slot_count // 4
    model_width = out_grad.shape[1]
    hidden_units = down_weight.shape[1]
    group_size = lax.axis_size("group")
    chips = group_size // 2
    shard_rows = hidden_units // group_size
    me = lax.axis_index("group")
    chip, core = me // 2, me % 2

    seat = lax.axis_index("expert").astype(jnp.int32).reshape(1)
    held_rows = -(-cap_rows // 16) * 16
    pad = ((0, 0), (0, held_rows - cap_rows), (0, 0))
    held_hidden = jnp.pad(saved_hidden[0, 0], pad).reshape(slot_count * held_rows, hidden_units)

    spread, rank, slot_of = place_routes(
        routes.T, copy_pick.T, gates.T, replica_plan, seat, expert_count, cap_rows, held_rows
    )

    by_owner = held_hidden.T.reshape(chips, 2, shard_rows, -1)
    by_owner = jnp.stack([by_owner[chip ^ d] for d in range(chips)])
    stay = by_owner[:, core].reshape(hidden_units // 2, -1)
    leave = by_owner[:, 1 - core].reshape(hidden_units // 2, -1)

    edges = np.cumsum((0,) + CHUNKS)
    spans = [(int(a), int(b)) for a, b in zip(edges[:-1], edges[1:])]
    ready = [all_rows_to_send(spread, out_grad, seat, span, []) for span in spans]
    pairs = slot_count - expert_count == HOT
    if pairs:
        first, perms = matchings(slot_count)
        pairing = matching_index(replica_plan, first)
    group_sum, projected = [], jnp.zeros((slot_count * held_rows, hidden_units), jnp.float32)
    rows, far, others = None, [], []
    early = ready[2:] + ([pairing.reshape(1)] if pairs else [])
    for span, sent in zip(spans, ready):
        if rows is not None:
            sent = hold(sent, [rows] + early)
            early = others[:1] + [projected]
        rows = lax.all_to_all(sent, "expert", split_axis=0, concat_axis=0, tiled=True)
        away = other_core_part(leave, rows, others[:1])
        near = lax.ppermute(away, "group", [(i, i ^ 1) for i in range(group_size)])
        mine, *others = add_near(stay, rows, near, chips, far[:1])
        far = [
            lax.ppermute(other, "group", [(i, i ^ (2 * d + 2)) for i in range(group_size)])
            for d, other in enumerate(others)
        ]
        group_sum.append(sum((f.astype(jnp.float32) for f in far), mine).astype(jnp.bfloat16))
        projected = projected + lax.dot_general(
            rows.reshape(slot_count * held_rows, -1),
            down_weight[0, :, span[0] : span[1]],
            (((1,), (1,)), ((), ())),
            preferred_element_type=jnp.float32,
        )

    route_score = jnp.sum(projected * held_hidden.astype(jnp.float32), axis=1)
    returned = lax.all_to_all(
        hold(route_score.reshape(slot_count, held_rows), others[:1]),
        "expert",
        split_axis=0,
        concat_axis=0,
        tiled=True,
    )
    route_grad = pl.pallas_call(
        return_kernel, out_shape=jax.ShapeDtypeStruct(gates.T.shape, jnp.float32)
    )(returned, rank, slot_of, gates.T).T
    hidden_grad = projected.astype(jnp.bfloat16).reshape(slot_count, held_rows, hidden_units)[:, :cap_rows]

    group_sum = jnp.concatenate(group_sum, axis=1)
    if pairs:
        other = lax.switch(
            pairing,
            [functools.partial(lax.ppermute, axis_name="expert", perm=perm) for perm in perms],
            group_sum,
        )
        copy_grad = (group_sum.astype(jnp.float32) + other.astype(jnp.float32)).astype(jnp.bfloat16)
    else:
        copy_grad = sum_copies_any(group_sum, replica_plan)
    return (route_grad, hidden_grad[None, None], copy_grad.reshape(1, shard_rows, model_width))


def solution(mesh):
    placed = (
        P(("group", "expert"), None),
        P(("group", "expert"), None),
        P(("group", "expert"), None),
        P(("group", "expert"), None),
        P(),
        P("expert", None, None),
        P("group", "expert", None, None, None),
    )
    return jax.shard_map(
        local,
        mesh=mesh,
        in_specs=placed,
        out_specs=(
            P(("group", "expert"), None),
            P("group", "expert", None, None, None),
            P("expert", "group", None),
        ),
        check_vma=False,
    )
```

```python
import functools
import itertools

import jax
import jax.numpy as jnp
import numpy as np
from jax import lax
from jax.experimental import pallas as pl
from jax.experimental.pallas import tpu as pltpu
from jax.sharding import PartitionSpec as P

HOT = 2
TILE = 512


def cost(flops):
    return pl.CostEstimate(flops=flops, bytes_accessed=flops // 300, transcendentals=0)
CHUNKS = (2048, 1024, 512)


def slot_layout(replica_plan):
    slot_count = replica_plan.shape[0]
    slot_ids = jnp.arange(slot_count, dtype=jnp.int32)
    same_expert = replica_plan[:, None] == replica_plan[None, :]
    earlier_slot = slot_ids[None, :] < slot_ids[:, None]
    ordinal = jnp.sum(same_expert & earlier_slot, axis=1)
    return (slot_ids, same_expert, ordinal)


def route_kernel(
    expert_count, cap_rows, seat, slot_plan, plan_row, routes, picks, gates, spread, rank_out, slot_out
):
    slot_count = plan_row.shape[1]
    top_count, tokens = routes.shape
    column = lax.broadcasted_iota(jnp.int32, (slot_count, 1), 0)
    plan = jnp.zeros((slot_count, 1), jnp.int32)
    for s in range(slot_count):
        plan = jnp.where(column == s, slot_plan[s], plan)
    same = plan == plan_row[...]
    slot_r = lax.broadcasted_iota(jnp.int32, (slot_count, slot_count), 0)
    slot_c = lax.broadcasted_iota(jnp.int32, (slot_count, slot_count), 1)
    copies = jnp.sum(jnp.where(same, 1.0, 0.0), axis=1, keepdims=True)
    ordinal = jnp.sum(jnp.where(same & (slot_c < slot_r), 1.0, 0.0), axis=1, keepdims=True)
    slot_ids = lax.broadcasted_iota(jnp.int32, (slot_count, tokens), 0)
    reach = jnp.zeros((slot_count, tokens), jnp.float32)
    gate_of = jnp.zeros((slot_count, tokens), jnp.float32)
    matches = []
    for k in range(top_count):
        route = routes[k : k + 1, :]
        pick = picks[k : k + 1, :].astype(jnp.float32)
        chosen = pick - copies * jnp.floor((pick + 0.5) / copies)
        match = (route == plan) & (chosen == ordinal) & (route < expert_count)
        matches.append(match)
        reach = jnp.where(match, 1.0, reach)
        gate_of = jnp.where(match, gates[k : k + 1, :], gate_of)
    before = lax.broadcasted_iota(jnp.int32, (tokens, tokens), 0) < lax.broadcasted_iota(
        jnp.int32, (tokens, tokens), 1
    )
    rank = lax.dot_general(
        reach.astype(jnp.bfloat16),
        jnp.where(before, 1.0, 0.0).astype(jnp.bfloat16),
        (((1,), (0,)), ((), ())),
        preferred_element_type=jnp.float32,
    ).astype(jnp.int32)
    kept = (reach > 0.0) & (rank < cap_rows)
    rank = jnp.where(kept, rank, -1)
    rank_out[...] = rank
    for k in range(top_count):
        slot_out[k : k + 1, :] = (
            jnp.sum(jnp.where(matches[k] & kept, slot_ids + 1, 0), axis=0, keepdims=True) - 1
        )
    row_ids = lax.broadcasted_iota(jnp.int32, spread.shape[1:], 0)
    for s in range(slot_count):
        placed = jnp.where(row_ids == rank[s : s + 1, :], gate_of[s : s + 1, :], 0.0)
        spread[seat[0] ^ s] = placed.astype(jnp.bfloat16)


def place_routes(routes, picks, gates, replica_plan, seat, expert_count, cap_rows, held_rows):
    slot_count = replica_plan.shape[0]
    top_count, tokens = routes.shape
    vmem = pl.BlockSpec(memory_space=pltpu.VMEM)
    return pl.pallas_call(
        functools.partial(route_kernel, expert_count, cap_rows),
        out_shape=(
            jax.ShapeDtypeStruct((slot_count, held_rows, tokens), jnp.bfloat16),
            jax.ShapeDtypeStruct((slot_count, tokens), jnp.int32),
            jax.ShapeDtypeStruct((top_count, tokens), jnp.int32),
        ),
        in_specs=[pl.BlockSpec(memory_space=pltpu.SMEM)] * 2 + [vmem] * 4,
        out_specs=(vmem, vmem, vmem),
    )(seat, replica_plan, replica_plan.reshape(1, slot_count), routes, picks, gates)


def send_all_kernel(seat, spread, rows, *rest):
    out = rest[-1]
    held_rows, tokens = spread.shape[1:]
    total = jnp.dot(spread[...].reshape(-1, tokens), rows[...], preferred_element_type=jnp.float32)
    for d in range(spread.shape[0]):
        out[seat[0] ^ d] = total[d * held_rows : (d + 1) * held_rows].astype(jnp.bfloat16)


def all_rows_to_send(spread, out_grad, seat, span, after):
    slot_count, held_rows, tokens = spread.shape
    start, stop = span
    return pl.pallas_call(
        send_all_kernel,
        grid=((stop - start) // TILE,),
        in_specs=[
            pl.BlockSpec(memory_space=pltpu.SMEM),
            pl.BlockSpec((slot_count, held_rows, tokens), lambda j: (0, 0, 0)),
            pl.BlockSpec((tokens, TILE), lambda j: (0, start // TILE + j)),
        ]
        + [pl.BlockSpec(memory_space=pl.ANY)] * len(after),
        out_specs=pl.BlockSpec((slot_count, held_rows, TILE), lambda j: (0, 0, j)),
        out_shape=jax.ShapeDtypeStruct((slot_count, held_rows, stop - start), jnp.bfloat16),
        cost_estimate=cost(2 * slot_count * held_rows * tokens * (stop - start)),
    )(seat, spread, out_grad, *after)


def part_kernel(leave, rows, *rest):
    flat = rows[...].reshape(-1, rows.shape[-1])
    rest[-1][...] = jnp.dot(leave[...], flat, preferred_element_type=jnp.float32).astype(jnp.bfloat16)


def other_core_part(leave, rows, after):
    slot_count, held_rows, width = rows.shape
    units, held = leave.shape
    return pl.pallas_call(
        part_kernel,
        grid=(width // TILE,),
        in_specs=[
            pl.BlockSpec((units, held), lambda j: (0, 0)),
            pl.BlockSpec((slot_count, held_rows, TILE), lambda j: (0, 0, j)),
        ]
        + [pl.BlockSpec(memory_space=pl.ANY)] * len(after),
        out_specs=pl.BlockSpec((units, TILE), lambda j: (0, j)),
        out_shape=jax.ShapeDtypeStruct((units, width), jnp.bfloat16),
        cost_estimate=cost(2 * units * held * width),
    )(leave, rows, *after)


def near_kernel(chips, stay, rows, near, *rest):
    mine, *others = rest[-chips:]
    flat = rows[...].reshape(-1, rows.shape[-1])
    shard = mine.shape[0]
    total = jnp.dot(stay[...], flat, preferred_element_type=jnp.float32) + near[...].astype(jnp.float32)
    mine[...] = total[:shard]
    for d, other in enumerate(others):
        other[...] = total[(d + 1) * shard : (d + 2) * shard].astype(jnp.bfloat16)


def add_near(stay, rows, near, chips, after):
    units, held = stay.shape
    width = rows.shape[-1]
    shard = units // chips
    return pl.pallas_call(
        functools.partial(near_kernel, chips),
        grid=(width // TILE,),
        in_specs=[
            pl.BlockSpec((units, held), lambda j: (0, 0)),
            pl.BlockSpec(rows.shape[:2] + (TILE,), lambda j: (0, 0, j)),
            pl.BlockSpec((units, TILE), lambda j: (0, j)),
        ]
        + [pl.BlockSpec(memory_space=pl.ANY)] * len(after),
        out_specs=(pl.BlockSpec((shard, TILE), lambda j: (0, j)),) * chips,
        out_shape=(jax.ShapeDtypeStruct((shard, width), jnp.float32),)
        + (jax.ShapeDtypeStruct((shard, width), jnp.bfloat16),) * (chips - 1),
        cost_estimate=cost(2 * units * held * width),
    )(stay, rows, near, *after)


def hold_kernel(*refs):
    pass


def hold(array, after):
    return pl.pallas_call(
        hold_kernel,
        in_specs=[pl.BlockSpec(memory_space=pl.ANY)] * (1 + len(after)),
        out_specs=pl.BlockSpec(memory_space=pl.ANY),
        out_shape=jax.ShapeDtypeStruct(array.shape, array.dtype),
        input_output_aliases={0: 0},
        cost_estimate=cost(1),
    )(array, *after)


def return_kernel(score, rank, slot_of, gates, out):
    slot_count, cap_rows = score.shape
    tokens = slot_of.shape[1]
    row_ids = lax.broadcasted_iota(jnp.int32, (cap_rows, tokens), 0)

    def one_slot(s, total):
        onehot = jnp.where(row_ids == rank[pl.ds(s, 1), :], 1.0, 0.0)
        value = lax.dot_general(
            score[pl.ds(s, 1), :],
            onehot,
            (((1,), (0,)), ((), ())),
            precision=lax.Precision.HIGHEST,
            preferred_element_type=jnp.float32,
        )
        return jnp.where(slot_of[...] == s, value, total)

    total = lax.fori_loop(0, slot_count, one_slot, jnp.zeros(slot_of.shape, jnp.float32))
    held_gate = gates[...].astype(jnp.bfloat16).astype(jnp.float32)
    out[...] = jnp.where(slot_of[...] >= 0, total / held_gate, 0.0)


def last_kernel(leave, stay, rows, away, own):
    flat = rows[...].reshape(-1, rows.shape[-1])
    away[...] = jnp.dot(leave[...], flat, preferred_element_type=jnp.float32).astype(jnp.bfloat16)
    own[...] = jnp.dot(stay[...], flat, preferred_element_type=jnp.float32)


def last_parts(leave, stay, rows):
    shape = (leave.shape[0], rows.shape[-1])
    return pl.pallas_call(
        last_kernel,
        out_shape=(jax.ShapeDtypeStruct(shape, jnp.bfloat16), jax.ShapeDtypeStruct(shape, jnp.float32)),
        cost_estimate=cost(4 * leave.size * rows.shape[-1]),
    )(leave, stay, rows)


def score_kernel(sum_so_far, rows, weight, hidden, hidden_grad, score):
    held_rows = rows.shape[1]

    @pl.loop(0, rows.shape[0] // 2)
    def _(i):
        at = pl.ds(pl.multiple_of(2 * held_rows * i, 16), 2 * held_rows)
        two = rows[pl.ds(2 * i, 2)].reshape(2 * held_rows, -1)
        projected = sum_so_far[at, :] + lax.dot_general(
            two, weight[...], (((1,), (1,)), ((), ())), preferred_element_type=jnp.float32
        )
        hidden_grad[at, :] = projected.astype(jnp.bfloat16)
        total = jnp.sum(projected * hidden[at, :].astype(jnp.float32), axis=1, keepdims=True)
        score[at, :] = total


def project_last(sum_so_far, rows, weight, hidden):
    held, units = hidden.shape
    return pl.pallas_call(
        score_kernel,
        out_shape=(
            jax.ShapeDtypeStruct((held, units), jnp.bfloat16),
            jax.ShapeDtypeStruct((held, 1), jnp.float32),
        ),
        compiler_params=pltpu.CompilerParams(vmem_limit_bytes=48 * 1024 * 1024),
        cost_estimate=cost(2 * held * units * rows.shape[-1]),
    )(sum_so_far, rows, weight, hidden)


def add_kernel(copied, mine, other, *rest):
    term = jnp.where(copied[0] > 0, other[...].astype(jnp.float32), 0.0)
    rest[-1][...] = (mine[...].astype(jnp.float32) + term).astype(jnp.bfloat16)


def add_copy(copied, mine, other, start, width, into):
    rows, columns = mine.shape
    tile = pl.BlockSpec((rows, TILE), lambda j: (0, j))
    return pl.pallas_call(
        add_kernel,
        grid=(columns // TILE,),
        in_specs=[pl.BlockSpec(memory_space=pltpu.SMEM), tile, tile]
        + [pl.BlockSpec(memory_space=pl.ANY)] * len(into),
        out_specs=pl.BlockSpec((rows, TILE), lambda j: (0, start // TILE + j)),
        out_shape=jax.ShapeDtypeStruct((rows, width), jnp.bfloat16),
        input_output_aliases={3: 0} if into else {},
        cost_estimate=cost(rows * columns * 300),
    )(copied, mine, other, *into)


def most_on_a_link(pairs):
    count = {}
    for a, b in pairs:
        for (row, side), (to_row, to_side) in ((divmod(a, 2), divmod(b, 2)), (divmod(b, 2), divmod(a, 2))):
            step = 1 if to_row > row else -1
            links = [(at, side, step) for at in range(row, to_row, step)]
            if side != to_side:
                links.append((to_row, side))
            for link in links:
                count[link] = count.get(link, 0) + 1
    return max(count.values())


def sets_of_pairs(slots):
    if not slots:
        yield ()
        return
    yield from sets_of_pairs(slots[1:])
    for i in range(1, len(slots)):
        for others in sets_of_pairs(slots[1:i] + slots[i + 1 :]):
            yield ((slots[0], slots[i]),) + others


def swap_choices(slot_count):
    sets = [pairs for pairs in sets_of_pairs(tuple(range(slot_count))) if len(pairs) >= 2]
    load = {pairs: most_on_a_link(pairs) for pairs in sets}
    serves = {
        pairs: [two for two in itertools.combinations(pairs, 2) if load[pairs] <= load[two]] for pairs in sets
    }
    left = [pairs for pairs in sets if len(pairs) == 2]
    table = np.zeros((3 << slot_count,), np.int32)
    perms = []
    while left:
        missing = set(left)
        best = max(sets, key=lambda pairs: sum(two in missing for two in serves[pairs]))
        for two in serves[best]:
            (a, b), (c, d) = two
            between = (a < c < b) + (a < d < b)
            table[3 * sum(1 << slot for slot in (a, b, c, d)) + between] = len(perms)
        left = [two for two in left if two not in serves[best]]
        perms.append([(a, b) for a, b in best] + [(b, a) for a, b in best])
    return table, perms


def swap_choice(replica_plan, table):
    slot_ids, same_expert, ordinal = slot_layout(replica_plan)
    hot = jnp.sum(same_expert, axis=1) > 1
    mask = jnp.sum(jnp.where(hot, 1 << slot_ids, 0))
    least = jnp.min(jnp.where(hot, slot_ids, slot_ids.shape[0]))
    expert = jnp.sum(jnp.where(slot_ids == least, replica_plan, 0))
    partner = jnp.max(jnp.where(replica_plan == expert, slot_ids, 0))
    between = jnp.sum(hot & (slot_ids > least) & (slot_ids < partner))
    place = jnp.arange(table.shape[0])
    choice = jnp.sum(jnp.where(place == 3 * mask + between, jnp.asarray(table), 0))
    mine = hot & (slot_ids == lax.axis_index("expert"))
    return choice, jnp.sum(mine).astype(jnp.int32).reshape(1)


def sum_copies_any(group_sum, replica_plan):
    slot_ids, same_expert, ordinal = slot_layout(replica_plan)
    copies = jnp.sum(same_expert, axis=1)
    hot_first = (copies > 1) & (ordinal == 0)
    hot_rank = jnp.sum(hot_first[None, :] & (replica_plan[None, :] < replica_plan[:, None]), axis=1)
    my_slot = slot_ids == lax.axis_index("expert")
    my_rank = jnp.sum(jnp.where(my_slot, hot_rank, 0))
    my_hot = jnp.any(my_slot & (copies > 1))
    place_hot = (jnp.arange(HOT, dtype=jnp.int32) == my_rank) & my_hot
    group_f = group_sum.astype(jnp.float32)
    table = jnp.where(place_hot[:, None, None], group_f[None], 0.0)
    summed = lax.psum(table.astype(jnp.bfloat16), "expert").astype(jnp.float32)
    picked = jnp.sum(jnp.where(place_hot[:, None, None], summed, 0.0), axis=0)
    return jnp.where(my_hot, picked, group_f).astype(jnp.bfloat16)


def local(out_grad, gates, routes, copy_pick, replica_plan, down_weight, saved_hidden):
    slot_count = replica_plan.shape[0]
    cap_rows = saved_hidden.shape[3]
    expert_count = slot_count - slot_count // 4
    model_width = out_grad.shape[1]
    hidden_units = down_weight.shape[1]
    group_size = lax.axis_size("group")
    chips = group_size // 2
    shard_rows = hidden_units // group_size
    me = lax.axis_index("group")
    chip, core = me // 2, me % 2

    seat = lax.axis_index("expert").astype(jnp.int32).reshape(1)
    held_rows = -(-cap_rows // 16) * 16
    pad = ((0, 0), (0, held_rows - cap_rows), (0, 0))
    held_hidden = jnp.pad(saved_hidden[0, 0], pad).reshape(slot_count * held_rows, hidden_units)

    spread, rank, slot_of = place_routes(
        routes.T, copy_pick.T, gates.T, replica_plan, seat, expert_count, cap_rows, held_rows
    )

    by_owner = held_hidden.T.reshape(chips, 2, shard_rows, -1)
    by_owner = jnp.stack([by_owner[chip ^ d] for d in range(chips)])
    stay = by_owner[:, core].reshape(hidden_units // 2, -1)
    leave = by_owner[:, 1 - core].reshape(hidden_units // 2, -1)

    edges = np.cumsum((0,) + CHUNKS)
    spans = [(int(a), int(b)) for a, b in zip(edges[:-1], edges[1:])]
    ready = [all_rows_to_send(spread, out_grad, seat, span, []) for span in spans]
    pairs = slot_count - expert_count == HOT
    if pairs:
        table, perms = swap_choices(slot_count)
        pairing, copied = swap_choice(replica_plan, table)
    else:
        copied = jnp.zeros((1,), jnp.int32)
    def to_core(away):
        return lax.ppermute(away, "group", [(i, i ^ 1) for i in range(group_size)])

    def to_chips(others):
        return [
            lax.ppermute(other, "group", [(i, i ^ (2 * d + 2)) for i in range(group_size)])
            for d, other in enumerate(others)
        ]

    def sum_chips(mine, far):
        return sum((f.astype(jnp.float32) for f in far), mine).astype(jnp.bfloat16)

    def project(rows, span):
        return lax.dot_general(
            rows.reshape(slot_count * held_rows, -1),
            down_weight[0, :, span[0] : span[1]],
            (((1,), (1,)), ((), ())),
            preferred_element_type=jnp.float32,
        )

    def travel(sent):
        return lax.all_to_all(sent, "expert", split_axis=0, concat_axis=0, tiled=True)

    rows = travel(ready[0])
    rows_1 = travel(hold(ready[1], [rows, ready[2]] + ([pairing.reshape(1)] if pairs else [])))
    projected = project(rows, spans[0])
    mine, *others = add_near(stay, rows, to_core(other_core_part(leave, rows, [])), chips, [])
    far = to_chips(others)
    rows_2 = travel(hold(ready[2], [rows_1, others[0], projected]))
    projected = projected + project(rows_1, spans[1])
    away = other_core_part(leave, rows_1, others[:1])
    mine_1, *others_1 = add_near(stay, rows_1, to_core(away), chips, far[:1])
    away_2, own_2 = last_parts(leave, stay, hold(rows_2, others_1[:1]))
    sum_0 = sum_chips(mine, far)
    last_weight = down_weight[0, :, spans[2][0] : spans[2][1]]

    def finish(swap, sum_0, mine_1, others_1, rows_2, away_2, own_2, projected, *rest):
        held_hidden, rank, slot_of, gates, weight, copied = rest
        got_0 = swap(sum_0)
        far_1 = to_chips(others_1)
        total_2 = (own_2 + to_core(away_2).astype(jnp.float32)).reshape(chips, shard_rows, -1)
        far_2 = to_chips([other.astype(jnp.bfloat16) for other in total_2[1:]])
        hidden_grad, route_score = project_last(projected, rows_2, weight, held_hidden)
        returned = travel(route_score.reshape(slot_count, held_rows))
        route_grad = pl.pallas_call(
            return_kernel, out_shape=jax.ShapeDtypeStruct(gates.shape, jnp.float32)
        )(returned, rank, slot_of, gates)
        sum_12 = jnp.concatenate([sum_chips(mine_1, far_1), sum_chips(total_2[0], far_2)], axis=1)
        got_12 = swap(hold(sum_12, [got_0]))
        copy_grad = add_copy(copied, sum_0, got_0, 0, model_width, [])
        copy_grad = add_copy(copied, sum_12, got_12, spans[1][0], model_width, [copy_grad])
        return route_grad, hidden_grad, copy_grad

    state = (sum_0, mine_1, others_1, rows_2, away_2, own_2, projected)
    state = state + (held_hidden, rank, slot_of, gates.T, last_weight, copied)
    if pairs:
        swaps = [functools.partial(lax.ppermute, axis_name="expert", perm=perm) for perm in perms]
        route_grad, hidden_grad, copy_grad = lax.switch(
            pairing, [functools.partial(finish, swap) for swap in swaps], *state
        )
    else:
        route_grad, hidden_grad, copy_grad = finish(jnp.zeros_like, *state)
    if not pairs:
        copy_grad = sum_copies_any(copy_grad, replica_plan)
    hidden_grad = hidden_grad.reshape(slot_count, held_rows, hidden_units)[:, :cap_rows]
    return (route_grad.T, hidden_grad[None, None], copy_grad.reshape(1, shard_rows, model_width))


def solution(mesh):
    placed = (
        P(("group", "expert"), None),
        P(("group", "expert"), None),
        P(("group", "expert"), None),
        P(("group", "expert"), None),
        P(),
        P("expert", None, None),
        P("group", "expert", None, None, None),
    )
    return jax.shard_map(
        local,
        mesh=mesh,
        in_specs=placed,
        out_specs=(
            P(("group", "expert"), None),
            P("group", "expert", None, None, None),
            P("expert", "group", None),
        ),
        check_vma=False,
    )
```

```python
import functools
import itertools

import jax
import jax.numpy as jnp
import numpy as np
from jax import lax
from jax.experimental import pallas as pl
from jax.experimental.pallas import tpu as pltpu
from jax.sharding import PartitionSpec as P

HOT = 2
TILE = 512


def cost(flops):
    return pl.CostEstimate(flops=flops, bytes_accessed=flops // 300, transcendentals=0)
CHUNKS = (2048, 1024, 512)


def slot_layout(replica_plan):
    slot_count = replica_plan.shape[0]
    slot_ids = jnp.arange(slot_count, dtype=jnp.int32)
    same_expert = replica_plan[:, None] == replica_plan[None, :]
    earlier_slot = slot_ids[None, :] < slot_ids[:, None]
    ordinal = jnp.sum(same_expert & earlier_slot, axis=1)
    return (slot_ids, same_expert, ordinal)


def route_kernel(
    expert_count, cap_rows, seat, slot_plan, plan_row, routes, picks, gates, spread, rank_out, slot_out
):
    slot_count = plan_row.shape[1]
    top_count, tokens = routes.shape
    column = lax.broadcasted_iota(jnp.int32, (slot_count, 1), 0)
    plan = jnp.zeros((slot_count, 1), jnp.int32)
    for s in range(slot_count):
        plan = jnp.where(column == s, slot_plan[s], plan)
    same = plan == plan_row[...]
    slot_r = lax.broadcasted_iota(jnp.int32, (slot_count, slot_count), 0)
    slot_c = lax.broadcasted_iota(jnp.int32, (slot_count, slot_count), 1)
    copies = jnp.sum(jnp.where(same, 1.0, 0.0), axis=1, keepdims=True)
    ordinal = jnp.sum(jnp.where(same & (slot_c < slot_r), 1.0, 0.0), axis=1, keepdims=True)
    slot_ids = lax.broadcasted_iota(jnp.int32, (slot_count, tokens), 0)
    reach = jnp.zeros((slot_count, tokens), jnp.float32)
    gate_of = jnp.zeros((slot_count, tokens), jnp.float32)
    matches = []
    for k in range(top_count):
        route = routes[k : k + 1, :]
        pick = picks[k : k + 1, :].astype(jnp.float32)
        chosen = pick - copies * jnp.floor((pick + 0.5) / copies)
        match = (route == plan) & (chosen == ordinal) & (route < expert_count)
        matches.append(match)
        reach = jnp.where(match, 1.0, reach)
        gate_of = jnp.where(match, gates[k : k + 1, :], gate_of)
    before = lax.broadcasted_iota(jnp.int32, (tokens, tokens), 0) < lax.broadcasted_iota(
        jnp.int32, (tokens, tokens), 1
    )
    rank = lax.dot_general(
        reach.astype(jnp.bfloat16),
        jnp.where(before, 1.0, 0.0).astype(jnp.bfloat16),
        (((1,), (0,)), ((), ())),
        preferred_element_type=jnp.float32,
    ).astype(jnp.int32)
    kept = (reach > 0.0) & (rank < cap_rows)
    rank = jnp.where(kept, rank, -1)
    rank_out[...] = rank
    for k in range(top_count):
        slot_out[k : k + 1, :] = (
            jnp.sum(jnp.where(matches[k] & kept, slot_ids + 1, 0), axis=0, keepdims=True) - 1
        )
    row_ids = lax.broadcasted_iota(jnp.int32, spread.shape[1:], 0)
    for s in range(slot_count):
        placed = jnp.where(row_ids == rank[s : s + 1, :], gate_of[s : s + 1, :], 0.0)
        spread[seat[0] ^ s] = placed.astype(jnp.bfloat16)


def place_routes(routes, picks, gates, replica_plan, seat, expert_count, cap_rows, held_rows):
    slot_count = replica_plan.shape[0]
    top_count, tokens = routes.shape
    vmem = pl.BlockSpec(memory_space=pltpu.VMEM)
    return pl.pallas_call(
        functools.partial(route_kernel, expert_count, cap_rows),
        out_shape=(
            jax.ShapeDtypeStruct((slot_count, held_rows, tokens), jnp.bfloat16),
            jax.ShapeDtypeStruct((slot_count, tokens), jnp.int32),
            jax.ShapeDtypeStruct((top_count, tokens), jnp.int32),
        ),
        in_specs=[pl.BlockSpec(memory_space=pltpu.SMEM)] * 2 + [vmem] * 4,
        out_specs=(vmem, vmem, vmem),
    )(seat, replica_plan, replica_plan.reshape(1, slot_count), routes, picks, gates)


def send_all_kernel(start, seat, spread, rows, out):
    slot_count, held_rows, tokens = spread.shape
    places = spread[...].reshape(-1, tokens)

    @pl.loop(0, out.shape[-1] // TILE)
    def _(j):
        at = pl.multiple_of(j * TILE, TILE)
        total = jnp.dot(places, rows[:, pl.ds(start + at, TILE)], preferred_element_type=jnp.float32)
        for d in range(slot_count):
            part = total[d * held_rows : (d + 1) * held_rows].astype(jnp.bfloat16)
            out[seat[0] ^ d, :, pl.ds(at, TILE)] = part


def all_rows_to_send(spread, out_grad, seat, span):
    slot_count, held_rows, tokens = spread.shape
    start, stop = span
    vmem = pl.BlockSpec(memory_space=pltpu.VMEM)
    return pl.pallas_call(
        functools.partial(send_all_kernel, start),
        in_specs=[pl.BlockSpec(memory_space=pltpu.SMEM), vmem, vmem],
        out_specs=vmem,
        out_shape=jax.ShapeDtypeStruct((slot_count, held_rows, stop - start), jnp.bfloat16),
        cost_estimate=cost(2 * slot_count * held_rows * tokens * (stop - start)),
    )(seat, spread, out_grad)


def part_kernel(leave, rows, *rest):
    flat = rows[...].reshape(-1, rows.shape[-1])
    rest[-1][...] = jnp.dot(leave[...], flat, preferred_element_type=jnp.float32).astype(jnp.bfloat16)


def other_core_part(leave, rows, after):
    slot_count, held_rows, width = rows.shape
    units, held = leave.shape
    return pl.pallas_call(
        part_kernel,
        grid=(width // TILE,),
        in_specs=[
            pl.BlockSpec((units, held), lambda j: (0, 0)),
            pl.BlockSpec((slot_count, held_rows, TILE), lambda j: (0, 0, j)),
        ]
        + [pl.BlockSpec(memory_space=pl.ANY)] * len(after),
        out_specs=pl.BlockSpec((units, TILE), lambda j: (0, j)),
        out_shape=jax.ShapeDtypeStruct((units, width), jnp.bfloat16),
        cost_estimate=cost(2 * units * held * width),
    )(leave, rows, *after)


def near_kernel(chips, stay, rows, near, *rest):
    mine, *others = rest[-chips:]
    flat = rows[...].reshape(-1, rows.shape[-1])
    shard = mine.shape[0]
    total = jnp.dot(stay[...], flat, preferred_element_type=jnp.float32) + near[...].astype(jnp.float32)
    mine[...] = total[:shard]
    for d, other in enumerate(others):
        other[...] = total[(d + 1) * shard : (d + 2) * shard].astype(jnp.bfloat16)


def add_near(stay, rows, near, chips, after):
    units, held = stay.shape
    width = rows.shape[-1]
    shard = units // chips
    return pl.pallas_call(
        functools.partial(near_kernel, chips),
        grid=(width // TILE,),
        in_specs=[
            pl.BlockSpec((units, held), lambda j: (0, 0)),
            pl.BlockSpec(rows.shape[:2] + (TILE,), lambda j: (0, 0, j)),
            pl.BlockSpec((units, TILE), lambda j: (0, j)),
        ]
        + [pl.BlockSpec(memory_space=pl.ANY)] * len(after),
        out_specs=(pl.BlockSpec((shard, TILE), lambda j: (0, j)),) * chips,
        out_shape=(jax.ShapeDtypeStruct((shard, width), jnp.float32),)
        + (jax.ShapeDtypeStruct((shard, width), jnp.bfloat16),) * (chips - 1),
        cost_estimate=cost(2 * units * held * width),
    )(stay, rows, near, *after)


def hold_kernel(*refs):
    pass


def hold(array, after):
    return pl.pallas_call(
        hold_kernel,
        in_specs=[pl.BlockSpec(memory_space=pl.ANY)] * (1 + len(after)),
        out_specs=pl.BlockSpec(memory_space=pl.ANY),
        out_shape=jax.ShapeDtypeStruct(array.shape, array.dtype),
        input_output_aliases={0: 0},
        cost_estimate=cost(1),
    )(array, *after)


def return_kernel(score, rank, slot_of, gates, out):
    slot_count, cap_rows = score.shape
    top_count, tokens = slot_of.shape
    row_ids = lax.broadcasted_iota(jnp.int32, (cap_rows, tokens), 0)
    total = jnp.zeros((top_count, tokens), jnp.float32)
    for s in range(slot_count):
        onehot = jnp.where(row_ids == rank[s : s + 1, :], 1.0, 0.0)
        value = lax.dot_general(
            score[s : s + 1, :],
            onehot,
            (((1,), (0,)), ((), ())),
            precision=lax.Precision.HIGHEST,
            preferred_element_type=jnp.float32,
        )
        total = jnp.where(slot_of[...] == s, value, total)
    held_gate = gates[...].astype(jnp.bfloat16).astype(jnp.float32)
    out[...] = jnp.where(slot_of[...] >= 0, total / held_gate, 0.0)


def matchings(slot_count):
    first = np.zeros((1 << slot_count,), np.int32)
    perms = []
    for four in itertools.combinations(range(slot_count), 4):
        first[sum(1 << s for s in four)] = len(perms)
        for other in range(3):
            rest = [four[1 + i] for i in range(3) if i != other]
            pairs = ((four[0], four[1 + other]), tuple(rest))
            swaps = {a: b for pair in pairs for a, b in (pair, pair[::-1])}
            perms.append([(slot, swaps.get(slot, slot)) for slot in range(slot_count)])
    return first, perms


def matching_index(replica_plan, first):
    slot_ids, same_expert, ordinal = slot_layout(replica_plan)
    hot = jnp.sum(same_expert, axis=1) > 1
    mask = jnp.sum(jnp.where(hot, 1 << slot_ids, 0))
    least = jnp.min(jnp.where(hot, slot_ids, slot_ids.shape[0]))
    expert = jnp.sum(jnp.where(slot_ids == least, replica_plan, 0))
    partner = jnp.max(jnp.where(replica_plan == expert, slot_ids, 0))
    between = jnp.sum(hot & (slot_ids > least) & (slot_ids < partner))
    base = jnp.sum(jnp.where(jnp.arange(first.shape[0]) == mask, jnp.asarray(first), 0))
    return base + between, jnp.any(hot & (slot_ids == lax.axis_index("expert")))


def sum_copies_any(group_sum, replica_plan):
    slot_ids, same_expert, ordinal = slot_layout(replica_plan)
    copies = jnp.sum(same_expert, axis=1)
    hot_first = (copies > 1) & (ordinal == 0)
    hot_rank = jnp.sum(hot_first[None, :] & (replica_plan[None, :] < replica_plan[:, None]), axis=1)
    my_slot = slot_ids == lax.axis_index("expert")
    my_rank = jnp.sum(jnp.where(my_slot, hot_rank, 0))
    my_hot = jnp.any(my_slot & (copies > 1))
    place_hot = (jnp.arange(HOT, dtype=jnp.int32) == my_rank) & my_hot
    group_f = group_sum.astype(jnp.float32)
    table = jnp.where(place_hot[:, None, None], group_f[None], 0.0)
    summed = lax.psum(table.astype(jnp.bfloat16), "expert").astype(jnp.float32)
    picked = jnp.sum(jnp.where(place_hot[:, None, None], summed, 0.0), axis=0)
    return jnp.where(my_hot, picked, group_f).astype(jnp.bfloat16)


def local(out_grad, gates, routes, copy_pick, replica_plan, down_weight, saved_hidden):
    slot_count = replica_plan.shape[0]
    cap_rows = saved_hidden.shape[3]
    expert_count = slot_count - slot_count // 4
    model_width = out_grad.shape[1]
    hidden_units = down_weight.shape[1]
    group_size = lax.axis_size("group")
    chips = group_size // 2
    shard_rows = hidden_units // group_size
    me = lax.axis_index("group")
    chip, core = me // 2, me % 2

    seat = lax.axis_index("expert").astype(jnp.int32).reshape(1)
    held_rows = -(-cap_rows // 16) * 16
    pad = ((0, 0), (0, held_rows - cap_rows), (0, 0))
    held_hidden = jnp.pad(saved_hidden[0, 0], pad).reshape(slot_count * held_rows, hidden_units)

    spread, rank, slot_of = place_routes(
        routes.T, copy_pick.T, gates.T, replica_plan, seat, expert_count, cap_rows, held_rows
    )

    by_owner = held_hidden.T.reshape(chips, 2, shard_rows, -1)
    by_owner = jnp.stack([by_owner[chip ^ d] for d in range(chips)])
    stay = by_owner[:, core].reshape(hidden_units // 2, -1)
    leave = by_owner[:, 1 - core].reshape(hidden_units // 2, -1)

    edges = np.cumsum((0,) + CHUNKS)
    spans = [(int(a), int(b)) for a, b in zip(edges[:-1], edges[1:])]
    ready = [all_rows_to_send(spread, out_grad, seat, span) for span in spans]
    pairs = slot_count - expert_count == HOT
    if pairs:
        first, perms = matchings(slot_count)
        pairing, copied = matching_index(replica_plan, first)

    def swapped(sums):
        if not pairs:
            return jnp.zeros_like(sums)
        return lax.switch(
            pairing,
            [functools.partial(lax.ppermute, axis_name="expert", perm=perm) for perm in perms],
            sums,
        )

    def add_copy(sums, got):
        if not pairs:
            return sums
        other = jnp.where(copied, got.astype(jnp.float32), 0.0)
        return (sums.astype(jnp.float32) + other).astype(jnp.bfloat16)

    def to_core(away):
        return lax.ppermute(away, "group", [(i, i ^ 1) for i in range(group_size)])

    def to_chips(others):
        return [
            lax.ppermute(other, "group", [(i, i ^ (2 * d + 2)) for i in range(group_size)])
            for d, other in enumerate(others)
        ]

    def sum_chips(mine, far):
        return sum((f.astype(jnp.float32) for f in far), mine).astype(jnp.bfloat16)

    def project(rows, span):
        return lax.dot_general(
            rows.reshape(slot_count * held_rows, -1),
            down_weight[0, :, span[0] : span[1]],
            (((1,), (1,)), ((), ())),
            preferred_element_type=jnp.float32,
        )

    def travel(sent):
        return lax.all_to_all(sent, "expert", split_axis=0, concat_axis=0, tiled=True)

    rows = travel(ready[0])
    rows_1 = travel(hold(ready[1], [rows, ready[2]] + ([pairing.reshape(1)] if pairs else [])))
    projected = project(rows, spans[0])
    mine, *others = add_near(stay, rows, to_core(other_core_part(leave, rows, [])), chips, [])
    far = to_chips(others)
    rows_2 = travel(hold(ready[2], [rows_1, others[0], projected]))
    projected = projected + project(rows_1, spans[1])
    away = other_core_part(leave, rows_1, others[:1])
    mine_1, *others_1 = add_near(stay, rows_1, to_core(away), chips, far[:1])
    far_1 = to_chips(others_1)
    away_2 = other_core_part(leave, rows_2, others_1[:1])
    sum_0 = hold(sum_chips(mine, far), [away_2])
    got_0 = swapped(sum_0)
    mine_2, *others_2 = add_near(stay, rows_2, to_core(away_2), chips, far_1[:1] + [got_0])
    far_2 = to_chips(others_2)

    projected = hold(projected, [got_0]) + project(rows_2, spans[2])
    route_score = jnp.sum(projected * held_hidden.astype(jnp.float32), axis=1)
    returned = travel(hold(route_score.reshape(slot_count, held_rows), others_2[:1]))
    route_grad = pl.pallas_call(
        return_kernel, out_shape=jax.ShapeDtypeStruct(gates.T.shape, jnp.float32)
    )(returned, rank, slot_of, gates.T).T
    hidden_grad = projected.astype(jnp.bfloat16).reshape(slot_count, held_rows, hidden_units)[:, :cap_rows]

    sum_12 = jnp.concatenate([sum_chips(mine_1, far_1), sum_chips(mine_2, far_2)], axis=1)
    got_12 = swapped(sum_12)
    copy_grad = jnp.concatenate([add_copy(sum_0, got_0), add_copy(sum_12, got_12)], axis=1)
    if not pairs:
        copy_grad = sum_copies_any(copy_grad, replica_plan)
    return (route_grad, hidden_grad[None, None], copy_grad.reshape(1, shard_rows, model_width))


def solution(mesh):
    placed = (
        P(("group", "expert"), None),
        P(("group", "expert"), None),
        P(("group", "expert"), None),
        P(("group", "expert"), None),
        P(),
        P("expert", None, None),
        P("group", "expert", None, None, None),
    )
    return jax.shard_map(
        local,
        mesh=mesh,
        in_specs=placed,
        out_specs=(
            P(("group", "expert"), None),
            P("group", "expert", None, None, None),
            P("expert", "group", None),
        ),
        check_vma=False,
    )
```

```python
import functools
import itertools

import jax
import jax.numpy as jnp
import numpy as np
from jax import lax
from jax.experimental import pallas as pl
from jax.experimental.pallas import tpu as pltpu
from jax.sharding import PartitionSpec as P

HOT = 2


def tile_of(width):
    return 512 if width % 512 == 0 else width


def cost(flops):
    return pl.CostEstimate(flops=flops, bytes_accessed=flops // 300, transcendentals=0)
CHUNKS = (2048, 896, 640)


def slot_layout(replica_plan):
    slot_count = replica_plan.shape[0]
    slot_ids = jnp.arange(slot_count, dtype=jnp.int32)
    same_expert = replica_plan[:, None] == replica_plan[None, :]
    earlier_slot = slot_ids[None, :] < slot_ids[:, None]
    ordinal = jnp.sum(same_expert & earlier_slot, axis=1)
    return (slot_ids, same_expert, ordinal)


def route_kernel(
    expert_count, cap_rows, seat, slot_plan, plan_row, routes, picks, gates, spread, rank_out, slot_out
):
    slot_count = plan_row.shape[1]
    top_count, tokens = routes.shape
    column = lax.broadcasted_iota(jnp.int32, (slot_count, 1), 0)
    plan = jnp.zeros((slot_count, 1), jnp.int32)
    for s in range(slot_count):
        plan = jnp.where(column == s, slot_plan[s], plan)
    same = plan == plan_row[...]
    slot_r = lax.broadcasted_iota(jnp.int32, (slot_count, slot_count), 0)
    slot_c = lax.broadcasted_iota(jnp.int32, (slot_count, slot_count), 1)
    copies = jnp.sum(jnp.where(same, 1.0, 0.0), axis=1, keepdims=True)
    ordinal = jnp.sum(jnp.where(same & (slot_c < slot_r), 1.0, 0.0), axis=1, keepdims=True)
    slot_ids = lax.broadcasted_iota(jnp.int32, (slot_count, tokens), 0)
    reach = jnp.zeros((slot_count, tokens), jnp.float32)
    gate_of = jnp.zeros((slot_count, tokens), jnp.float32)
    matches = []
    for k in range(top_count):
        route = routes[k : k + 1, :]
        pick = picks[k : k + 1, :].astype(jnp.float32)
        chosen = pick - copies * jnp.floor((pick + 0.5) / copies)
        match = (route == plan) & (chosen == ordinal) & (route < expert_count)
        matches.append(match)
        reach = jnp.where(match, 1.0, reach)
        gate_of = jnp.where(match, gates[k : k + 1, :], gate_of)
    before = lax.broadcasted_iota(jnp.int32, (tokens, tokens), 0) < lax.broadcasted_iota(
        jnp.int32, (tokens, tokens), 1
    )
    rank = lax.dot_general(
        reach.astype(jnp.bfloat16),
        jnp.where(before, 1.0, 0.0).astype(jnp.bfloat16),
        (((1,), (0,)), ((), ())),
        preferred_element_type=jnp.float32,
    ).astype(jnp.int32)
    kept = (reach > 0.0) & (rank < cap_rows)
    rank = jnp.where(kept, rank, -1)
    rank_out[...] = rank
    for k in range(top_count):
        slot_out[k : k + 1, :] = (
            jnp.sum(jnp.where(matches[k] & kept, slot_ids + 1, 0), axis=0, keepdims=True) - 1
        )
    row_ids = lax.broadcasted_iota(jnp.int32, spread.shape[1:], 0)
    for s in range(slot_count):
        placed = jnp.where(row_ids == rank[s : s + 1, :], gate_of[s : s + 1, :], 0.0)
        spread[seat[0] ^ s] = placed.astype(jnp.bfloat16)


def place_routes(routes, picks, gates, replica_plan, seat, expert_count, cap_rows, held_rows):
    slot_count = replica_plan.shape[0]
    top_count, tokens = routes.shape
    vmem = pl.BlockSpec(memory_space=pltpu.VMEM)
    return pl.pallas_call(
        functools.partial(route_kernel, expert_count, cap_rows),
        out_shape=(
            jax.ShapeDtypeStruct((slot_count, held_rows, tokens), jnp.bfloat16),
            jax.ShapeDtypeStruct((slot_count, tokens), jnp.int32),
            jax.ShapeDtypeStruct((top_count, tokens), jnp.int32),
        ),
        in_specs=[pl.BlockSpec(memory_space=pltpu.SMEM)] * 2 + [vmem] * 4,
        out_specs=(vmem, vmem, vmem),
    )(seat, replica_plan, replica_plan.reshape(1, slot_count), routes, picks, gates)


def send_all_kernel(start, seat, spread, rows, out):
    slot_count, held_rows, tokens = spread.shape
    places = spread[...].reshape(-1, tokens)

    width = tile_of(out.shape[-1])

    @pl.loop(0, out.shape[-1] // width)
    def _(j):
        at = pl.multiple_of(j * width, width)
        total = jnp.dot(places, rows[:, pl.ds(start + at, width)], preferred_element_type=jnp.float32)
        for d in range(slot_count):
            part = total[d * held_rows : (d + 1) * held_rows].astype(jnp.bfloat16)
            out[seat[0] ^ d, :, pl.ds(at, width)] = part


def all_rows_to_send(spread, out_grad, seat, span):
    slot_count, held_rows, tokens = spread.shape
    start, stop = span
    vmem = pl.BlockSpec(memory_space=pltpu.VMEM)
    return pl.pallas_call(
        functools.partial(send_all_kernel, start),
        in_specs=[pl.BlockSpec(memory_space=pltpu.SMEM), vmem, vmem],
        out_specs=vmem,
        out_shape=jax.ShapeDtypeStruct((slot_count, held_rows, stop - start), jnp.bfloat16),
        cost_estimate=cost(2 * slot_count * held_rows * tokens * (stop - start)),
    )(seat, spread, out_grad)


def part_kernel(leave, rows, *rest):
    flat = rows[...].reshape(-1, rows.shape[-1])
    rest[-1][...] = jnp.dot(leave[...], flat, preferred_element_type=jnp.float32).astype(jnp.bfloat16)


def other_core_part(leave, rows, after):
    slot_count, held_rows, width = rows.shape
    units, held = leave.shape
    tile = tile_of(width)
    return pl.pallas_call(
        part_kernel,
        grid=(width // tile,),
        in_specs=[
            pl.BlockSpec((units, held), lambda j: (0, 0)),
            pl.BlockSpec((slot_count, held_rows, tile), lambda j: (0, 0, j)),
        ]
        + [pl.BlockSpec(memory_space=pl.ANY)] * len(after),
        out_specs=pl.BlockSpec((units, tile), lambda j: (0, j)),
        out_shape=jax.ShapeDtypeStruct((units, width), jnp.bfloat16),
        cost_estimate=cost(2 * units * held * width),
    )(leave, rows, *after)


def near_kernel(chips, stay, rows, near, *rest):
    mine, *others = rest[-chips:]
    flat = rows[...].reshape(-1, rows.shape[-1])
    shard = mine.shape[0]
    total = jnp.dot(stay[...], flat, preferred_element_type=jnp.float32) + near[...].astype(jnp.float32)
    mine[...] = total[:shard]
    for d, other in enumerate(others):
        other[...] = total[(d + 1) * shard : (d + 2) * shard].astype(jnp.bfloat16)


def add_near(stay, rows, near, chips, after):
    units, held = stay.shape
    width = rows.shape[-1]
    shard = units // chips
    tile = tile_of(width)
    return pl.pallas_call(
        functools.partial(near_kernel, chips),
        grid=(width // tile,),
        in_specs=[
            pl.BlockSpec((units, held), lambda j: (0, 0)),
            pl.BlockSpec(rows.shape[:2] + (tile,), lambda j: (0, 0, j)),
            pl.BlockSpec((units, tile), lambda j: (0, j)),
        ]
        + [pl.BlockSpec(memory_space=pl.ANY)] * len(after),
        out_specs=(pl.BlockSpec((shard, tile), lambda j: (0, j)),) * chips,
        out_shape=(jax.ShapeDtypeStruct((shard, width), jnp.float32),)
        + (jax.ShapeDtypeStruct((shard, width), jnp.bfloat16),) * (chips - 1),
        cost_estimate=cost(2 * units * held * width),
    )(stay, rows, near, *after)


def hold_kernel(*refs):
    pass


def hold(array, after):
    return pl.pallas_call(
        hold_kernel,
        in_specs=[pl.BlockSpec(memory_space=pl.ANY)] * (1 + len(after)),
        out_specs=pl.BlockSpec(memory_space=pl.ANY),
        out_shape=jax.ShapeDtypeStruct(array.shape, array.dtype),
        input_output_aliases={0: 0},
        cost_estimate=cost(1),
    )(array, *after)


def return_kernel(score, rank, slot_of, gates, out):
    slot_count, cap_rows = score.shape
    top_count, tokens = slot_of.shape
    row_ids = lax.broadcasted_iota(jnp.int32, (cap_rows, tokens), 0)
    total = jnp.zeros((top_count, tokens), jnp.float32)
    for s in range(slot_count):
        onehot = jnp.where(row_ids == rank[s : s + 1, :], 1.0, 0.0)
        value = lax.dot_general(
            score[s : s + 1, :],
            onehot,
            (((1,), (0,)), ((), ())),
            precision=lax.Precision.HIGHEST,
            preferred_element_type=jnp.float32,
        )
        total = jnp.where(slot_of[...] == s, value, total)
    held_gate = gates[...].astype(jnp.bfloat16).astype(jnp.float32)
    out[...] = jnp.where(slot_of[...] >= 0, total / held_gate, 0.0)


def matchings(slot_count):
    first = np.zeros((1 << slot_count,), np.int32)
    perms = []
    for four in itertools.combinations(range(slot_count), 4):
        first[sum(1 << s for s in four)] = len(perms)
        for other in range(3):
            rest = [four[1 + i] for i in range(3) if i != other]
            pairs = ((four[0], four[1 + other]), tuple(rest))
            perms.append([(a, b) for a, b in pairs] + [(b, a) for a, b in pairs])
    return first, perms


def matching_index(replica_plan, first):
    slot_ids, same_expert, ordinal = slot_layout(replica_plan)
    hot = jnp.sum(same_expert, axis=1) > 1
    mask = jnp.sum(jnp.where(hot, 1 << slot_ids, 0))
    least = jnp.min(jnp.where(hot, slot_ids, slot_ids.shape[0]))
    expert = jnp.sum(jnp.where(slot_ids == least, replica_plan, 0))
    partner = jnp.max(jnp.where(replica_plan == expert, slot_ids, 0))
    between = jnp.sum(hot & (slot_ids > least) & (slot_ids < partner))
    base = jnp.sum(jnp.where(jnp.arange(first.shape[0]) == mask, jnp.asarray(first), 0))
    return base + between


def sum_copies_any(group_sum, replica_plan):
    slot_ids, same_expert, ordinal = slot_layout(replica_plan)
    copies = jnp.sum(same_expert, axis=1)
    hot_first = (copies > 1) & (ordinal == 0)
    hot_rank = jnp.sum(hot_first[None, :] & (replica_plan[None, :] < replica_plan[:, None]), axis=1)
    my_slot = slot_ids == lax.axis_index("expert")
    my_rank = jnp.sum(jnp.where(my_slot, hot_rank, 0))
    my_hot = jnp.any(my_slot & (copies > 1))
    place_hot = (jnp.arange(HOT, dtype=jnp.int32) == my_rank) & my_hot
    group_f = group_sum.astype(jnp.float32)
    table = jnp.where(place_hot[:, None, None], group_f[None], 0.0)
    summed = lax.psum(table.astype(jnp.bfloat16), "expert").astype(jnp.float32)
    picked = jnp.sum(jnp.where(place_hot[:, None, None], summed, 0.0), axis=0)
    return jnp.where(my_hot, picked, group_f).astype(jnp.bfloat16)


def local(out_grad, gates, routes, copy_pick, replica_plan, down_weight, saved_hidden):
    slot_count = replica_plan.shape[0]
    cap_rows = saved_hidden.shape[3]
    expert_count = slot_count - slot_count // 4
    model_width = out_grad.shape[1]
    hidden_units = down_weight.shape[1]
    group_size = lax.axis_size("group")
    chips = group_size // 2
    shard_rows = hidden_units // group_size
    me = lax.axis_index("group")
    chip, core = me // 2, me % 2

    seat = lax.axis_index("expert").astype(jnp.int32).reshape(1)
    held_rows = -(-cap_rows // 16) * 16
    pad = ((0, 0), (0, held_rows - cap_rows), (0, 0))
    held_hidden = jnp.pad(saved_hidden[0, 0], pad).reshape(slot_count * held_rows, hidden_units)

    spread, rank, slot_of = place_routes(
        routes.T, copy_pick.T, gates.T, replica_plan, seat, expert_count, cap_rows, held_rows
    )

    by_owner = held_hidden.T.reshape(chips, 2, shard_rows, -1)
    by_owner = jnp.stack([by_owner[chip ^ d] for d in range(chips)])
    stay = by_owner[:, core].reshape(hidden_units // 2, -1)
    leave = by_owner[:, 1 - core].reshape(hidden_units // 2, -1)

    edges = np.cumsum((0,) + CHUNKS)
    spans = [(int(a), int(b)) for a, b in zip(edges[:-1], edges[1:])]
    ready = [all_rows_to_send(spread, out_grad, seat, span) for span in spans]
    pairs = slot_count - expert_count == HOT
    if pairs:
        first, perms = matchings(slot_count)
        pairing = matching_index(replica_plan, first)
    group_sum, projected = [], jnp.zeros((slot_count * held_rows, hidden_units), jnp.float32)
    far, others = [], []
    early = ready[2:] + ([pairing.reshape(1)] if pairs else [])
    sent = ready[0]
    for at, span in enumerate(spans):
        rows = lax.all_to_all(sent, "expert", split_axis=0, concat_axis=0, tiled=True)
        after = others[:1] + ([projected] if at else [])
        if at + 1 < len(spans):
            sent = hold(ready[at + 1], [rows] + early)
            after = after + [sent]
        away = other_core_part(leave, rows, after)
        near = lax.ppermute(away, "group", [(i, i ^ 1) for i in range(group_size)])
        mine, *others = add_near(stay, rows, near, chips, far[:1])
        far = [
            lax.ppermute(other, "group", [(i, i ^ (2 * d + 2)) for i in range(group_size)])
            for d, other in enumerate(others)
        ]
        group_sum.append(sum((f.astype(jnp.float32) for f in far), mine).astype(jnp.bfloat16))
        projected = projected + lax.dot_general(
            rows.reshape(slot_count * held_rows, -1),
            down_weight[0, :, span[0] : span[1]],
            (((1,), (1,)), ((), ())),
            preferred_element_type=jnp.float32,
        )
        early = others[:1] + [projected]

    route_score = jnp.sum(projected * held_hidden.astype(jnp.float32), axis=1)
    returned = lax.all_to_all(
        route_score.reshape(slot_count, held_rows),
        "expert",
        split_axis=0,
        concat_axis=0,
        tiled=True,
    )
    route_grad = pl.pallas_call(
        return_kernel, out_shape=jax.ShapeDtypeStruct(gates.T.shape, jnp.float32)
    )(returned, rank, slot_of, gates.T).T
    hidden_grad = projected.astype(jnp.bfloat16).reshape(slot_count, held_rows, hidden_units)[:, :cap_rows]

    group_sum = hold(jnp.concatenate(group_sum, axis=1), [])
    if pairs:
        other = lax.switch(
            pairing,
            [functools.partial(lax.ppermute, axis_name="expert", perm=perm) for perm in perms],
            group_sum,
        )
        copy_grad = (group_sum.astype(jnp.float32) + other.astype(jnp.float32)).astype(jnp.bfloat16)
    else:
        copy_grad = sum_copies_any(group_sum, replica_plan)
    return (route_grad, hidden_grad[None, None], copy_grad.reshape(1, shard_rows, model_width))


def solution(mesh):
    placed = (
        P(("group", "expert"), None),
        P(("group", "expert"), None),
        P(("group", "expert"), None),
        P(("group", "expert"), None),
        P(),
        P("expert", None, None),
        P("group", "expert", None, None, None),
    )
    return jax.shard_map(
        local,
        mesh=mesh,
        in_specs=placed,
        out_specs=(
            P(("group", "expert"), None),
            P("group", "expert", None, None, None),
            P("expert", "group", None),
        ),
        check_vma=False,
    )
```

```python
import functools
import itertools

import jax
import jax.numpy as jnp
import numpy as np
from jax import lax
from jax.experimental import pallas as pl
from jax.experimental.pallas import tpu as pltpu
from jax.sharding import PartitionSpec as P

HOT = 2
TILE = 512


def cost(flops):
    return pl.CostEstimate(flops=flops, bytes_accessed=flops // 300, transcendentals=0)
CHUNKS = (2048, 1024, 512)


def slot_layout(replica_plan):
    slot_count = replica_plan.shape[0]
    slot_ids = jnp.arange(slot_count, dtype=jnp.int32)
    same_expert = replica_plan[:, None] == replica_plan[None, :]
    earlier_slot = slot_ids[None, :] < slot_ids[:, None]
    ordinal = jnp.sum(same_expert & earlier_slot, axis=1)
    return (slot_ids, same_expert, ordinal)


def route_kernel(
    expert_count, cap_rows, seat, slot_plan, plan_row, routes, picks, gates, spread, rank_out, slot_out
):
    slot_count = plan_row.shape[1]
    top_count, tokens = routes.shape
    column = lax.broadcasted_iota(jnp.int32, (slot_count, 1), 0)
    plan = jnp.zeros((slot_count, 1), jnp.int32)
    for s in range(slot_count):
        plan = jnp.where(column == s, slot_plan[s], plan)
    same = plan == plan_row[...]
    slot_r = lax.broadcasted_iota(jnp.int32, (slot_count, slot_count), 0)
    slot_c = lax.broadcasted_iota(jnp.int32, (slot_count, slot_count), 1)
    copies = jnp.sum(jnp.where(same, 1.0, 0.0), axis=1, keepdims=True)
    ordinal = jnp.sum(jnp.where(same & (slot_c < slot_r), 1.0, 0.0), axis=1, keepdims=True)
    slot_ids = lax.broadcasted_iota(jnp.int32, (slot_count, tokens), 0)
    reach = jnp.zeros((slot_count, tokens), jnp.float32)
    gate_of = jnp.zeros((slot_count, tokens), jnp.float32)
    matches = []
    for k in range(top_count):
        route = routes[k : k + 1, :]
        pick = picks[k : k + 1, :].astype(jnp.float32)
        chosen = pick - copies * jnp.floor((pick + 0.5) / copies)
        match = (route == plan) & (chosen == ordinal) & (route < expert_count)
        matches.append(match)
        reach = jnp.where(match, 1.0, reach)
        gate_of = jnp.where(match, gates[k : k + 1, :], gate_of)
    before = lax.broadcasted_iota(jnp.int32, (tokens, tokens), 0) < lax.broadcasted_iota(
        jnp.int32, (tokens, tokens), 1
    )
    rank = lax.dot_general(
        reach.astype(jnp.bfloat16),
        jnp.where(before, 1.0, 0.0).astype(jnp.bfloat16),
        (((1,), (0,)), ((), ())),
        preferred_element_type=jnp.float32,
    ).astype(jnp.int32)
    kept = (reach > 0.0) & (rank < cap_rows)
    rank = jnp.where(kept, rank, -1)
    rank_out[...] = rank
    for k in range(top_count):
        slot_out[k : k + 1, :] = (
            jnp.sum(jnp.where(matches[k] & kept, slot_ids + 1, 0), axis=0, keepdims=True) - 1
        )
    row_ids = lax.broadcasted_iota(jnp.int32, spread.shape[1:], 0)
    for s in range(slot_count):
        placed = jnp.where(row_ids == rank[s : s + 1, :], gate_of[s : s + 1, :], 0.0)
        spread[seat[0] ^ s] = placed.astype(jnp.bfloat16)


def place_routes(routes, picks, gates, replica_plan, seat, expert_count, cap_rows, held_rows):
    slot_count = replica_plan.shape[0]
    top_count, tokens = routes.shape
    vmem = pl.BlockSpec(memory_space=pltpu.VMEM)
    return pl.pallas_call(
        functools.partial(route_kernel, expert_count, cap_rows),
        out_shape=(
            jax.ShapeDtypeStruct((slot_count, held_rows, tokens), jnp.bfloat16),
            jax.ShapeDtypeStruct((slot_count, tokens), jnp.int32),
            jax.ShapeDtypeStruct((top_count, tokens), jnp.int32),
        ),
        in_specs=[pl.BlockSpec(memory_space=pltpu.SMEM)] * 2 + [vmem] * 4,
        out_specs=(vmem, vmem, vmem),
    )(seat, replica_plan, replica_plan.reshape(1, slot_count), routes, picks, gates)


def send_all_kernel(seat, spread, rows, *rest):
    out = rest[-1]
    held_rows, tokens = spread.shape[1:]
    total = jnp.dot(spread[...].reshape(-1, tokens), rows[...], preferred_element_type=jnp.float32)
    for d in range(spread.shape[0]):
        out[seat[0] ^ d] = total[d * held_rows : (d + 1) * held_rows].astype(jnp.bfloat16)


def all_rows_to_send(spread, out_grad, seat, span, after):
    slot_count, held_rows, tokens = spread.shape
    start, stop = span
    return pl.pallas_call(
        send_all_kernel,
        grid=((stop - start) // TILE,),
        in_specs=[
            pl.BlockSpec(memory_space=pltpu.SMEM),
            pl.BlockSpec((slot_count, held_rows, tokens), lambda j: (0, 0, 0)),
            pl.BlockSpec((tokens, TILE), lambda j: (0, start // TILE + j)),
        ]
        + [pl.BlockSpec(memory_space=pl.ANY)] * len(after),
        out_specs=pl.BlockSpec((slot_count, held_rows, TILE), lambda j: (0, 0, j)),
        out_shape=jax.ShapeDtypeStruct((slot_count, held_rows, stop - start), jnp.bfloat16),
        cost_estimate=cost(2 * slot_count * held_rows * tokens * (stop - start)),
    )(seat, spread, out_grad, *after)


def part_kernel(leave, rows, *rest):
    flat = rows[...].reshape(-1, rows.shape[-1])
    rest[-1][...] = jnp.dot(leave[...], flat, preferred_element_type=jnp.float32).astype(jnp.bfloat16)


def other_core_part(leave, rows, after):
    slot_count, held_rows, width = rows.shape
    units, held = leave.shape
    return pl.pallas_call(
        part_kernel,
        grid=(width // TILE,),
        in_specs=[
            pl.BlockSpec((units, held), lambda j: (0, 0)),
            pl.BlockSpec((slot_count, held_rows, TILE), lambda j: (0, 0, j)),
        ]
        + [pl.BlockSpec(memory_space=pl.ANY)] * len(after),
        out_specs=pl.BlockSpec((units, TILE), lambda j: (0, j)),
        out_shape=jax.ShapeDtypeStruct((units, width), jnp.bfloat16),
        cost_estimate=cost(2 * units * held * width),
    )(leave, rows, *after)


def near_kernel(chips, stay, rows, near, *rest):
    mine, *others = rest[-chips:]
    flat = rows[...].reshape(-1, rows.shape[-1])
    shard = mine.shape[0]
    total = jnp.dot(stay[...], flat, preferred_element_type=jnp.float32) + near[...].astype(jnp.float32)
    mine[...] = total[:shard]
    for d, other in enumerate(others):
        other[...] = total[(d + 1) * shard : (d + 2) * shard].astype(jnp.bfloat16)


def add_near(stay, rows, near, chips, after):
    units, held = stay.shape
    width = rows.shape[-1]
    shard = units // chips
    return pl.pallas_call(
        functools.partial(near_kernel, chips),
        grid=(width // TILE,),
        in_specs=[
            pl.BlockSpec((units, held), lambda j: (0, 0)),
            pl.BlockSpec(rows.shape[:2] + (TILE,), lambda j: (0, 0, j)),
            pl.BlockSpec((units, TILE), lambda j: (0, j)),
        ]
        + [pl.BlockSpec(memory_space=pl.ANY)] * len(after),
        out_specs=(pl.BlockSpec((shard, TILE), lambda j: (0, j)),) * chips,
        out_shape=(jax.ShapeDtypeStruct((shard, width), jnp.float32),)
        + (jax.ShapeDtypeStruct((shard, width), jnp.bfloat16),) * (chips - 1),
        cost_estimate=cost(2 * units * held * width),
    )(stay, rows, near, *after)


def hold_kernel(*refs):
    pass


def hold(array, after):
    return pl.pallas_call(
        hold_kernel,
        in_specs=[pl.BlockSpec(memory_space=pl.ANY)] * (1 + len(after)),
        out_specs=pl.BlockSpec(memory_space=pl.ANY),
        out_shape=jax.ShapeDtypeStruct(array.shape, array.dtype),
        input_output_aliases={0: 0},
        cost_estimate=cost(1),
    )(array, *after)


def return_kernel(score, rank, slot_of, gates, out):
    slot_count, cap_rows = score.shape
    tokens = slot_of.shape[1]
    row_ids = lax.broadcasted_iota(jnp.int32, (cap_rows, tokens), 0)

    def one_slot(s, total):
        onehot = jnp.where(row_ids == rank[pl.ds(s, 1), :], 1.0, 0.0)
        value = lax.dot_general(
            score[pl.ds(s, 1), :],
            onehot,
            (((1,), (0,)), ((), ())),
            precision=lax.Precision.HIGHEST,
            preferred_element_type=jnp.float32,
        )
        return jnp.where(slot_of[...] == s, value, total)

    total = lax.fori_loop(0, slot_count, one_slot, jnp.zeros(slot_of.shape, jnp.float32))
    held_gate = gates[...].astype(jnp.bfloat16).astype(jnp.float32)
    out[...] = jnp.where(slot_of[...] >= 0, total / held_gate, 0.0)


def most_on_a_link(pairs):
    count = {}
    for a, b in pairs:
        for (row, side), (to_row, to_side) in ((divmod(a, 2), divmod(b, 2)), (divmod(b, 2), divmod(a, 2))):
            step = 1 if to_row > row else -1
            links = [(at, side, step) for at in range(row, to_row, step)]
            if side != to_side:
                links.append((to_row, side))
            for link in links:
                count[link] = count.get(link, 0) + 1
    return max(count.values())


def sets_of_pairs(slots):
    if not slots:
        yield ()
        return
    yield from sets_of_pairs(slots[1:])
    for i in range(1, len(slots)):
        for others in sets_of_pairs(slots[1:i] + slots[i + 1 :]):
            yield ((slots[0], slots[i]),) + others


def swap_choices(slot_count):
    sets = [pairs for pairs in sets_of_pairs(tuple(range(slot_count))) if len(pairs) >= 2]
    load = {pairs: most_on_a_link(pairs) for pairs in sets}
    serves = {
        pairs: [two for two in itertools.combinations(pairs, 2) if load[pairs] <= load[two]] for pairs in sets
    }
    left = [pairs for pairs in sets if len(pairs) == 2]
    table = np.zeros((3 << slot_count,), np.int32)
    perms = []
    while left:
        missing = set(left)
        best = max(sets, key=lambda pairs: sum(two in missing for two in serves[pairs]))
        for two in serves[best]:
            (a, b), (c, d) = two
            between = (a < c < b) + (a < d < b)
            table[3 * sum(1 << slot for slot in (a, b, c, d)) + between] = len(perms)
        left = [two for two in left if two not in serves[best]]
        perms.append([(a, b) for a, b in best] + [(b, a) for a, b in best])
    return table, perms


def swap_choice(replica_plan, table):
    slot_ids, same_expert, ordinal = slot_layout(replica_plan)
    hot = jnp.sum(same_expert, axis=1) > 1
    mask = jnp.sum(jnp.where(hot, 1 << slot_ids, 0))
    least = jnp.min(jnp.where(hot, slot_ids, slot_ids.shape[0]))
    expert = jnp.sum(jnp.where(slot_ids == least, replica_plan, 0))
    partner = jnp.max(jnp.where(replica_plan == expert, slot_ids, 0))
    between = jnp.sum(hot & (slot_ids > least) & (slot_ids < partner))
    place = jnp.arange(table.shape[0])
    choice = jnp.sum(jnp.where(place == 3 * mask + between, jnp.asarray(table), 0))
    mine = hot & (slot_ids == lax.axis_index("expert"))
    return choice, jnp.any(mine)


def sum_copies_any(group_sum, replica_plan):
    slot_ids, same_expert, ordinal = slot_layout(replica_plan)
    copies = jnp.sum(same_expert, axis=1)
    hot_first = (copies > 1) & (ordinal == 0)
    hot_rank = jnp.sum(hot_first[None, :] & (replica_plan[None, :] < replica_plan[:, None]), axis=1)
    my_slot = slot_ids == lax.axis_index("expert")
    my_rank = jnp.sum(jnp.where(my_slot, hot_rank, 0))
    my_hot = jnp.any(my_slot & (copies > 1))
    place_hot = (jnp.arange(HOT, dtype=jnp.int32) == my_rank) & my_hot
    group_f = group_sum.astype(jnp.float32)
    table = jnp.where(place_hot[:, None, None], group_f[None], 0.0)
    summed = lax.psum(table.astype(jnp.bfloat16), "expert").astype(jnp.float32)
    picked = jnp.sum(jnp.where(place_hot[:, None, None], summed, 0.0), axis=0)
    return jnp.where(my_hot, picked, group_f).astype(jnp.bfloat16)


def local(out_grad, gates, routes, copy_pick, replica_plan, down_weight, saved_hidden):
    slot_count = replica_plan.shape[0]
    cap_rows = saved_hidden.shape[3]
    expert_count = slot_count - slot_count // 4
    model_width = out_grad.shape[1]
    hidden_units = down_weight.shape[1]
    group_size = lax.axis_size("group")
    chips = group_size // 2
    shard_rows = hidden_units // group_size
    me = lax.axis_index("group")
    chip, core = me // 2, me % 2

    seat = lax.axis_index("expert").astype(jnp.int32).reshape(1)
    held_rows = -(-cap_rows // 16) * 16
    pad = ((0, 0), (0, held_rows - cap_rows), (0, 0))
    held_hidden = jnp.pad(saved_hidden[0, 0], pad).reshape(slot_count * held_rows, hidden_units)

    spread, rank, slot_of = place_routes(
        routes.T, copy_pick.T, gates.T, replica_plan, seat, expert_count, cap_rows, held_rows
    )

    by_owner = held_hidden.T.reshape(chips, 2, shard_rows, -1)
    by_owner = jnp.stack([by_owner[chip ^ d] for d in range(chips)])
    stay = by_owner[:, core].reshape(hidden_units // 2, -1)
    leave = by_owner[:, 1 - core].reshape(hidden_units // 2, -1)

    edges = np.cumsum((0,) + CHUNKS)
    spans = [(int(a), int(b)) for a, b in zip(edges[:-1], edges[1:])]
    ready = [all_rows_to_send(spread, out_grad, seat, span, []) for span in spans]
    pairs = slot_count - expert_count == HOT
    if pairs:
        table, perms = swap_choices(slot_count)
        pairing, copied = swap_choice(replica_plan, table)
    group_sum, projected = [], jnp.zeros((slot_count * held_rows, hidden_units), jnp.float32)
    rows, far, others = None, [], []
    early = ready[2:] + ([pairing.reshape(1)] if pairs else [])
    for span, sent in zip(spans, ready):
        if rows is not None:
            sent = hold(sent, [rows] + early)
            early = others[:1] + [projected]
        rows = lax.all_to_all(sent, "expert", split_axis=0, concat_axis=0, tiled=True)
        away = other_core_part(leave, rows, others[:1])
        near = lax.ppermute(away, "group", [(i, i ^ 1) for i in range(group_size)])
        mine, *others = add_near(stay, rows, near, chips, far[:1])
        far = [
            lax.ppermute(other, "group", [(i, i ^ (2 * d + 2)) for i in range(group_size)])
            for d, other in enumerate(others)
        ]
        group_sum.append(sum((f.astype(jnp.float32) for f in far), mine).astype(jnp.bfloat16))
        projected = projected + lax.dot_general(
            rows.reshape(slot_count * held_rows, -1),
            down_weight[0, :, span[0] : span[1]],
            (((1,), (1,)), ((), ())),
            preferred_element_type=jnp.float32,
        )

    route_score = jnp.sum(projected * held_hidden.astype(jnp.float32), axis=1)
    hidden_grad = projected.astype(jnp.bfloat16).reshape(slot_count, held_rows, hidden_units)[:, :cap_rows]
    group_sum = jnp.concatenate(group_sum, axis=1)

    def finish(swap, sums, scores, rank, slot_of, gates):
        returned = lax.all_to_all(scores, "expert", split_axis=0, concat_axis=0, tiled=True)
        route_grad = pl.pallas_call(
            return_kernel, out_shape=jax.ShapeDtypeStruct(gates.shape, jnp.float32)
        )(returned, rank, slot_of, gates)
        return swap(sums), route_grad

    scores = hold(route_score.reshape(slot_count, held_rows), [])
    state = (group_sum, scores, rank, slot_of, gates.T)
    if pairs:
        swaps = [functools.partial(lax.ppermute, axis_name="expert", perm=perm) for perm in perms]
        other, route_grad = lax.switch(pairing, [functools.partial(finish, swap) for swap in swaps], *state)
        other = jnp.where(copied, other.astype(jnp.float32), 0.0)
        copy_grad = (group_sum.astype(jnp.float32) + other).astype(jnp.bfloat16)
    else:
        _, route_grad = finish(jnp.zeros_like, *state)
        copy_grad = sum_copies_any(group_sum, replica_plan)
    return (route_grad.T, hidden_grad[None, None], copy_grad.reshape(1, shard_rows, model_width))


def solution(mesh):
    placed = (
        P(("group", "expert"), None),
        P(("group", "expert"), None),
        P(("group", "expert"), None),
        P(("group", "expert"), None),
        P(),
        P("expert", None, None),
        P("group", "expert", None, None, None),
    )
    return jax.shard_map(
        local,
        mesh=mesh,
        in_specs=placed,
        out_specs=(
            P(("group", "expert"), None),
            P("group", "expert", None, None, None),
            P("expert", "group", None),
        ),
        check_vma=False,
    )
```

```python
import functools
import itertools

import jax
import jax.numpy as jnp
import numpy as np
from jax import lax
from jax.experimental import pallas as pl
from jax.experimental.pallas import tpu as pltpu
from jax.sharding import PartitionSpec as P

HOT = 2
tile = 512


def tile_of(width, start=0):
    return next(t for t in (512, 896, 640, 384, 256, 128, width) if width % t == 0 and start % t == 0)


def cost(flops):
    return pl.CostEstimate(flops=flops, bytes_accessed=flops // 300, transcendentals=0)
CHUNKS = (2048, 1024, 512)


def slot_layout(replica_plan):
    slot_count = replica_plan.shape[0]
    slot_ids = jnp.arange(slot_count, dtype=jnp.int32)
    same_expert = replica_plan[:, None] == replica_plan[None, :]
    earlier_slot = slot_ids[None, :] < slot_ids[:, None]
    ordinal = jnp.sum(same_expert & earlier_slot, axis=1)
    return (slot_ids, same_expert, ordinal)


def route_kernel(
    expert_count, cap_rows, seat, slot_plan, plan_row, routes, picks, gates, spread, rank_out, slot_out
):
    slot_count = plan_row.shape[1]
    top_count, tokens = routes.shape
    column = lax.broadcasted_iota(jnp.int32, (slot_count, 1), 0)
    plan = jnp.zeros((slot_count, 1), jnp.int32)
    for s in range(slot_count):
        plan = jnp.where(column == s, slot_plan[s], plan)
    same = plan == plan_row[...]
    slot_r = lax.broadcasted_iota(jnp.int32, (slot_count, slot_count), 0)
    slot_c = lax.broadcasted_iota(jnp.int32, (slot_count, slot_count), 1)
    copies = jnp.sum(jnp.where(same, 1.0, 0.0), axis=1, keepdims=True)
    ordinal = jnp.sum(jnp.where(same & (slot_c < slot_r), 1.0, 0.0), axis=1, keepdims=True)
    slot_ids = lax.broadcasted_iota(jnp.int32, (slot_count, tokens), 0)
    reach = jnp.zeros((slot_count, tokens), jnp.float32)
    gate_of = jnp.zeros((slot_count, tokens), jnp.float32)
    matches = []
    for k in range(top_count):
        route = routes[k : k + 1, :]
        pick = picks[k : k + 1, :].astype(jnp.float32)
        chosen = pick - copies * jnp.floor((pick + 0.5) / copies)
        match = (route == plan) & (chosen == ordinal) & (route < expert_count)
        matches.append(match)
        reach = jnp.where(match, 1.0, reach)
        gate_of = jnp.where(match, gates[k : k + 1, :], gate_of)
    before = lax.broadcasted_iota(jnp.int32, (tokens, tokens), 0) < lax.broadcasted_iota(
        jnp.int32, (tokens, tokens), 1
    )
    rank = lax.dot_general(
        reach.astype(jnp.bfloat16),
        jnp.where(before, 1.0, 0.0).astype(jnp.bfloat16),
        (((1,), (0,)), ((), ())),
        preferred_element_type=jnp.float32,
    ).astype(jnp.int32)
    kept = (reach > 0.0) & (rank < cap_rows)
    rank = jnp.where(kept, rank, -1)
    rank_out[...] = rank
    for k in range(top_count):
        slot_out[k : k + 1, :] = (
            jnp.sum(jnp.where(matches[k] & kept, slot_ids + 1, 0), axis=0, keepdims=True) - 1
        )
    row_ids = lax.broadcasted_iota(jnp.int32, spread.shape[1:], 0)
    for s in range(slot_count):
        placed = jnp.where(row_ids == rank[s : s + 1, :], gate_of[s : s + 1, :], 0.0)
        spread[seat[0] ^ s] = placed.astype(jnp.bfloat16)


def place_routes(routes, picks, gates, replica_plan, seat, expert_count, cap_rows, held_rows):
    slot_count = replica_plan.shape[0]
    top_count, tokens = routes.shape
    vmem = pl.BlockSpec(memory_space=pltpu.VMEM)
    return pl.pallas_call(
        functools.partial(route_kernel, expert_count, cap_rows),
        out_shape=(
            jax.ShapeDtypeStruct((slot_count, held_rows, tokens), jnp.bfloat16),
            jax.ShapeDtypeStruct((slot_count, tokens), jnp.int32),
            jax.ShapeDtypeStruct((top_count, tokens), jnp.int32),
        ),
        in_specs=[pl.BlockSpec(memory_space=pltpu.SMEM)] * 2 + [vmem] * 4,
        out_specs=(vmem, vmem, vmem),
    )(seat, replica_plan, replica_plan.reshape(1, slot_count), routes, picks, gates)


def send_all_kernel(seat, spread, rows, *rest):
    out = rest[-1]
    held_rows, tokens = spread.shape[1:]
    total = jnp.dot(spread[...].reshape(-1, tokens), rows[...], preferred_element_type=jnp.float32)
    for d in range(spread.shape[0]):
        out[seat[0] ^ d] = total[d * held_rows : (d + 1) * held_rows].astype(jnp.bfloat16)


def all_rows_to_send(spread, out_grad, seat, span, after):
    slot_count, held_rows, tokens = spread.shape
    start, stop = span
    tile = tile_of(stop - start, start)
    return pl.pallas_call(
        send_all_kernel,
        grid=((stop - start) // tile,),
        in_specs=[
            pl.BlockSpec(memory_space=pltpu.SMEM),
            pl.BlockSpec((slot_count, held_rows, tokens), lambda j: (0, 0, 0)),
            pl.BlockSpec((tokens, tile), lambda j: (0, start // tile + j)),
        ]
        + [pl.BlockSpec(memory_space=pl.ANY)] * len(after),
        out_specs=pl.BlockSpec((slot_count, held_rows, tile), lambda j: (0, 0, j)),
        out_shape=jax.ShapeDtypeStruct((slot_count, held_rows, stop - start), jnp.bfloat16),
        cost_estimate=cost(2 * slot_count * held_rows * tokens * (stop - start)),
    )(seat, spread, out_grad, *after)


def part_kernel(leave, rows, *rest):
    flat = rows[...].reshape(-1, rows.shape[-1])
    rest[-1][...] = jnp.dot(leave[...], flat, preferred_element_type=jnp.float32).astype(jnp.bfloat16)


def other_core_part(leave, rows, after):
    slot_count, held_rows, width = rows.shape
    units, held = leave.shape
    tile = tile_of(width)
    return pl.pallas_call(
        part_kernel,
        grid=(width // tile,),
        in_specs=[
            pl.BlockSpec((units, held), lambda j: (0, 0)),
            pl.BlockSpec((slot_count, held_rows, tile), lambda j: (0, 0, j)),
        ]
        + [pl.BlockSpec(memory_space=pl.ANY)] * len(after),
        out_specs=pl.BlockSpec((units, tile), lambda j: (0, j)),
        out_shape=jax.ShapeDtypeStruct((units, width), jnp.bfloat16),
        cost_estimate=cost(2 * units * held * width),
    )(leave, rows, *after)


def near_kernel(chips, stay, rows, near, *rest):
    mine, *others = rest[-chips:]
    flat = rows[...].reshape(-1, rows.shape[-1])
    shard = mine.shape[0]
    total = jnp.dot(stay[...], flat, preferred_element_type=jnp.float32) + near[...].astype(jnp.float32)
    mine[...] = total[:shard]
    for d, other in enumerate(others):
        other[...] = total[(d + 1) * shard : (d + 2) * shard].astype(jnp.bfloat16)


def add_near(stay, rows, near, chips, after):
    units, held = stay.shape
    width = rows.shape[-1]
    shard = units // chips
    tile = tile_of(width)
    return pl.pallas_call(
        functools.partial(near_kernel, chips),
        grid=(width // tile,),
        in_specs=[
            pl.BlockSpec((units, held), lambda j: (0, 0)),
            pl.BlockSpec(rows.shape[:2] + (tile,), lambda j: (0, 0, j)),
            pl.BlockSpec((units, tile), lambda j: (0, j)),
        ]
        + [pl.BlockSpec(memory_space=pl.ANY)] * len(after),
        out_specs=(pl.BlockSpec((shard, tile), lambda j: (0, j)),) * chips,
        out_shape=(jax.ShapeDtypeStruct((shard, width), jnp.float32),)
        + (jax.ShapeDtypeStruct((shard, width), jnp.bfloat16),) * (chips - 1),
        cost_estimate=cost(2 * units * held * width),
    )(stay, rows, near, *after)


def hold_kernel(*refs):
    pass


def hold(array, after):
    return pl.pallas_call(
        hold_kernel,
        in_specs=[pl.BlockSpec(memory_space=pl.ANY)] * (1 + len(after)),
        out_specs=pl.BlockSpec(memory_space=pl.ANY),
        out_shape=jax.ShapeDtypeStruct(array.shape, array.dtype),
        input_output_aliases={0: 0},
        cost_estimate=cost(1),
    )(array, *after)


def return_kernel(score, rank, slot_of, gates, out):
    slot_count, cap_rows = score.shape
    top_count, tokens = slot_of.shape
    row_ids = lax.broadcasted_iota(jnp.int32, (cap_rows, tokens), 0)
    total = jnp.zeros((top_count, tokens), jnp.float32)
    for s in range(slot_count):
        onehot = jnp.where(row_ids == rank[s : s + 1, :], 1.0, 0.0)
        value = lax.dot_general(
            score[s : s + 1, :],
            onehot,
            (((1,), (0,)), ((), ())),
            precision=lax.Precision.HIGHEST,
            preferred_element_type=jnp.float32,
        )
        total = jnp.where(slot_of[...] == s, value, total)
    held_gate = gates[...].astype(jnp.bfloat16).astype(jnp.float32)
    out[...] = jnp.where(slot_of[...] >= 0, total / held_gate, 0.0)


def matchings(slot_count):
    first = np.zeros((1 << slot_count,), np.int32)
    perms = []
    for four in itertools.combinations(range(slot_count), 4):
        first[sum(1 << s for s in four)] = len(perms)
        for other in range(3):
            rest = [four[1 + i] for i in range(3) if i != other]
            pairs = ((four[0], four[1 + other]), tuple(rest))
            perms.append([(a, b) for a, b in pairs] + [(b, a) for a, b in pairs])
    return first, perms


def matching_index(replica_plan, first):
    slot_ids, same_expert, ordinal = slot_layout(replica_plan)
    hot = jnp.sum(same_expert, axis=1) > 1
    mask = jnp.sum(jnp.where(hot, 1 << slot_ids, 0))
    least = jnp.min(jnp.where(hot, slot_ids, slot_ids.shape[0]))
    expert = jnp.sum(jnp.where(slot_ids == least, replica_plan, 0))
    partner = jnp.max(jnp.where(replica_plan == expert, slot_ids, 0))
    between = jnp.sum(hot & (slot_ids > least) & (slot_ids < partner))
    base = jnp.sum(jnp.where(jnp.arange(first.shape[0]) == mask, jnp.asarray(first), 0))
    return base + between


def sum_copies_any(group_sum, replica_plan):
    slot_ids, same_expert, ordinal = slot_layout(replica_plan)
    copies = jnp.sum(same_expert, axis=1)
    hot_first = (copies > 1) & (ordinal == 0)
    hot_rank = jnp.sum(hot_first[None, :] & (replica_plan[None, :] < replica_plan[:, None]), axis=1)
    my_slot = slot_ids == lax.axis_index("expert")
    my_rank = jnp.sum(jnp.where(my_slot, hot_rank, 0))
    my_hot = jnp.any(my_slot & (copies > 1))
    place_hot = (jnp.arange(HOT, dtype=jnp.int32) == my_rank) & my_hot
    group_f = group_sum.astype(jnp.float32)
    table = jnp.where(place_hot[:, None, None], group_f[None], 0.0)
    summed = lax.psum(table.astype(jnp.bfloat16), "expert").astype(jnp.float32)
    picked = jnp.sum(jnp.where(place_hot[:, None, None], summed, 0.0), axis=0)
    return jnp.where(my_hot, picked, group_f).astype(jnp.bfloat16)


def local(out_grad, gates, routes, copy_pick, replica_plan, down_weight, saved_hidden):
    slot_count = replica_plan.shape[0]
    cap_rows = saved_hidden.shape[3]
    expert_count = slot_count - slot_count // 4
    model_width = out_grad.shape[1]
    hidden_units = down_weight.shape[1]
    group_size = lax.axis_size("group")
    chips = group_size // 2
    shard_rows = hidden_units // group_size
    me = lax.axis_index("group")
    chip, core = me // 2, me % 2

    seat = lax.axis_index("expert").astype(jnp.int32).reshape(1)
    held_rows = -(-cap_rows // 16) * 16
    pad = ((0, 0), (0, held_rows - cap_rows), (0, 0))
    held_hidden = jnp.pad(saved_hidden[0, 0], pad).reshape(slot_count * held_rows, hidden_units)

    spread, rank, slot_of = place_routes(
        routes.T, copy_pick.T, gates.T, replica_plan, seat, expert_count, cap_rows, held_rows
    )

    by_owner = held_hidden.T.reshape(chips, 2, shard_rows, -1)
    by_owner = jnp.stack([by_owner[chip ^ d] for d in range(chips)])
    stay = by_owner[:, core].reshape(hidden_units // 2, -1)
    leave = by_owner[:, 1 - core].reshape(hidden_units // 2, -1)

    edges = np.cumsum((0,) + CHUNKS)
    spans = [(int(a), int(b)) for a, b in zip(edges[:-1], edges[1:])]
    ready = [all_rows_to_send(spread, out_grad, seat, span, []) for span in spans]
    pairs = slot_count - expert_count == HOT
    if pairs:
        first, perms = matchings(slot_count)
        pairing = matching_index(replica_plan, first)
    group_sum, projected = [], jnp.zeros((slot_count * held_rows, hidden_units), jnp.float32)
    rows, far, others = None, [], []
    early = ready[2:] + ([pairing.reshape(1)] if pairs else [])
    for span, sent in zip(spans, ready):
        if rows is not None:
            sent = hold(sent, [rows] + early)
            early = others[:1] + [projected]
        rows = lax.all_to_all(sent, "expert", split_axis=0, concat_axis=0, tiled=True)
        away = other_core_part(leave, rows, others[:1])
        near = lax.ppermute(away, "group", [(i, i ^ 1) for i in range(group_size)])
        mine, *others = add_near(stay, rows, near, chips, far[:1])
        far = [
            lax.ppermute(other, "group", [(i, i ^ (2 * d + 2)) for i in range(group_size)])
            for d, other in enumerate(others)
        ]
        group_sum.append(sum((f.astype(jnp.float32) for f in far), mine).astype(jnp.bfloat16))
        projected = projected + lax.dot_general(
            rows.reshape(slot_count * held_rows, -1),
            down_weight[0, :, span[0] : span[1]],
            (((1,), (1,)), ((), ())),
            preferred_element_type=jnp.float32,
        )

    route_score = jnp.sum(projected * held_hidden.astype(jnp.float32), axis=1)
    returned = lax.all_to_all(
        hold(route_score.reshape(slot_count, held_rows), others[:1]),
        "expert",
        split_axis=0,
        concat_axis=0,
        tiled=True,
    )
    route_grad = pl.pallas_call(
        return_kernel, out_shape=jax.ShapeDtypeStruct(gates.T.shape, jnp.float32)
    )(returned, rank, slot_of, gates.T).T
    hidden_grad = projected.astype(jnp.bfloat16).reshape(slot_count, held_rows, hidden_units)[:, :cap_rows]

    group_sum = jnp.concatenate(group_sum, axis=1)
    if pairs:
        other = lax.switch(
            pairing,
            [functools.partial(lax.ppermute, axis_name="expert", perm=perm) for perm in perms],
            group_sum,
        )
        copy_grad = (group_sum.astype(jnp.float32) + other.astype(jnp.float32)).astype(jnp.bfloat16)
    else:
        copy_grad = sum_copies_any(group_sum, replica_plan)
    return (route_grad, hidden_grad[None, None], copy_grad.reshape(1, shard_rows, model_width))


def solution(mesh):
    placed = (
        P(("group", "expert"), None),
        P(("group", "expert"), None),
        P(("group", "expert"), None),
        P(("group", "expert"), None),
        P(),
        P("expert", None, None),
        P("group", "expert", None, None, None),
    )
    return jax.shard_map(
        local,
        mesh=mesh,
        in_specs=placed,
        out_specs=(
            P(("group", "expert"), None),
            P("group", "expert", None, None, None),
            P("expert", "group", None),
        ),
        check_vma=False,
    )
```

```python
import functools
import itertools

import jax
import jax.numpy as jnp
import numpy as np
from jax import lax
from jax.experimental import pallas as pl
from jax.experimental.pallas import tpu as pltpu
from jax.sharding import PartitionSpec as P

HOT = 2


def cost(flops):
    return pl.CostEstimate(flops=flops, bytes_accessed=flops // 300, transcendentals=0)
CHUNKS = (2048, 896, 640)
VMEM_BYTES = 32 * 1024 * 1024


def slot_layout(replica_plan):
    slot_count = replica_plan.shape[0]
    slot_ids = jnp.arange(slot_count, dtype=jnp.int32)
    same_expert = replica_plan[:, None] == replica_plan[None, :]
    earlier_slot = slot_ids[None, :] < slot_ids[:, None]
    ordinal = jnp.sum(same_expert & earlier_slot, axis=1)
    return (slot_ids, same_expert, ordinal)


def route_kernel(
    expert_count, cap_rows, seat, slot_plan, plan_row, routes, picks, gates, spread, rank_out, slot_out
):
    slot_count = plan_row.shape[1]
    top_count, tokens = routes.shape
    column = lax.broadcasted_iota(jnp.int32, (slot_count, 1), 0)
    plan = jnp.zeros((slot_count, 1), jnp.int32)
    for s in range(slot_count):
        plan = jnp.where(column == s, slot_plan[s], plan)
    same = plan == plan_row[...]
    slot_r = lax.broadcasted_iota(jnp.int32, (slot_count, slot_count), 0)
    slot_c = lax.broadcasted_iota(jnp.int32, (slot_count, slot_count), 1)
    copies = jnp.sum(jnp.where(same, 1.0, 0.0), axis=1, keepdims=True)
    ordinal = jnp.sum(jnp.where(same & (slot_c < slot_r), 1.0, 0.0), axis=1, keepdims=True)
    slot_ids = lax.broadcasted_iota(jnp.int32, (slot_count, tokens), 0)
    reach = jnp.zeros((slot_count, tokens), jnp.float32)
    gate_of = jnp.zeros((slot_count, tokens), jnp.float32)
    matches = []
    for k in range(top_count):
        route = routes[k : k + 1, :]
        pick = picks[k : k + 1, :].astype(jnp.float32)
        chosen = pick - copies * jnp.floor((pick + 0.5) / copies)
        match = (route == plan) & (chosen == ordinal) & (route < expert_count)
        matches.append(match)
        reach = jnp.where(match, 1.0, reach)
        gate_of = jnp.where(match, gates[k : k + 1, :], gate_of)
    before = lax.broadcasted_iota(jnp.int32, (tokens, tokens), 0) < lax.broadcasted_iota(
        jnp.int32, (tokens, tokens), 1
    )
    rank = lax.dot_general(
        reach.astype(jnp.bfloat16),
        jnp.where(before, 1.0, 0.0).astype(jnp.bfloat16),
        (((1,), (0,)), ((), ())),
        preferred_element_type=jnp.float32,
    ).astype(jnp.int32)
    kept = (reach > 0.0) & (rank < cap_rows)
    rank = jnp.where(kept, rank, -1)
    rank_out[...] = rank
    for k in range(top_count):
        slot_out[k : k + 1, :] = (
            jnp.sum(jnp.where(matches[k] & kept, slot_ids + 1, 0), axis=0, keepdims=True) - 1
        )
    row_ids = lax.broadcasted_iota(jnp.int32, spread.shape[1:], 0)
    for s in range(slot_count):
        placed = jnp.where(row_ids == rank[s : s + 1, :], gate_of[s : s + 1, :], 0.0)
        spread[seat[0] ^ s] = placed.astype(jnp.bfloat16)


def place_routes(routes, picks, gates, replica_plan, seat, expert_count, cap_rows, held_rows):
    slot_count = replica_plan.shape[0]
    top_count, tokens = routes.shape
    vmem = pl.BlockSpec(memory_space=pltpu.VMEM)
    return pl.pallas_call(
        functools.partial(route_kernel, expert_count, cap_rows),
        out_shape=(
            jax.ShapeDtypeStruct((slot_count, held_rows, tokens), jnp.bfloat16),
            jax.ShapeDtypeStruct((slot_count, tokens), jnp.int32),
            jax.ShapeDtypeStruct((top_count, tokens), jnp.int32),
        ),
        in_specs=[pl.BlockSpec(memory_space=pltpu.SMEM)] * 2 + [vmem] * 4,
        out_specs=(vmem, vmem, vmem),
    )(seat, replica_plan, replica_plan.reshape(1, slot_count), routes, picks, gates)


def send_all_kernel(seat, spread, rows, *rest):
    out = rest[-1]
    held_rows, tokens = spread.shape[1:]
    total = jnp.dot(spread[...].reshape(-1, tokens), rows[...], preferred_element_type=jnp.float32)
    for d in range(spread.shape[0]):
        out[seat[0] ^ d] = total[d * held_rows : (d + 1) * held_rows].astype(jnp.bfloat16)


def all_rows_to_send(spread, out_grad, seat, span, after):
    slot_count, held_rows, tokens = spread.shape
    start, stop = span
    tile = next(t for t in (512, 256, 128) if start % t == 0 and stop % t == 0)
    return pl.pallas_call(
        send_all_kernel,
        grid=((stop - start) // tile,),
        in_specs=[
            pl.BlockSpec(memory_space=pltpu.SMEM),
            pl.BlockSpec((slot_count, held_rows, tokens), lambda j: (0, 0, 0)),
            pl.BlockSpec((tokens, tile), lambda j: (0, start // tile + j)),
        ]
        + [pl.BlockSpec(memory_space=pl.ANY)] * len(after),
        out_specs=pl.BlockSpec((slot_count, held_rows, tile), lambda j: (0, 0, j)),
        out_shape=jax.ShapeDtypeStruct((slot_count, held_rows, stop - start), jnp.bfloat16),
        cost_estimate=cost(2 * slot_count * held_rows * tokens * (stop - start)),
    )(seat, spread, out_grad, *after)


def columns(body, width):
    tile = 512 if width % 512 == 0 else width

    @pl.loop(0, width // tile)
    def _(j):
        body(pl.ds(pl.multiple_of(j * tile, tile), tile))


def part_kernel(leave, rows, *rest):
    def some(at):
        flat = rows[:, :, at].reshape(leave.shape[1], -1)
        rest[-1][:, at] = jnp.dot(leave[...], flat, preferred_element_type=jnp.float32).astype(jnp.bfloat16)

    columns(some, rows.shape[-1])


def other_core_part(leave, rows, after):
    width = rows.shape[-1]
    units, held = leave.shape
    vmem = pl.BlockSpec(memory_space=pltpu.VMEM)
    return pl.pallas_call(
        part_kernel,
        in_specs=[vmem] * 2 + [pl.BlockSpec(memory_space=pl.ANY)] * len(after),
        out_specs=vmem,
        out_shape=jax.ShapeDtypeStruct((units, width), jnp.bfloat16),
        compiler_params=pltpu.CompilerParams(vmem_limit_bytes=VMEM_BYTES),
        cost_estimate=cost(2 * units * held * width),
    )(leave, rows, *after)


def near_kernel(chips, stay, rows, near, *rest):
    mine, *others = rest[-chips:]
    shard = mine.shape[0]

    def some(at):
        flat = rows[:, :, at].reshape(stay.shape[1], -1)
        total = jnp.dot(stay[...], flat, preferred_element_type=jnp.float32) + near[:, at].astype(jnp.float32)
        mine[:, at] = total[:shard]
        for d, other in enumerate(others):
            other[:, at] = total[(d + 1) * shard : (d + 2) * shard].astype(jnp.bfloat16)

    columns(some, rows.shape[-1])


def add_near(stay, rows, near, chips, after):
    units, held = stay.shape
    width = rows.shape[-1]
    shard = units // chips
    vmem = pl.BlockSpec(memory_space=pltpu.VMEM)
    return pl.pallas_call(
        functools.partial(near_kernel, chips),
        in_specs=[vmem] * 3 + [pl.BlockSpec(memory_space=pl.ANY)] * len(after),
        out_specs=(vmem,) * chips,
        out_shape=(jax.ShapeDtypeStruct((shard, width), jnp.float32),)
        + (jax.ShapeDtypeStruct((shard, width), jnp.bfloat16),) * (chips - 1),
        compiler_params=pltpu.CompilerParams(vmem_limit_bytes=VMEM_BYTES),
        cost_estimate=cost(2 * units * held * width),
    )(stay, rows, near, *after)


def hold_kernel(*refs):
    pass


def some_of(array):
    return array[(slice(0, 1),) * (array.ndim - 2) + (slice(0, 16), slice(0, 128))]


def hold(array, after):
    return pl.pallas_call(
        hold_kernel,
        in_specs=[pl.BlockSpec(memory_space=pl.ANY)] * (1 + len(after)),
        out_specs=pl.BlockSpec(memory_space=pl.ANY),
        out_shape=jax.ShapeDtypeStruct(array.shape, array.dtype),
        input_output_aliases={0: 0},
        cost_estimate=cost(1),
    )(array, *after)


def return_kernel(score, rank, slot_of, gates, out):
    slot_count, cap_rows = score.shape
    top_count, tokens = slot_of.shape
    row_ids = lax.broadcasted_iota(jnp.int32, (cap_rows, tokens), 0)
    total = jnp.zeros((top_count, tokens), jnp.float32)
    for s in range(slot_count):
        onehot = jnp.where(row_ids == rank[s : s + 1, :], 1.0, 0.0)
        value = lax.dot_general(
            score[s : s + 1, :],
            onehot,
            (((1,), (0,)), ((), ())),
            precision=lax.Precision.HIGHEST,
            preferred_element_type=jnp.float32,
        )
        total = jnp.where(slot_of[...] == s, value, total)
    held_gate = gates[...].astype(jnp.bfloat16).astype(jnp.float32)
    out[...] = jnp.where(slot_of[...] >= 0, total / held_gate, 0.0)


def matchings(slot_count):
    first = np.zeros((1 << slot_count,), np.int32)
    perms = []
    for four in itertools.combinations(range(slot_count), 4):
        first[sum(1 << s for s in four)] = len(perms)
        for other in range(3):
            rest = [four[1 + i] for i in range(3) if i != other]
            pairs = ((four[0], four[1 + other]), tuple(rest))
            perms.append([(a, b) for a, b in pairs] + [(b, a) for a, b in pairs])
    return first, perms


def matching_index(replica_plan, first):
    slot_ids, same_expert, ordinal = slot_layout(replica_plan)
    hot = jnp.sum(same_expert, axis=1) > 1
    mask = jnp.sum(jnp.where(hot, 1 << slot_ids, 0))
    least = jnp.min(jnp.where(hot, slot_ids, slot_ids.shape[0]))
    expert = jnp.sum(jnp.where(slot_ids == least, replica_plan, 0))
    partner = jnp.max(jnp.where(replica_plan == expert, slot_ids, 0))
    between = jnp.sum(hot & (slot_ids > least) & (slot_ids < partner))
    base = jnp.sum(jnp.where(jnp.arange(first.shape[0]) == mask, jnp.asarray(first), 0))
    return base + between


def sum_copies_any(group_sum, replica_plan):
    slot_ids, same_expert, ordinal = slot_layout(replica_plan)
    copies = jnp.sum(same_expert, axis=1)
    hot_first = (copies > 1) & (ordinal == 0)
    hot_rank = jnp.sum(hot_first[None, :] & (replica_plan[None, :] < replica_plan[:, None]), axis=1)
    my_slot = slot_ids == lax.axis_index("expert")
    my_rank = jnp.sum(jnp.where(my_slot, hot_rank, 0))
    my_hot = jnp.any(my_slot & (copies > 1))
    place_hot = (jnp.arange(HOT, dtype=jnp.int32) == my_rank) & my_hot
    group_f = group_sum.astype(jnp.float32)
    table = jnp.where(place_hot[:, None, None], group_f[None], 0.0)
    summed = lax.psum(table.astype(jnp.bfloat16), "expert").astype(jnp.float32)
    picked = jnp.sum(jnp.where(place_hot[:, None, None], summed, 0.0), axis=0)
    return jnp.where(my_hot, picked, group_f).astype(jnp.bfloat16)


def local(out_grad, gates, routes, copy_pick, replica_plan, down_weight, saved_hidden):
    slot_count = replica_plan.shape[0]
    cap_rows = saved_hidden.shape[3]
    expert_count = slot_count - slot_count // 4
    model_width = out_grad.shape[1]
    hidden_units = down_weight.shape[1]
    group_size = lax.axis_size("group")
    chips = group_size // 2
    shard_rows = hidden_units // group_size
    me = lax.axis_index("group")
    chip, core = me // 2, me % 2

    seat = lax.axis_index("expert").astype(jnp.int32).reshape(1)
    held_rows = -(-cap_rows // 16) * 16
    pad = ((0, 0), (0, held_rows - cap_rows), (0, 0))
    held_hidden = jnp.pad(saved_hidden[0, 0], pad).reshape(slot_count * held_rows, hidden_units)

    spread, rank, slot_of = place_routes(
        routes.T, copy_pick.T, gates.T, replica_plan, seat, expert_count, cap_rows, held_rows
    )

    by_owner = held_hidden.T.reshape(chips, 2, shard_rows, -1)
    by_owner = jnp.stack([by_owner[chip ^ d] for d in range(chips)])
    stay = by_owner[:, core].reshape(hidden_units // 2, -1)
    leave = by_owner[:, 1 - core].reshape(hidden_units // 2, -1)

    edges = np.cumsum((0,) + CHUNKS)
    spans = [(int(a), int(b)) for a, b in zip(edges[:-1], edges[1:])]
    ready = [all_rows_to_send(spread, out_grad, seat, span, []) for span in spans]
    pairs = slot_count - expert_count == HOT
    if pairs:
        first, perms = matchings(slot_count)
        pairing = matching_index(replica_plan, first)
    group_sum, projected = [], jnp.zeros((slot_count * held_rows, hidden_units), jnp.float32)
    rows, far, others = None, [], []
    early = [some_of(ready[2])] + ([pairing.reshape(1)] if pairs else [])
    for span, sent in zip(spans, ready):
        if rows is not None:
            sent = hold(sent, [some_of(rows)] + early)
            early = [some_of(others[0]), some_of(projected)]
        rows = lax.all_to_all(sent, "expert", split_axis=0, concat_axis=0, tiled=True)
        after = [some_of(other) for other in others[:1]]
        if span == spans[-1]:
            after = after + [some_of(projected)]
        away = other_core_part(leave, rows, after)
        near = lax.ppermute(away, "group", [(i, i ^ 1) for i in range(group_size)])
        mine, *others = add_near(stay, rows, near, chips, [some_of(other) for other in far[:1]])
        far = [
            lax.ppermute(other, "group", [(i, i ^ (2 * d + 2)) for i in range(group_size)])
            for d, other in enumerate(others)
        ]
        group_sum.append(sum((f.astype(jnp.float32) for f in far), mine).astype(jnp.bfloat16))
        projected = projected + lax.dot_general(
            rows.reshape(slot_count * held_rows, -1),
            down_weight[0, :, span[0] : span[1]],
            (((1,), (1,)), ((), ())),
            preferred_element_type=jnp.float32,
        )

    route_score = jnp.sum(projected * held_hidden.astype(jnp.float32), axis=1)
    returned = lax.all_to_all(
        hold(route_score.reshape(slot_count, held_rows), [some_of(others[0])]),
        "expert",
        split_axis=0,
        concat_axis=0,
        tiled=True,
    )
    route_grad = pl.pallas_call(
        return_kernel, out_shape=jax.ShapeDtypeStruct(gates.T.shape, jnp.float32)
    )(returned, rank, slot_of, gates.T).T
    hidden_grad = projected.astype(jnp.bfloat16).reshape(slot_count, held_rows, hidden_units)[:, :cap_rows]

    group_sum = jnp.concatenate(group_sum, axis=1)
    if pairs:
        other = lax.switch(
            pairing,
            [functools.partial(lax.ppermute, axis_name="expert", perm=perm) for perm in perms],
            group_sum,
        )
        copy_grad = (group_sum.astype(jnp.float32) + other.astype(jnp.float32)).astype(jnp.bfloat16)
    else:
        copy_grad = sum_copies_any(group_sum, replica_plan)
    return (route_grad, hidden_grad[None, None], copy_grad.reshape(1, shard_rows, model_width))


def solution(mesh):
    placed = (
        P(("group", "expert"), None),
        P(("group", "expert"), None),
        P(("group", "expert"), None),
        P(("group", "expert"), None),
        P(),
        P("expert", None, None),
        P("group", "expert", None, None, None),
    )
    return jax.shard_map(
        local,
        mesh=mesh,
        in_specs=placed,
        out_specs=(
            P(("group", "expert"), None),
            P("group", "expert", None, None, None),
            P("expert", "group", None),
        ),
        check_vma=False,
    )
```

```python
import functools
import itertools

import jax
import jax.numpy as jnp
import numpy as np
from jax import lax
from jax.experimental import pallas as pl
from jax.experimental.pallas import tpu as pltpu
from jax.sharding import PartitionSpec as P

HOT = 2


def tile_of(width, start=0):
    return next(t for t in (512, 896, 640, 384, 256, 128, width) if width % t == 0 and start % t == 0)


def cost(flops):
    return pl.CostEstimate(flops=flops, bytes_accessed=flops // 300, transcendentals=0)
CHUNKS = (2048, 896, 640)


def slot_layout(replica_plan):
    slot_count = replica_plan.shape[0]
    slot_ids = jnp.arange(slot_count, dtype=jnp.int32)
    same_expert = replica_plan[:, None] == replica_plan[None, :]
    earlier_slot = slot_ids[None, :] < slot_ids[:, None]
    ordinal = jnp.sum(same_expert & earlier_slot, axis=1)
    return (slot_ids, same_expert, ordinal)


def route_kernel(
    expert_count, cap_rows, seat, slot_plan, plan_row, routes, picks, gates, spread, rank_out, slot_out
):
    slot_count = plan_row.shape[1]
    top_count, tokens = routes.shape
    column = lax.broadcasted_iota(jnp.int32, (slot_count, 1), 0)
    plan = jnp.zeros((slot_count, 1), jnp.int32)
    for s in range(slot_count):
        plan = jnp.where(column == s, slot_plan[s], plan)
    same = plan == plan_row[...]
    slot_r = lax.broadcasted_iota(jnp.int32, (slot_count, slot_count), 0)
    slot_c = lax.broadcasted_iota(jnp.int32, (slot_count, slot_count), 1)
    copies = jnp.sum(jnp.where(same, 1.0, 0.0), axis=1, keepdims=True)
    ordinal = jnp.sum(jnp.where(same & (slot_c < slot_r), 1.0, 0.0), axis=1, keepdims=True)
    slot_ids = lax.broadcasted_iota(jnp.int32, (slot_count, tokens), 0)
    reach = jnp.zeros((slot_count, tokens), jnp.float32)
    gate_of = jnp.zeros((slot_count, tokens), jnp.float32)
    matches = []
    for k in range(top_count):
        route = routes[k : k + 1, :]
        pick = picks[k : k + 1, :].astype(jnp.float32)
        chosen = pick - copies * jnp.floor((pick + 0.5) / copies)
        match = (route == plan) & (chosen == ordinal) & (route < expert_count)
        matches.append(match)
        reach = jnp.where(match, 1.0, reach)
        gate_of = jnp.where(match, gates[k : k + 1, :], gate_of)
    before = lax.broadcasted_iota(jnp.int32, (tokens, tokens), 0) < lax.broadcasted_iota(
        jnp.int32, (tokens, tokens), 1
    )
    rank = lax.dot_general(
        reach.astype(jnp.bfloat16),
        jnp.where(before, 1.0, 0.0).astype(jnp.bfloat16),
        (((1,), (0,)), ((), ())),
        preferred_element_type=jnp.float32,
    ).astype(jnp.int32)
    kept = (reach > 0.0) & (rank < cap_rows)
    rank = jnp.where(kept, rank, -1)
    rank_out[...] = rank
    for k in range(top_count):
        slot_out[k : k + 1, :] = (
            jnp.sum(jnp.where(matches[k] & kept, slot_ids + 1, 0), axis=0, keepdims=True) - 1
        )
    row_ids = lax.broadcasted_iota(jnp.int32, spread.shape[1:], 0)
    for s in range(slot_count):
        placed = jnp.where(row_ids == rank[s : s + 1, :], gate_of[s : s + 1, :], 0.0)
        spread[seat[0] ^ s] = placed.astype(jnp.bfloat16)


def place_routes(routes, picks, gates, replica_plan, seat, expert_count, cap_rows, held_rows):
    slot_count = replica_plan.shape[0]
    top_count, tokens = routes.shape
    vmem = pl.BlockSpec(memory_space=pltpu.VMEM)
    return pl.pallas_call(
        functools.partial(route_kernel, expert_count, cap_rows),
        out_shape=(
            jax.ShapeDtypeStruct((slot_count, held_rows, tokens), jnp.bfloat16),
            jax.ShapeDtypeStruct((slot_count, tokens), jnp.int32),
            jax.ShapeDtypeStruct((top_count, tokens), jnp.int32),
        ),
        in_specs=[pl.BlockSpec(memory_space=pltpu.SMEM)] * 2 + [vmem] * 4,
        out_specs=(vmem, vmem, vmem),
    )(seat, replica_plan, replica_plan.reshape(1, slot_count), routes, picks, gates)


def send_all_kernel(seat, spread, rows, *rest):
    out = rest[-1]
    held_rows, tokens = spread.shape[1:]
    total = jnp.dot(spread[...].reshape(-1, tokens), rows[...], preferred_element_type=jnp.float32)
    for d in range(spread.shape[0]):
        out[seat[0] ^ d] = total[d * held_rows : (d + 1) * held_rows].astype(jnp.bfloat16)


def all_rows_to_send(spread, out_grad, seat, span, after):
    slot_count, held_rows, tokens = spread.shape
    start, stop = span
    tile = tile_of(stop - start, start)
    return pl.pallas_call(
        send_all_kernel,
        grid=((stop - start) // tile,),
        in_specs=[
            pl.BlockSpec(memory_space=pltpu.SMEM),
            pl.BlockSpec((slot_count, held_rows, tokens), lambda j: (0, 0, 0)),
            pl.BlockSpec((tokens, tile), lambda j: (0, start // tile + j)),
        ]
        + [pl.BlockSpec(memory_space=pl.ANY)] * len(after),
        out_specs=pl.BlockSpec((slot_count, held_rows, tile), lambda j: (0, 0, j)),
        out_shape=jax.ShapeDtypeStruct((slot_count, held_rows, stop - start), jnp.bfloat16),
        cost_estimate=cost(2 * slot_count * held_rows * tokens * (stop - start)),
    )(seat, spread, out_grad, *after)


def part_kernel(leave, rows, *rest):
    flat = rows[...].reshape(-1, rows.shape[-1])
    rest[-1][...] = jnp.dot(leave[...], flat, preferred_element_type=jnp.float32).astype(jnp.bfloat16)


def other_core_part(leave, rows, after):
    slot_count, held_rows, width = rows.shape
    units, held = leave.shape
    tile = tile_of(width)
    return pl.pallas_call(
        part_kernel,
        grid=(width // tile,),
        in_specs=[
            pl.BlockSpec((units, held), lambda j: (0, 0)),
            pl.BlockSpec((slot_count, held_rows, tile), lambda j: (0, 0, j)),
        ]
        + [pl.BlockSpec(memory_space=pl.ANY)] * len(after),
        out_specs=pl.BlockSpec((units, tile), lambda j: (0, j)),
        out_shape=jax.ShapeDtypeStruct((units, width), jnp.bfloat16),
        cost_estimate=cost(2 * units * held * width),
    )(leave, rows, *after)


def near_kernel(chips, stay, rows, near, *rest):
    mine, *others = rest[-chips:]
    flat = rows[...].reshape(-1, rows.shape[-1])
    shard = mine.shape[0]
    total = jnp.dot(stay[...], flat, preferred_element_type=jnp.float32) + near[...].astype(jnp.float32)
    mine[...] = total[:shard]
    for d, other in enumerate(others):
        other[...] = total[(d + 1) * shard : (d + 2) * shard].astype(jnp.bfloat16)


def add_near(stay, rows, near, chips, after):
    units, held = stay.shape
    width = rows.shape[-1]
    shard = units // chips
    tile = tile_of(width)
    return pl.pallas_call(
        functools.partial(near_kernel, chips),
        grid=(width // tile,),
        in_specs=[
            pl.BlockSpec((units, held), lambda j: (0, 0)),
            pl.BlockSpec(rows.shape[:2] + (tile,), lambda j: (0, 0, j)),
            pl.BlockSpec((units, tile), lambda j: (0, j)),
        ]
        + [pl.BlockSpec(memory_space=pl.ANY)] * len(after),
        out_specs=(pl.BlockSpec((shard, tile), lambda j: (0, j)),) * chips,
        out_shape=(jax.ShapeDtypeStruct((shard, width), jnp.float32),)
        + (jax.ShapeDtypeStruct((shard, width), jnp.bfloat16),) * (chips - 1),
        cost_estimate=cost(2 * units * held * width),
    )(stay, rows, near, *after)


def last_part(leave, rows, after):
    vmem = pl.BlockSpec(memory_space=pltpu.VMEM)
    return pl.pallas_call(
        part_kernel,
        in_specs=[vmem] * 2 + [pl.BlockSpec(memory_space=pl.ANY)] * len(after),
        out_specs=vmem,
        out_shape=jax.ShapeDtypeStruct((leave.shape[0], rows.shape[-1]), jnp.bfloat16),
        compiler_params=pltpu.CompilerParams(vmem_limit_bytes=32 * 1024 * 1024),
        cost_estimate=cost(2 * leave.size * rows.shape[-1]),
    )(leave, rows, *after)


def last_near(stay, rows, near, chips, after):
    shape = (stay.shape[0] // chips, rows.shape[-1])
    vmem = pl.BlockSpec(memory_space=pltpu.VMEM)
    return pl.pallas_call(
        functools.partial(near_kernel, chips),
        in_specs=[vmem] * 3 + [pl.BlockSpec(memory_space=pl.ANY)] * len(after),
        out_specs=(vmem,) * chips,
        out_shape=(jax.ShapeDtypeStruct(shape, jnp.float32),)
        + (jax.ShapeDtypeStruct(shape, jnp.bfloat16),) * (chips - 1),
        compiler_params=pltpu.CompilerParams(vmem_limit_bytes=32 * 1024 * 1024),
        cost_estimate=cost(2 * stay.size * rows.shape[-1]),
    )(stay, rows, near, *after)


def hold_kernel(*refs):
    pass


def hold(array, after):
    return pl.pallas_call(
        hold_kernel,
        in_specs=[pl.BlockSpec(memory_space=pl.ANY)] * (1 + len(after)),
        out_specs=pl.BlockSpec(memory_space=pl.ANY),
        out_shape=jax.ShapeDtypeStruct(array.shape, array.dtype),
        input_output_aliases={0: 0},
        cost_estimate=cost(1),
    )(array, *after)


def return_kernel(score, rank, slot_of, gates, out):
    slot_count, cap_rows = score.shape
    top_count, tokens = slot_of.shape
    row_ids = lax.broadcasted_iota(jnp.int32, (cap_rows, tokens), 0)
    total = jnp.zeros((top_count, tokens), jnp.float32)
    for s in range(slot_count):
        onehot = jnp.where(row_ids == rank[s : s + 1, :], 1.0, 0.0)
        value = lax.dot_general(
            score[s : s + 1, :],
            onehot,
            (((1,), (0,)), ((), ())),
            precision=lax.Precision.HIGHEST,
            preferred_element_type=jnp.float32,
        )
        total = jnp.where(slot_of[...] == s, value, total)
    held_gate = gates[...].astype(jnp.bfloat16).astype(jnp.float32)
    out[...] = jnp.where(slot_of[...] >= 0, total / held_gate, 0.0)


def matchings(slot_count):
    first = np.zeros((1 << slot_count,), np.int32)
    perms = []
    for four in itertools.combinations(range(slot_count), 4):
        first[sum(1 << s for s in four)] = len(perms)
        for other in range(3):
            rest = [four[1 + i] for i in range(3) if i != other]
            pairs = ((four[0], four[1 + other]), tuple(rest))
            perms.append([(a, b) for a, b in pairs] + [(b, a) for a, b in pairs])
    return first, perms


def matching_index(replica_plan, first):
    slot_ids, same_expert, ordinal = slot_layout(replica_plan)
    hot = jnp.sum(same_expert, axis=1) > 1
    mask = jnp.sum(jnp.where(hot, 1 << slot_ids, 0))
    least = jnp.min(jnp.where(hot, slot_ids, slot_ids.shape[0]))
    expert = jnp.sum(jnp.where(slot_ids == least, replica_plan, 0))
    partner = jnp.max(jnp.where(replica_plan == expert, slot_ids, 0))
    between = jnp.sum(hot & (slot_ids > least) & (slot_ids < partner))
    base = jnp.sum(jnp.where(jnp.arange(first.shape[0]) == mask, jnp.asarray(first), 0))
    return base + between


def sum_copies_any(group_sum, replica_plan):
    slot_ids, same_expert, ordinal = slot_layout(replica_plan)
    copies = jnp.sum(same_expert, axis=1)
    hot_first = (copies > 1) & (ordinal == 0)
    hot_rank = jnp.sum(hot_first[None, :] & (replica_plan[None, :] < replica_plan[:, None]), axis=1)
    my_slot = slot_ids == lax.axis_index("expert")
    my_rank = jnp.sum(jnp.where(my_slot, hot_rank, 0))
    my_hot = jnp.any(my_slot & (copies > 1))
    place_hot = (jnp.arange(HOT, dtype=jnp.int32) == my_rank) & my_hot
    group_f = group_sum.astype(jnp.float32)
    table = jnp.where(place_hot[:, None, None], group_f[None], 0.0)
    summed = lax.psum(table.astype(jnp.bfloat16), "expert").astype(jnp.float32)
    picked = jnp.sum(jnp.where(place_hot[:, None, None], summed, 0.0), axis=0)
    return jnp.where(my_hot, picked, group_f).astype(jnp.bfloat16)


def local(out_grad, gates, routes, copy_pick, replica_plan, down_weight, saved_hidden):
    slot_count = replica_plan.shape[0]
    cap_rows = saved_hidden.shape[3]
    expert_count = slot_count - slot_count // 4
    model_width = out_grad.shape[1]
    hidden_units = down_weight.shape[1]
    group_size = lax.axis_size("group")
    chips = group_size // 2
    shard_rows = hidden_units // group_size
    me = lax.axis_index("group")
    chip, core = me // 2, me % 2

    seat = lax.axis_index("expert").astype(jnp.int32).reshape(1)
    held_rows = -(-cap_rows // 16) * 16
    pad = ((0, 0), (0, held_rows - cap_rows), (0, 0))
    held_hidden = jnp.pad(saved_hidden[0, 0], pad).reshape(slot_count * held_rows, hidden_units)

    spread, rank, slot_of = place_routes(
        routes.T, copy_pick.T, gates.T, replica_plan, seat, expert_count, cap_rows, held_rows
    )

    by_owner = held_hidden.T.reshape(chips, 2, shard_rows, -1)
    by_owner = jnp.stack([by_owner[chip ^ d] for d in range(chips)])
    stay = by_owner[:, core].reshape(hidden_units // 2, -1)
    leave = by_owner[:, 1 - core].reshape(hidden_units // 2, -1)

    edges = np.cumsum((0,) + CHUNKS)
    spans = [(int(a), int(b)) for a, b in zip(edges[:-1], edges[1:])]
    ready = [all_rows_to_send(spread, out_grad, seat, span, []) for span in spans]
    pairs = slot_count - expert_count == HOT
    if pairs:
        first, perms = matchings(slot_count)
        pairing = matching_index(replica_plan, first)
    group_sum, projected = [], jnp.zeros((slot_count * held_rows, hidden_units), jnp.float32)
    rows, far, others = None, [], []
    early = ready[2:] + ([pairing.reshape(1)] if pairs else [])
    for span, sent in zip(spans, ready):
        if rows is not None:
            sent = hold(sent, [rows] + early)
            early = others[:1] + [projected]
        rows = lax.all_to_all(sent, "expert", split_axis=0, concat_axis=0, tiled=True)
        last = span == spans[-1]
        away = (last_part if last else other_core_part)(leave, rows, others[:1])
        near = lax.ppermute(away, "group", [(i, i ^ 1) for i in range(group_size)])
        mine, *others = (last_near if last else add_near)(stay, rows, near, chips, far[:1])
        far = [
            lax.ppermute(other, "group", [(i, i ^ (2 * d + 2)) for i in range(group_size)])
            for d, other in enumerate(others)
        ]
        group_sum.append(sum((f.astype(jnp.float32) for f in far), mine).astype(jnp.bfloat16))
        projected = projected + lax.dot_general(
            rows.reshape(slot_count * held_rows, -1),
            down_weight[0, :, span[0] : span[1]],
            (((1,), (1,)), ((), ())),
            preferred_element_type=jnp.float32,
        )

    route_score = jnp.sum(projected * held_hidden.astype(jnp.float32), axis=1)
    returned = lax.all_to_all(
        hold(route_score.reshape(slot_count, held_rows), others[:1]),
        "expert",
        split_axis=0,
        concat_axis=0,
        tiled=True,
    )
    route_grad = pl.pallas_call(
        return_kernel, out_shape=jax.ShapeDtypeStruct(gates.T.shape, jnp.float32)
    )(returned, rank, slot_of, gates.T).T
    hidden_grad = projected.astype(jnp.bfloat16).reshape(slot_count, held_rows, hidden_units)[:, :cap_rows]

    group_sum = jnp.concatenate(group_sum, axis=1)
    if pairs:
        other = lax.switch(
            pairing,
            [functools.partial(lax.ppermute, axis_name="expert", perm=perm) for perm in perms],
            group_sum,
        )
        copy_grad = (group_sum.astype(jnp.float32) + other.astype(jnp.float32)).astype(jnp.bfloat16)
    else:
        copy_grad = sum_copies_any(group_sum, replica_plan)
    return (route_grad, hidden_grad[None, None], copy_grad.reshape(1, shard_rows, model_width))


def solution(mesh):
    placed = (
        P(("group", "expert"), None),
        P(("group", "expert"), None),
        P(("group", "expert"), None),
        P(("group", "expert"), None),
        P(),
        P("expert", None, None),
        P("group", "expert", None, None, None),
    )
    return jax.shard_map(
        local,
        mesh=mesh,
        in_specs=placed,
        out_specs=(
            P(("group", "expert"), None),
            P("group", "expert", None, None, None),
            P("expert", "group", None),
        ),
        check_vma=False,
    )
```

```python
import functools
import itertools

import jax
import jax.numpy as jnp
import numpy as np
from jax import lax
from jax.experimental import pallas as pl
from jax.experimental.pallas import tpu as pltpu
from jax.sharding import PartitionSpec as P

HOT = 2


def tile_of(width, start=0):
    return next(t for t in (512, 640, 768, 384, 256, 128, width) if width % t == 0 and start % t == 0)


def cost(flops):
    return pl.CostEstimate(flops=flops, bytes_accessed=flops // 300, transcendentals=0)
CHUNKS = (1536, 1280, 768)


def slot_layout(replica_plan):
    slot_count = replica_plan.shape[0]
    slot_ids = jnp.arange(slot_count, dtype=jnp.int32)
    same_expert = replica_plan[:, None] == replica_plan[None, :]
    earlier_slot = slot_ids[None, :] < slot_ids[:, None]
    ordinal = jnp.sum(same_expert & earlier_slot, axis=1)
    return (slot_ids, same_expert, ordinal)


def route_kernel(
    expert_count, cap_rows, seat, slot_plan, plan_row, routes, picks, gates, spread, rank_out, slot_out
):
    slot_count = plan_row.shape[1]
    top_count, tokens = routes.shape
    column = lax.broadcasted_iota(jnp.int32, (slot_count, 1), 0)
    plan = jnp.zeros((slot_count, 1), jnp.int32)
    for s in range(slot_count):
        plan = jnp.where(column == s, slot_plan[s], plan)
    same = plan == plan_row[...]
    slot_r = lax.broadcasted_iota(jnp.int32, (slot_count, slot_count), 0)
    slot_c = lax.broadcasted_iota(jnp.int32, (slot_count, slot_count), 1)
    copies = jnp.sum(jnp.where(same, 1.0, 0.0), axis=1, keepdims=True)
    ordinal = jnp.sum(jnp.where(same & (slot_c < slot_r), 1.0, 0.0), axis=1, keepdims=True)
    slot_ids = lax.broadcasted_iota(jnp.int32, (slot_count, tokens), 0)
    reach = jnp.zeros((slot_count, tokens), jnp.float32)
    gate_of = jnp.zeros((slot_count, tokens), jnp.float32)
    matches = []
    for k in range(top_count):
        route = routes[k : k + 1, :]
        pick = picks[k : k + 1, :].astype(jnp.float32)
        chosen = pick - copies * jnp.floor((pick + 0.5) / copies)
        match = (route == plan) & (chosen == ordinal) & (route < expert_count)
        matches.append(match)
        reach = jnp.where(match, 1.0, reach)
        gate_of = jnp.where(match, gates[k : k + 1, :], gate_of)
    before = lax.broadcasted_iota(jnp.int32, (tokens, tokens), 0) < lax.broadcasted_iota(
        jnp.int32, (tokens, tokens), 1
    )
    rank = lax.dot_general(
        reach.astype(jnp.bfloat16),
        jnp.where(before, 1.0, 0.0).astype(jnp.bfloat16),
        (((1,), (0,)), ((), ())),
        preferred_element_type=jnp.float32,
    ).astype(jnp.int32)
    kept = (reach > 0.0) & (rank < cap_rows)
    rank = jnp.where(kept, rank, -1)
    rank_out[...] = rank
    for k in range(top_count):
        slot_out[k : k + 1, :] = (
            jnp.sum(jnp.where(matches[k] & kept, slot_ids + 1, 0), axis=0, keepdims=True) - 1
        )
    row_ids = lax.broadcasted_iota(jnp.int32, spread.shape[1:], 0)
    for s in range(slot_count):
        placed = jnp.where(row_ids == rank[s : s + 1, :], gate_of[s : s + 1, :], 0.0)
        spread[seat[0] ^ s] = placed.astype(jnp.bfloat16)


def place_routes(routes, picks, gates, replica_plan, seat, expert_count, cap_rows, held_rows):
    slot_count = replica_plan.shape[0]
    top_count, tokens = routes.shape
    vmem = pl.BlockSpec(memory_space=pltpu.VMEM)
    return pl.pallas_call(
        functools.partial(route_kernel, expert_count, cap_rows),
        out_shape=(
            jax.ShapeDtypeStruct((slot_count, held_rows, tokens), jnp.bfloat16),
            jax.ShapeDtypeStruct((slot_count, tokens), jnp.int32),
            jax.ShapeDtypeStruct((top_count, tokens), jnp.int32),
        ),
        in_specs=[pl.BlockSpec(memory_space=pltpu.SMEM)] * 2 + [vmem] * 4,
        out_specs=(vmem, vmem, vmem),
    )(seat, replica_plan, replica_plan.reshape(1, slot_count), routes, picks, gates)


def send_all_kernel(seat, spread, rows, *rest):
    out = rest[-1]
    held_rows, tokens = spread.shape[1:]
    total = jnp.dot(spread[...].reshape(-1, tokens), rows[...], preferred_element_type=jnp.float32)
    for d in range(spread.shape[0]):
        out[seat[0] ^ d] = total[d * held_rows : (d + 1) * held_rows].astype(jnp.bfloat16)


def all_rows_to_send(spread, out_grad, seat, span, after):
    slot_count, held_rows, tokens = spread.shape
    start, stop = span
    tile = tile_of(stop - start, start)
    return pl.pallas_call(
        send_all_kernel,
        grid=((stop - start) // tile,),
        in_specs=[
            pl.BlockSpec(memory_space=pltpu.SMEM),
            pl.BlockSpec((slot_count, held_rows, tokens), lambda j: (0, 0, 0)),
            pl.BlockSpec((tokens, tile), lambda j: (0, start // tile + j)),
        ]
        + [pl.BlockSpec(memory_space=pl.ANY)] * len(after),
        out_specs=pl.BlockSpec((slot_count, held_rows, tile), lambda j: (0, 0, j)),
        out_shape=jax.ShapeDtypeStruct((slot_count, held_rows, stop - start), jnp.bfloat16),
        cost_estimate=cost(2 * slot_count * held_rows * tokens * (stop - start)),
    )(seat, spread, out_grad, *after)


def part_kernel(leave, rows, *rest):
    flat = rows[...].reshape(-1, rows.shape[-1])
    rest[-1][...] = jnp.dot(leave[...], flat, preferred_element_type=jnp.float32).astype(jnp.bfloat16)


def other_core_part(leave, rows, after):
    slot_count, held_rows, width = rows.shape
    units, held = leave.shape
    tile = tile_of(width)
    return pl.pallas_call(
        part_kernel,
        grid=(width // tile,),
        in_specs=[
            pl.BlockSpec((units, held), lambda j: (0, 0)),
            pl.BlockSpec((slot_count, held_rows, tile), lambda j: (0, 0, j)),
        ]
        + [pl.BlockSpec(memory_space=pl.ANY)] * len(after),
        out_specs=pl.BlockSpec((units, tile), lambda j: (0, j)),
        out_shape=jax.ShapeDtypeStruct((units, width), jnp.bfloat16),
        cost_estimate=cost(2 * units * held * width),
    )(leave, rows, *after)


def near_kernel(chips, stay, rows, near, *rest):
    mine, *others = rest[-chips:]
    flat = rows[...].reshape(-1, rows.shape[-1])
    shard = mine.shape[0]
    total = jnp.dot(stay[...], flat, preferred_element_type=jnp.float32) + near[...].astype(jnp.float32)
    mine[...] = total[:shard]
    for d, other in enumerate(others):
        other[...] = total[(d + 1) * shard : (d + 2) * shard].astype(jnp.bfloat16)


def add_near(stay, rows, near, chips, after):
    units, held = stay.shape
    width = rows.shape[-1]
    shard = units // chips
    tile = tile_of(width)
    return pl.pallas_call(
        functools.partial(near_kernel, chips),
        grid=(width // tile,),
        in_specs=[
            pl.BlockSpec((units, held), lambda j: (0, 0)),
            pl.BlockSpec(rows.shape[:2] + (tile,), lambda j: (0, 0, j)),
            pl.BlockSpec((units, tile), lambda j: (0, j)),
        ]
        + [pl.BlockSpec(memory_space=pl.ANY)] * len(after),
        out_specs=(pl.BlockSpec((shard, tile), lambda j: (0, j)),) * chips,
        out_shape=(jax.ShapeDtypeStruct((shard, width), jnp.float32),)
        + (jax.ShapeDtypeStruct((shard, width), jnp.bfloat16),) * (chips - 1),
        cost_estimate=cost(2 * units * held * width),
    )(stay, rows, near, *after)


def last_part(leave, rows, after):
    vmem = pl.BlockSpec(memory_space=pltpu.VMEM)
    return pl.pallas_call(
        part_kernel,
        in_specs=[vmem] * 2 + [pl.BlockSpec(memory_space=pl.ANY)] * len(after),
        out_specs=vmem,
        out_shape=jax.ShapeDtypeStruct((leave.shape[0], rows.shape[-1]), jnp.bfloat16),
        compiler_params=pltpu.CompilerParams(vmem_limit_bytes=32 * 1024 * 1024),
        cost_estimate=cost(2 * leave.size * rows.shape[-1]),
    )(leave, rows, *after)


def last_near(stay, rows, near, chips, after):
    shape = (stay.shape[0] // chips, rows.shape[-1])
    vmem = pl.BlockSpec(memory_space=pltpu.VMEM)
    return pl.pallas_call(
        functools.partial(near_kernel, chips),
        in_specs=[vmem] * 3 + [pl.BlockSpec(memory_space=pl.ANY)] * len(after),
        out_specs=(vmem,) * chips,
        out_shape=(jax.ShapeDtypeStruct(shape, jnp.float32),)
        + (jax.ShapeDtypeStruct(shape, jnp.bfloat16),) * (chips - 1),
        compiler_params=pltpu.CompilerParams(vmem_limit_bytes=32 * 1024 * 1024),
        cost_estimate=cost(2 * stay.size * rows.shape[-1]),
    )(stay, rows, near, *after)


def hold_kernel(*refs):
    pass


def hold(array, after):
    return pl.pallas_call(
        hold_kernel,
        in_specs=[pl.BlockSpec(memory_space=pl.ANY)] * (1 + len(after)),
        out_specs=pl.BlockSpec(memory_space=pl.ANY),
        out_shape=jax.ShapeDtypeStruct(array.shape, array.dtype),
        input_output_aliases={0: 0},
        cost_estimate=cost(1),
    )(array, *after)


def return_kernel(score, rank, slot_of, gates, out):
    slot_count, cap_rows = score.shape
    top_count, tokens = slot_of.shape
    row_ids = lax.broadcasted_iota(jnp.int32, (cap_rows, tokens), 0)
    total = jnp.zeros((top_count, tokens), jnp.float32)
    for s in range(slot_count):
        onehot = jnp.where(row_ids == rank[s : s + 1, :], 1.0, 0.0)
        value = lax.dot_general(
            score[s : s + 1, :],
            onehot,
            (((1,), (0,)), ((), ())),
            precision=lax.Precision.HIGHEST,
            preferred_element_type=jnp.float32,
        )
        total = jnp.where(slot_of[...] == s, value, total)
    held_gate = gates[...].astype(jnp.bfloat16).astype(jnp.float32)
    out[...] = jnp.where(slot_of[...] >= 0, total / held_gate, 0.0)


def matchings(slot_count):
    first = np.zeros((1 << slot_count,), np.int32)
    perms = []
    for four in itertools.combinations(range(slot_count), 4):
        first[sum(1 << s for s in four)] = len(perms)
        for other in range(3):
            rest = [four[1 + i] for i in range(3) if i != other]
            pairs = ((four[0], four[1 + other]), tuple(rest))
            perms.append([(a, b) for a, b in pairs] + [(b, a) for a, b in pairs])
    return first, perms


def matching_index(replica_plan, first):
    slot_ids, same_expert, ordinal = slot_layout(replica_plan)
    hot = jnp.sum(same_expert, axis=1) > 1
    mask = jnp.sum(jnp.where(hot, 1 << slot_ids, 0))
    least = jnp.min(jnp.where(hot, slot_ids, slot_ids.shape[0]))
    expert = jnp.sum(jnp.where(slot_ids == least, replica_plan, 0))
    partner = jnp.max(jnp.where(replica_plan == expert, slot_ids, 0))
    between = jnp.sum(hot & (slot_ids > least) & (slot_ids < partner))
    base = jnp.sum(jnp.where(jnp.arange(first.shape[0]) == mask, jnp.asarray(first), 0))
    return base + between


def sum_copies_any(group_sum, replica_plan):
    slot_ids, same_expert, ordinal = slot_layout(replica_plan)
    copies = jnp.sum(same_expert, axis=1)
    hot_first = (copies > 1) & (ordinal == 0)
    hot_rank = jnp.sum(hot_first[None, :] & (replica_plan[None, :] < replica_plan[:, None]), axis=1)
    my_slot = slot_ids == lax.axis_index("expert")
    my_rank = jnp.sum(jnp.where(my_slot, hot_rank, 0))
    my_hot = jnp.any(my_slot & (copies > 1))
    place_hot = (jnp.arange(HOT, dtype=jnp.int32) == my_rank) & my_hot
    group_f = group_sum.astype(jnp.float32)
    table = jnp.where(place_hot[:, None, None], group_f[None], 0.0)
    summed = lax.psum(table.astype(jnp.bfloat16), "expert").astype(jnp.float32)
    picked = jnp.sum(jnp.where(place_hot[:, None, None], summed, 0.0), axis=0)
    return jnp.where(my_hot, picked, group_f).astype(jnp.bfloat16)


def local(out_grad, gates, routes, copy_pick, replica_plan, down_weight, saved_hidden):
    slot_count = replica_plan.shape[0]
    cap_rows = saved_hidden.shape[3]
    expert_count = slot_count - slot_count // 4
    model_width = out_grad.shape[1]
    hidden_units = down_weight.shape[1]
    group_size = lax.axis_size("group")
    chips = group_size // 2
    shard_rows = hidden_units // group_size
    me = lax.axis_index("group")
    chip, core = me // 2, me % 2

    seat = lax.axis_index("expert").astype(jnp.int32).reshape(1)
    held_rows = -(-cap_rows // 16) * 16
    pad = ((0, 0), (0, held_rows - cap_rows), (0, 0))
    held_hidden = jnp.pad(saved_hidden[0, 0], pad).reshape(slot_count * held_rows, hidden_units)

    spread, rank, slot_of = place_routes(
        routes.T, copy_pick.T, gates.T, replica_plan, seat, expert_count, cap_rows, held_rows
    )

    by_owner = held_hidden.T.reshape(chips, 2, shard_rows, -1)
    by_owner = jnp.stack([by_owner[chip ^ d] for d in range(chips)])
    stay = by_owner[:, core].reshape(hidden_units // 2, -1)
    leave = by_owner[:, 1 - core].reshape(hidden_units // 2, -1)

    edges = np.cumsum((0,) + CHUNKS)
    spans = [(int(a), int(b)) for a, b in zip(edges[:-1], edges[1:])]
    ready = [all_rows_to_send(spread, out_grad, seat, span, []) for span in spans]
    pairs = slot_count - expert_count == HOT
    if pairs:
        first, perms = matchings(slot_count)
        pairing = matching_index(replica_plan, first)
    group_sum, projected = [], jnp.zeros((slot_count * held_rows, hidden_units), jnp.float32)
    far, others = [], []
    early = ready[2:] + ([pairing.reshape(1)] if pairs else [])
    sent = ready[0]
    for at, span in enumerate(spans):
        last = span == spans[-1]
        rows = lax.all_to_all(sent, "expert", split_axis=0, concat_axis=0, tiled=True)
        after = others[:1] + ([projected] if at else [])
        if not last:
            sent = hold(ready[at + 1], [rows] + early)
            after = after + [sent]
        away = (last_part if last else other_core_part)(leave, rows, after)
        near = lax.ppermute(away, "group", [(i, i ^ 1) for i in range(group_size)])
        mine, *others = (last_near if last else add_near)(stay, rows, near, chips, far[:1])
        far = [
            lax.ppermute(other, "group", [(i, i ^ (2 * d + 2)) for i in range(group_size)])
            for d, other in enumerate(others)
        ]
        group_sum.append(sum((f.astype(jnp.float32) for f in far), mine).astype(jnp.bfloat16))
        projected = projected + lax.dot_general(
            rows.reshape(slot_count * held_rows, -1),
            down_weight[0, :, span[0] : span[1]],
            (((1,), (1,)), ((), ())),
            preferred_element_type=jnp.float32,
        )
        early = far[:1] + [projected]

    route_score = jnp.sum(projected * held_hidden.astype(jnp.float32), axis=1)
    returned = lax.all_to_all(
        hold(route_score.reshape(slot_count, held_rows), others[:1]),
        "expert",
        split_axis=0,
        concat_axis=0,
        tiled=True,
    )
    route_grad = pl.pallas_call(
        return_kernel, out_shape=jax.ShapeDtypeStruct(gates.T.shape, jnp.float32)
    )(returned, rank, slot_of, gates.T).T
    hidden_grad = projected.astype(jnp.bfloat16).reshape(slot_count, held_rows, hidden_units)[:, :cap_rows]

    group_sum = jnp.concatenate(group_sum, axis=1)
    if pairs:
        other = lax.switch(
            pairing,
            [functools.partial(lax.ppermute, axis_name="expert", perm=perm) for perm in perms],
            group_sum,
        )
        copy_grad = (group_sum.astype(jnp.float32) + other.astype(jnp.float32)).astype(jnp.bfloat16)
    else:
        copy_grad = sum_copies_any(group_sum, replica_plan)
    return (route_grad, hidden_grad[None, None], copy_grad.reshape(1, shard_rows, model_width))


def solution(mesh):
    placed = (
        P(("group", "expert"), None),
        P(("group", "expert"), None),
        P(("group", "expert"), None),
        P(("group", "expert"), None),
        P(),
        P("expert", None, None),
        P("group", "expert", None, None, None),
    )
    return jax.shard_map(
        local,
        mesh=mesh,
        in_specs=placed,
        out_specs=(
            P(("group", "expert"), None),
            P("group", "expert", None, None, None),
            P("expert", "group", None),
        ),
        check_vma=False,
    )
```

```python
import functools
import itertools

import jax
import jax.numpy as jnp
import numpy as np
from jax import lax
from jax.experimental import pallas as pl
from jax.experimental.pallas import tpu as pltpu
from jax.sharding import PartitionSpec as P

HOT = 2


def tile_of(width, start=0):
    return next(t for t in (512, 640, 768, 1408, 896, 384, 256, 128, width) if width % t == 0 and start % t == 0)


def cost(flops):
    return pl.CostEstimate(flops=flops, bytes_accessed=flops // 300, transcendentals=0)
CHUNKS = (1280, 1408, 896)


def slot_layout(replica_plan):
    slot_count = replica_plan.shape[0]
    slot_ids = jnp.arange(slot_count, dtype=jnp.int32)
    same_expert = replica_plan[:, None] == replica_plan[None, :]
    earlier_slot = slot_ids[None, :] < slot_ids[:, None]
    ordinal = jnp.sum(same_expert & earlier_slot, axis=1)
    return (slot_ids, same_expert, ordinal)


def route_kernel(
    expert_count, cap_rows, seat, slot_plan, plan_row, routes, picks, gates, spread, rank_out, slot_out
):
    slot_count = plan_row.shape[1]
    top_count, tokens = routes.shape
    column = lax.broadcasted_iota(jnp.int32, (slot_count, 1), 0)
    plan = jnp.zeros((slot_count, 1), jnp.int32)
    for s in range(slot_count):
        plan = jnp.where(column == s, slot_plan[s], plan)
    same = plan == plan_row[...]
    slot_r = lax.broadcasted_iota(jnp.int32, (slot_count, slot_count), 0)
    slot_c = lax.broadcasted_iota(jnp.int32, (slot_count, slot_count), 1)
    copies = jnp.sum(jnp.where(same, 1.0, 0.0), axis=1, keepdims=True)
    ordinal = jnp.sum(jnp.where(same & (slot_c < slot_r), 1.0, 0.0), axis=1, keepdims=True)
    slot_ids = lax.broadcasted_iota(jnp.int32, (slot_count, tokens), 0)
    reach = jnp.zeros((slot_count, tokens), jnp.float32)
    gate_of = jnp.zeros((slot_count, tokens), jnp.float32)
    matches = []
    for k in range(top_count):
        route = routes[k : k + 1, :]
        pick = picks[k : k + 1, :].astype(jnp.float32)
        chosen = pick - copies * jnp.floor((pick + 0.5) / copies)
        match = (route == plan) & (chosen == ordinal) & (route < expert_count)
        matches.append(match)
        reach = jnp.where(match, 1.0, reach)
        gate_of = jnp.where(match, gates[k : k + 1, :], gate_of)
    before = lax.broadcasted_iota(jnp.int32, (tokens, tokens), 0) < lax.broadcasted_iota(
        jnp.int32, (tokens, tokens), 1
    )
    rank = lax.dot_general(
        reach.astype(jnp.bfloat16),
        jnp.where(before, 1.0, 0.0).astype(jnp.bfloat16),
        (((1,), (0,)), ((), ())),
        preferred_element_type=jnp.float32,
    ).astype(jnp.int32)
    kept = (reach > 0.0) & (rank < cap_rows)
    rank = jnp.where(kept, rank, -1)
    rank_out[...] = rank
    for k in range(top_count):
        slot_out[k : k + 1, :] = (
            jnp.sum(jnp.where(matches[k] & kept, slot_ids + 1, 0), axis=0, keepdims=True) - 1
        )
    row_ids = lax.broadcasted_iota(jnp.int32, spread.shape[1:], 0)
    for s in range(slot_count):
        placed = jnp.where(row_ids == rank[s : s + 1, :], gate_of[s : s + 1, :], 0.0)
        spread[seat[0] ^ s] = placed.astype(jnp.bfloat16)


def place_routes(routes, picks, gates, replica_plan, seat, expert_count, cap_rows, held_rows):
    slot_count = replica_plan.shape[0]
    top_count, tokens = routes.shape
    vmem = pl.BlockSpec(memory_space=pltpu.VMEM)
    return pl.pallas_call(
        functools.partial(route_kernel, expert_count, cap_rows),
        out_shape=(
            jax.ShapeDtypeStruct((slot_count, held_rows, tokens), jnp.bfloat16),
            jax.ShapeDtypeStruct((slot_count, tokens), jnp.int32),
            jax.ShapeDtypeStruct((top_count, tokens), jnp.int32),
        ),
        in_specs=[pl.BlockSpec(memory_space=pltpu.SMEM)] * 2 + [vmem] * 4,
        out_specs=(vmem, vmem, vmem),
    )(seat, replica_plan, replica_plan.reshape(1, slot_count), routes, picks, gates)


def send_all_kernel(seat, spread, rows, *rest):
    out = rest[-1]
    held_rows, tokens = spread.shape[1:]
    total = jnp.dot(spread[...].reshape(-1, tokens), rows[...], preferred_element_type=jnp.float32)
    for d in range(spread.shape[0]):
        out[seat[0] ^ d] = total[d * held_rows : (d + 1) * held_rows].astype(jnp.bfloat16)


def all_rows_to_send(spread, out_grad, seat, span, after):
    slot_count, held_rows, tokens = spread.shape
    start, stop = span
    tile = tile_of(stop - start, start)
    return pl.pallas_call(
        send_all_kernel,
        grid=((stop - start) // tile,),
        in_specs=[
            pl.BlockSpec(memory_space=pltpu.SMEM),
            pl.BlockSpec((slot_count, held_rows, tokens), lambda j: (0, 0, 0)),
            pl.BlockSpec((tokens, tile), lambda j: (0, start // tile + j)),
        ]
        + [pl.BlockSpec(memory_space=pl.ANY)] * len(after),
        out_specs=pl.BlockSpec((slot_count, held_rows, tile), lambda j: (0, 0, j)),
        out_shape=jax.ShapeDtypeStruct((slot_count, held_rows, stop - start), jnp.bfloat16),
        cost_estimate=cost(2 * slot_count * held_rows * tokens * (stop - start)),
    )(seat, spread, out_grad, *after)


def part_kernel(leave, rows, *rest):
    flat = rows[...].reshape(-1, rows.shape[-1])
    rest[-1][...] = jnp.dot(leave[...], flat, preferred_element_type=jnp.float32).astype(jnp.bfloat16)


def other_core_part(leave, rows, after):
    slot_count, held_rows, width = rows.shape
    units, held = leave.shape
    tile = tile_of(width)
    return pl.pallas_call(
        part_kernel,
        grid=(width // tile,),
        in_specs=[
            pl.BlockSpec((units, held), lambda j: (0, 0)),
            pl.BlockSpec((slot_count, held_rows, tile), lambda j: (0, 0, j)),
        ]
        + [pl.BlockSpec(memory_space=pl.ANY)] * len(after),
        out_specs=pl.BlockSpec((units, tile), lambda j: (0, j)),
        out_shape=jax.ShapeDtypeStruct((units, width), jnp.bfloat16),
        compiler_params=pltpu.CompilerParams(vmem_limit_bytes=48 * 1024 * 1024),
        cost_estimate=cost(2 * units * held * width),
    )(leave, rows, *after)


def near_kernel(chips, stay, rows, near, *rest):
    mine, *others = rest[-chips:]
    flat = rows[...].reshape(-1, rows.shape[-1])
    shard = mine.shape[0]
    total = jnp.dot(stay[...], flat, preferred_element_type=jnp.float32) + near[...].astype(jnp.float32)
    mine[...] = total[:shard]
    for d, other in enumerate(others):
        other[...] = total[(d + 1) * shard : (d + 2) * shard].astype(jnp.bfloat16)


def add_near(stay, rows, near, chips, after):
    units, held = stay.shape
    width = rows.shape[-1]
    shard = units // chips
    tile = tile_of(width)
    return pl.pallas_call(
        functools.partial(near_kernel, chips),
        grid=(width // tile,),
        in_specs=[
            pl.BlockSpec((units, held), lambda j: (0, 0)),
            pl.BlockSpec(rows.shape[:2] + (tile,), lambda j: (0, 0, j)),
            pl.BlockSpec((units, tile), lambda j: (0, j)),
        ]
        + [pl.BlockSpec(memory_space=pl.ANY)] * len(after),
        out_specs=(pl.BlockSpec((shard, tile), lambda j: (0, j)),) * chips,
        out_shape=(jax.ShapeDtypeStruct((shard, width), jnp.float32),)
        + (jax.ShapeDtypeStruct((shard, width), jnp.bfloat16),) * (chips - 1),
        compiler_params=pltpu.CompilerParams(vmem_limit_bytes=48 * 1024 * 1024),
        cost_estimate=cost(2 * units * held * width),
    )(stay, rows, near, *after)


def last_part(leave, rows, after):
    vmem = pl.BlockSpec(memory_space=pltpu.VMEM)
    return pl.pallas_call(
        part_kernel,
        in_specs=[vmem] * 2 + [pl.BlockSpec(memory_space=pl.ANY)] * len(after),
        out_specs=vmem,
        out_shape=jax.ShapeDtypeStruct((leave.shape[0], rows.shape[-1]), jnp.bfloat16),
        compiler_params=pltpu.CompilerParams(vmem_limit_bytes=32 * 1024 * 1024),
        cost_estimate=cost(2 * leave.size * rows.shape[-1]),
    )(leave, rows, *after)


def last_near(stay, rows, near, chips, after):
    shape = (stay.shape[0] // chips, rows.shape[-1])
    vmem = pl.BlockSpec(memory_space=pltpu.VMEM)
    return pl.pallas_call(
        functools.partial(near_kernel, chips),
        in_specs=[vmem] * 3 + [pl.BlockSpec(memory_space=pl.ANY)] * len(after),
        out_specs=(vmem,) * chips,
        out_shape=(jax.ShapeDtypeStruct(shape, jnp.float32),)
        + (jax.ShapeDtypeStruct(shape, jnp.bfloat16),) * (chips - 1),
        compiler_params=pltpu.CompilerParams(vmem_limit_bytes=32 * 1024 * 1024),
        cost_estimate=cost(2 * stay.size * rows.shape[-1]),
    )(stay, rows, near, *after)


def hold_kernel(*refs):
    pass


def hold(array, after):
    return pl.pallas_call(
        hold_kernel,
        in_specs=[pl.BlockSpec(memory_space=pl.ANY)] * (1 + len(after)),
        out_specs=pl.BlockSpec(memory_space=pl.ANY),
        out_shape=jax.ShapeDtypeStruct(array.shape, array.dtype),
        input_output_aliases={0: 0},
        cost_estimate=cost(1),
    )(array, *after)


def return_kernel(score, rank, slot_of, gates, out):
    slot_count, cap_rows = score.shape
    top_count, tokens = slot_of.shape
    row_ids = lax.broadcasted_iota(jnp.int32, (cap_rows, tokens), 0)
    total = jnp.zeros((top_count, tokens), jnp.float32)
    for s in range(slot_count):
        onehot = jnp.where(row_ids == rank[s : s + 1, :], 1.0, 0.0)
        value = lax.dot_general(
            score[s : s + 1, :],
            onehot,
            (((1,), (0,)), ((), ())),
            precision=lax.Precision.HIGHEST,
            preferred_element_type=jnp.float32,
        )
        total = jnp.where(slot_of[...] == s, value, total)
    held_gate = gates[...].astype(jnp.bfloat16).astype(jnp.float32)
    out[...] = jnp.where(slot_of[...] >= 0, total / held_gate, 0.0)


def matchings(slot_count):
    first = np.zeros((1 << slot_count,), np.int32)
    perms = []
    for four in itertools.combinations(range(slot_count), 4):
        first[sum(1 << s for s in four)] = len(perms)
        for other in range(3):
            rest = [four[1 + i] for i in range(3) if i != other]
            pairs = ((four[0], four[1 + other]), tuple(rest))
            perms.append([(a, b) for a, b in pairs] + [(b, a) for a, b in pairs])
    return first, perms


def matching_index(replica_plan, first):
    slot_ids, same_expert, ordinal = slot_layout(replica_plan)
    hot = jnp.sum(same_expert, axis=1) > 1
    mask = jnp.sum(jnp.where(hot, 1 << slot_ids, 0))
    least = jnp.min(jnp.where(hot, slot_ids, slot_ids.shape[0]))
    expert = jnp.sum(jnp.where(slot_ids == least, replica_plan, 0))
    partner = jnp.max(jnp.where(replica_plan == expert, slot_ids, 0))
    between = jnp.sum(hot & (slot_ids > least) & (slot_ids < partner))
    base = jnp.sum(jnp.where(jnp.arange(first.shape[0]) == mask, jnp.asarray(first), 0))
    return base + between


def sum_copies_any(group_sum, replica_plan):
    slot_ids, same_expert, ordinal = slot_layout(replica_plan)
    copies = jnp.sum(same_expert, axis=1)
    hot_first = (copies > 1) & (ordinal == 0)
    hot_rank = jnp.sum(hot_first[None, :] & (replica_plan[None, :] < replica_plan[:, None]), axis=1)
    my_slot = slot_ids == lax.axis_index("expert")
    my_rank = jnp.sum(jnp.where(my_slot, hot_rank, 0))
    my_hot = jnp.any(my_slot & (copies > 1))
    place_hot = (jnp.arange(HOT, dtype=jnp.int32) == my_rank) & my_hot
    group_f = group_sum.astype(jnp.float32)
    table = jnp.where(place_hot[:, None, None], group_f[None], 0.0)
    summed = lax.psum(table.astype(jnp.bfloat16), "expert").astype(jnp.float32)
    picked = jnp.sum(jnp.where(place_hot[:, None, None], summed, 0.0), axis=0)
    return jnp.where(my_hot, picked, group_f).astype(jnp.bfloat16)


def local(out_grad, gates, routes, copy_pick, replica_plan, down_weight, saved_hidden):
    slot_count = replica_plan.shape[0]
    cap_rows = saved_hidden.shape[3]
    expert_count = slot_count - slot_count // 4
    model_width = out_grad.shape[1]
    hidden_units = down_weight.shape[1]
    group_size = lax.axis_size("group")
    chips = group_size // 2
    shard_rows = hidden_units // group_size
    me = lax.axis_index("group")
    chip, core = me // 2, me % 2

    seat = lax.axis_index("expert").astype(jnp.int32).reshape(1)
    held_rows = -(-cap_rows // 16) * 16
    pad = ((0, 0), (0, held_rows - cap_rows), (0, 0))
    held_hidden = jnp.pad(saved_hidden[0, 0], pad).reshape(slot_count * held_rows, hidden_units)

    spread, rank, slot_of = place_routes(
        routes.T, copy_pick.T, gates.T, replica_plan, seat, expert_count, cap_rows, held_rows
    )

    by_owner = held_hidden.T.reshape(chips, 2, shard_rows, -1)
    by_owner = jnp.stack([by_owner[chip ^ d] for d in range(chips)])
    stay = by_owner[:, core].reshape(hidden_units // 2, -1)
    leave = by_owner[:, 1 - core].reshape(hidden_units // 2, -1)

    edges = np.cumsum((0,) + CHUNKS)
    spans = [(int(a), int(b)) for a, b in zip(edges[:-1], edges[1:])]
    ready = [all_rows_to_send(spread, out_grad, seat, span, []) for span in spans]
    pairs = slot_count - expert_count == HOT
    if pairs:
        first, perms = matchings(slot_count)
        pairing = matching_index(replica_plan, first)
    group_sum, projected = [], jnp.zeros((slot_count * held_rows, hidden_units), jnp.float32)
    far, others = [], []
    early = ready[2:] + ([pairing.reshape(1)] if pairs else [])
    sent = ready[0]
    for at, span in enumerate(spans):
        last = span == spans[-1]
        rows = lax.all_to_all(sent, "expert", split_axis=0, concat_axis=0, tiled=True)
        after = others[:1] + ([projected] if at else [])
        if not last:
            sent = hold(ready[at + 1], [rows] + early)
            after = after + [sent]
        away = (last_part if last else other_core_part)(leave, rows, after)
        near = lax.ppermute(away, "group", [(i, i ^ 1) for i in range(group_size)])
        mine, *others = (last_near if last else add_near)(stay, rows, near, chips, far[:1])
        far = [
            lax.ppermute(other, "group", [(i, i ^ (2 * d + 2)) for i in range(group_size)])
            for d, other in enumerate(others)
        ]
        group_sum.append(sum((f.astype(jnp.float32) for f in far), mine).astype(jnp.bfloat16))
        projected = projected + lax.dot_general(
            rows.reshape(slot_count * held_rows, -1),
            down_weight[0, :, span[0] : span[1]],
            (((1,), (1,)), ((), ())),
            preferred_element_type=jnp.float32,
        )
        early = far[:1] + [projected]

    route_score = jnp.sum(projected * held_hidden.astype(jnp.float32), axis=1)
    returned = lax.all_to_all(
        hold(route_score.reshape(slot_count, held_rows), others[:1]),
        "expert",
        split_axis=0,
        concat_axis=0,
        tiled=True,
    )
    route_grad = pl.pallas_call(
        return_kernel, out_shape=jax.ShapeDtypeStruct(gates.T.shape, jnp.float32)
    )(returned, rank, slot_of, gates.T).T
    hidden_grad = projected.astype(jnp.bfloat16).reshape(slot_count, held_rows, hidden_units)[:, :cap_rows]

    group_sum = jnp.concatenate(group_sum, axis=1)
    if pairs:
        other = lax.switch(
            pairing,
            [functools.partial(lax.ppermute, axis_name="expert", perm=perm) for perm in perms],
            group_sum,
        )
        copy_grad = (group_sum.astype(jnp.float32) + other.astype(jnp.float32)).astype(jnp.bfloat16)
    else:
        copy_grad = sum_copies_any(group_sum, replica_plan)
    return (route_grad, hidden_grad[None, None], copy_grad.reshape(1, shard_rows, model_width))


def solution(mesh):
    placed = (
        P(("group", "expert"), None),
        P(("group", "expert"), None),
        P(("group", "expert"), None),
        P(("group", "expert"), None),
        P(),
        P("expert", None, None),
        P("group", "expert", None, None, None),
    )
    return jax.shard_map(
        local,
        mesh=mesh,
        in_specs=placed,
        out_specs=(
            P(("group", "expert"), None),
            P("group", "expert", None, None, None),
            P("expert", "group", None),
        ),
        check_vma=False,
    )
```

```python
import functools
import itertools

import jax
import jax.numpy as jnp
import numpy as np
from jax import lax
from jax.experimental import pallas as pl
from jax.experimental.pallas import tpu as pltpu
from jax.sharding import PartitionSpec as P

HOT = 2


def tile_of(width, start=0):
    return next(t for t in (512, 640, 768, 1408, 896, 384, 256, 128, width) if width % t == 0 and start % t == 0)


def cost(flops):
    return pl.CostEstimate(flops=flops, bytes_accessed=flops // 300, transcendentals=0)
CHUNKS = (1536, 1408, 640)


def slot_layout(replica_plan):
    slot_count = replica_plan.shape[0]
    slot_ids = jnp.arange(slot_count, dtype=jnp.int32)
    same_expert = replica_plan[:, None] == replica_plan[None, :]
    earlier_slot = slot_ids[None, :] < slot_ids[:, None]
    ordinal = jnp.sum(same_expert & earlier_slot, axis=1)
    return (slot_ids, same_expert, ordinal)


def route_kernel(
    expert_count, cap_rows, seat, slot_plan, plan_row, routes, picks, gates, spread, rank_out, slot_out
):
    slot_count = plan_row.shape[1]
    top_count, tokens = routes.shape
    column = lax.broadcasted_iota(jnp.int32, (slot_count, 1), 0)
    plan = jnp.zeros((slot_count, 1), jnp.int32)
    for s in range(slot_count):
        plan = jnp.where(column == s, slot_plan[s], plan)
    same = plan == plan_row[...]
    slot_r = lax.broadcasted_iota(jnp.int32, (slot_count, slot_count), 0)
    slot_c = lax.broadcasted_iota(jnp.int32, (slot_count, slot_count), 1)
    copies = jnp.sum(jnp.where(same, 1.0, 0.0), axis=1, keepdims=True)
    ordinal = jnp.sum(jnp.where(same & (slot_c < slot_r), 1.0, 0.0), axis=1, keepdims=True)
    slot_ids = lax.broadcasted_iota(jnp.int32, (slot_count, tokens), 0)
    reach = jnp.zeros((slot_count, tokens), jnp.float32)
    gate_of = jnp.zeros((slot_count, tokens), jnp.float32)
    matches = []
    for k in range(top_count):
        route = routes[k : k + 1, :]
        pick = picks[k : k + 1, :].astype(jnp.float32)
        chosen = pick - copies * jnp.floor((pick + 0.5) / copies)
        match = (route == plan) & (chosen == ordinal) & (route < expert_count)
        matches.append(match)
        reach = jnp.where(match, 1.0, reach)
        gate_of = jnp.where(match, gates[k : k + 1, :], gate_of)
    before = lax.broadcasted_iota(jnp.int32, (tokens, tokens), 0) < lax.broadcasted_iota(
        jnp.int32, (tokens, tokens), 1
    )
    rank = lax.dot_general(
        reach.astype(jnp.bfloat16),
        jnp.where(before, 1.0, 0.0).astype(jnp.bfloat16),
        (((1,), (0,)), ((), ())),
        preferred_element_type=jnp.float32,
    ).astype(jnp.int32)
    kept = (reach > 0.0) & (rank < cap_rows)
    rank = jnp.where(kept, rank, -1)
    rank_out[...] = rank
    for k in range(top_count):
        slot_out[k : k + 1, :] = (
            jnp.sum(jnp.where(matches[k] & kept, slot_ids + 1, 0), axis=0, keepdims=True) - 1
        )
    row_ids = lax.broadcasted_iota(jnp.int32, spread.shape[1:], 0)
    for s in range(slot_count):
        placed = jnp.where(row_ids == rank[s : s + 1, :], gate_of[s : s + 1, :], 0.0)
        spread[seat[0] ^ s] = placed.astype(jnp.bfloat16)


def place_routes(routes, picks, gates, replica_plan, seat, expert_count, cap_rows, held_rows):
    slot_count = replica_plan.shape[0]
    top_count, tokens = routes.shape
    vmem = pl.BlockSpec(memory_space=pltpu.VMEM)
    return pl.pallas_call(
        functools.partial(route_kernel, expert_count, cap_rows),
        out_shape=(
            jax.ShapeDtypeStruct((slot_count, held_rows, tokens), jnp.bfloat16),
            jax.ShapeDtypeStruct((slot_count, tokens), jnp.int32),
            jax.ShapeDtypeStruct((top_count, tokens), jnp.int32),
        ),
        in_specs=[pl.BlockSpec(memory_space=pltpu.SMEM)] * 2 + [vmem] * 4,
        out_specs=(vmem, vmem, vmem),
    )(seat, replica_plan, replica_plan.reshape(1, slot_count), routes, picks, gates)


def send_all_kernel(seat, spread, rows, *rest):
    out = rest[-1]
    held_rows, tokens = spread.shape[1:]
    total = jnp.dot(spread[...].reshape(-1, tokens), rows[...], preferred_element_type=jnp.float32)
    for d in range(spread.shape[0]):
        out[seat[0] ^ d] = total[d * held_rows : (d + 1) * held_rows].astype(jnp.bfloat16)


def all_rows_to_send(spread, out_grad, seat, span, after):
    slot_count, held_rows, tokens = spread.shape
    start, stop = span
    tile = tile_of(stop - start, start)
    return pl.pallas_call(
        send_all_kernel,
        grid=((stop - start) // tile,),
        in_specs=[
            pl.BlockSpec(memory_space=pltpu.SMEM),
            pl.BlockSpec((slot_count, held_rows, tokens), lambda j: (0, 0, 0)),
            pl.BlockSpec((tokens, tile), lambda j: (0, start // tile + j)),
        ]
        + [pl.BlockSpec(memory_space=pl.ANY)] * len(after),
        out_specs=pl.BlockSpec((slot_count, held_rows, tile), lambda j: (0, 0, j)),
        out_shape=jax.ShapeDtypeStruct((slot_count, held_rows, stop - start), jnp.bfloat16),
        cost_estimate=cost(2 * slot_count * held_rows * tokens * (stop - start)),
    )(seat, spread, out_grad, *after)


def part_kernel(leave, rows, *rest):
    flat = rows[...].reshape(-1, rows.shape[-1])
    rest[-1][...] = jnp.dot(leave[...], flat, preferred_element_type=jnp.float32).astype(jnp.bfloat16)


def other_core_part(leave, rows, after):
    slot_count, held_rows, width = rows.shape
    units, held = leave.shape
    tile = tile_of(width)
    return pl.pallas_call(
        part_kernel,
        grid=(width // tile,),
        in_specs=[
            pl.BlockSpec((units, held), lambda j: (0, 0)),
            pl.BlockSpec((slot_count, held_rows, tile), lambda j: (0, 0, j)),
        ]
        + [pl.BlockSpec(memory_space=pl.ANY)] * len(after),
        out_specs=pl.BlockSpec((units, tile), lambda j: (0, j)),
        out_shape=jax.ShapeDtypeStruct((units, width), jnp.bfloat16),
        compiler_params=pltpu.CompilerParams(vmem_limit_bytes=48 * 1024 * 1024),
        cost_estimate=cost(2 * units * held * width),
    )(leave, rows, *after)


def near_kernel(chips, stay, rows, near, *rest):
    mine, *others = rest[-chips:]
    flat = rows[...].reshape(-1, rows.shape[-1])
    shard = mine.shape[0]
    total = jnp.dot(stay[...], flat, preferred_element_type=jnp.float32) + near[...].astype(jnp.float32)
    mine[...] = total[:shard]
    for d, other in enumerate(others):
        other[...] = total[(d + 1) * shard : (d + 2) * shard].astype(jnp.bfloat16)


def add_near(stay, rows, near, chips, after):
    units, held = stay.shape
    width = rows.shape[-1]
    shard = units // chips
    tile = tile_of(width)
    return pl.pallas_call(
        functools.partial(near_kernel, chips),
        grid=(width // tile,),
        in_specs=[
            pl.BlockSpec((units, held), lambda j: (0, 0)),
            pl.BlockSpec(rows.shape[:2] + (tile,), lambda j: (0, 0, j)),
            pl.BlockSpec((units, tile), lambda j: (0, j)),
        ]
        + [pl.BlockSpec(memory_space=pl.ANY)] * len(after),
        out_specs=(pl.BlockSpec((shard, tile), lambda j: (0, j)),) * chips,
        out_shape=(jax.ShapeDtypeStruct((shard, width), jnp.float32),)
        + (jax.ShapeDtypeStruct((shard, width), jnp.bfloat16),) * (chips - 1),
        compiler_params=pltpu.CompilerParams(vmem_limit_bytes=48 * 1024 * 1024),
        cost_estimate=cost(2 * units * held * width),
    )(stay, rows, near, *after)


def last_part(leave, rows, after):
    vmem = pl.BlockSpec(memory_space=pltpu.VMEM)
    return pl.pallas_call(
        part_kernel,
        in_specs=[vmem] * 2 + [pl.BlockSpec(memory_space=pl.ANY)] * len(after),
        out_specs=vmem,
        out_shape=jax.ShapeDtypeStruct((leave.shape[0], rows.shape[-1]), jnp.bfloat16),
        compiler_params=pltpu.CompilerParams(vmem_limit_bytes=32 * 1024 * 1024),
        cost_estimate=cost(2 * leave.size * rows.shape[-1]),
    )(leave, rows, *after)


def last_near(stay, rows, near, chips, after):
    shape = (stay.shape[0] // chips, rows.shape[-1])
    vmem = pl.BlockSpec(memory_space=pltpu.VMEM)
    return pl.pallas_call(
        functools.partial(near_kernel, chips),
        in_specs=[vmem] * 3 + [pl.BlockSpec(memory_space=pl.ANY)] * len(after),
        out_specs=(vmem,) * chips,
        out_shape=(jax.ShapeDtypeStruct(shape, jnp.float32),)
        + (jax.ShapeDtypeStruct(shape, jnp.bfloat16),) * (chips - 1),
        compiler_params=pltpu.CompilerParams(vmem_limit_bytes=32 * 1024 * 1024),
        cost_estimate=cost(2 * stay.size * rows.shape[-1]),
    )(stay, rows, near, *after)


def hold_kernel(*refs):
    pass


def hold(array, after):
    return pl.pallas_call(
        hold_kernel,
        in_specs=[pl.BlockSpec(memory_space=pl.ANY)] * (1 + len(after)),
        out_specs=pl.BlockSpec(memory_space=pl.ANY),
        out_shape=jax.ShapeDtypeStruct(array.shape, array.dtype),
        input_output_aliases={0: 0},
        cost_estimate=cost(1),
    )(array, *after)


def return_kernel(score, rank, slot_of, gates, out):
    slot_count, cap_rows = score.shape
    top_count, tokens = slot_of.shape
    row_ids = lax.broadcasted_iota(jnp.int32, (cap_rows, tokens), 0)
    total = jnp.zeros((top_count, tokens), jnp.float32)
    for s in range(slot_count):
        onehot = jnp.where(row_ids == rank[s : s + 1, :], 1.0, 0.0)
        value = lax.dot_general(
            score[s : s + 1, :],
            onehot,
            (((1,), (0,)), ((), ())),
            precision=lax.Precision.HIGHEST,
            preferred_element_type=jnp.float32,
        )
        total = jnp.where(slot_of[...] == s, value, total)
    held_gate = gates[...].astype(jnp.bfloat16).astype(jnp.float32)
    out[...] = jnp.where(slot_of[...] >= 0, total / held_gate, 0.0)


def matchings(slot_count):
    first = np.zeros((1 << slot_count,), np.int32)
    perms = []
    for four in itertools.combinations(range(slot_count), 4):
        first[sum(1 << s for s in four)] = len(perms)
        for other in range(3):
            rest = [four[1 + i] for i in range(3) if i != other]
            pairs = ((four[0], four[1 + other]), tuple(rest))
            perms.append([(a, b) for a, b in pairs] + [(b, a) for a, b in pairs])
    return first, perms


def matching_index(replica_plan, first):
    slot_ids, same_expert, ordinal = slot_layout(replica_plan)
    hot = jnp.sum(same_expert, axis=1) > 1
    mask = jnp.sum(jnp.where(hot, 1 << slot_ids, 0))
    least = jnp.min(jnp.where(hot, slot_ids, slot_ids.shape[0]))
    expert = jnp.sum(jnp.where(slot_ids == least, replica_plan, 0))
    partner = jnp.max(jnp.where(replica_plan == expert, slot_ids, 0))
    between = jnp.sum(hot & (slot_ids > least) & (slot_ids < partner))
    base = jnp.sum(jnp.where(jnp.arange(first.shape[0]) == mask, jnp.asarray(first), 0))
    return base + between


def sum_copies_any(group_sum, replica_plan):
    slot_ids, same_expert, ordinal = slot_layout(replica_plan)
    copies = jnp.sum(same_expert, axis=1)
    hot_first = (copies > 1) & (ordinal == 0)
    hot_rank = jnp.sum(hot_first[None, :] & (replica_plan[None, :] < replica_plan[:, None]), axis=1)
    my_slot = slot_ids == lax.axis_index("expert")
    my_rank = jnp.sum(jnp.where(my_slot, hot_rank, 0))
    my_hot = jnp.any(my_slot & (copies > 1))
    place_hot = (jnp.arange(HOT, dtype=jnp.int32) == my_rank) & my_hot
    group_f = group_sum.astype(jnp.float32)
    table = jnp.where(place_hot[:, None, None], group_f[None], 0.0)
    summed = lax.psum(table.astype(jnp.bfloat16), "expert").astype(jnp.float32)
    picked = jnp.sum(jnp.where(place_hot[:, None, None], summed, 0.0), axis=0)
    return jnp.where(my_hot, picked, group_f).astype(jnp.bfloat16)


def local(out_grad, gates, routes, copy_pick, replica_plan, down_weight, saved_hidden):
    slot_count = replica_plan.shape[0]
    cap_rows = saved_hidden.shape[3]
    expert_count = slot_count - slot_count // 4
    model_width = out_grad.shape[1]
    hidden_units = down_weight.shape[1]
    group_size = lax.axis_size("group")
    chips = group_size // 2
    shard_rows = hidden_units // group_size
    me = lax.axis_index("group")
    chip, core = me // 2, me % 2

    seat = lax.axis_index("expert").astype(jnp.int32).reshape(1)
    held_rows = -(-cap_rows // 16) * 16
    pad = ((0, 0), (0, held_rows - cap_rows), (0, 0))
    held_hidden = jnp.pad(saved_hidden[0, 0], pad).reshape(slot_count * held_rows, hidden_units)

    spread, rank, slot_of = place_routes(
        routes.T, copy_pick.T, gates.T, replica_plan, seat, expert_count, cap_rows, held_rows
    )

    by_owner = held_hidden.T.reshape(chips, 2, shard_rows, -1)
    by_owner = jnp.stack([by_owner[chip ^ d] for d in range(chips)])
    stay = by_owner[:, core].reshape(hidden_units // 2, -1)
    leave = by_owner[:, 1 - core].reshape(hidden_units // 2, -1)

    edges = np.cumsum((0,) + CHUNKS)
    spans = [(int(a), int(b)) for a, b in zip(edges[:-1], edges[1:])]
    ready = [all_rows_to_send(spread, out_grad, seat, span, []) for span in spans]
    pairs = slot_count - expert_count == HOT
    if pairs:
        first, perms = matchings(slot_count)
        pairing = matching_index(replica_plan, first)
    group_sum, projected = [], jnp.zeros((slot_count * held_rows, hidden_units), jnp.float32)
    far, others = [], []
    early = ready[2:] + ([pairing.reshape(1)] if pairs else [])
    sent = ready[0]
    for at, span in enumerate(spans):
        last = span == spans[-1]
        rows = lax.all_to_all(sent, "expert", split_axis=0, concat_axis=0, tiled=True)
        after = others[:1] + ([projected] if at else [])
        if not last:
            sent = hold(ready[at + 1], [rows] + early)
            after = after + [sent]
        away = (last_part if last else other_core_part)(leave, rows, after)
        near = lax.ppermute(away, "group", [(i, i ^ 1) for i in range(group_size)])
        mine, *others = (last_near if last else add_near)(stay, rows, near, chips, far[:1])
        far = [
            lax.ppermute(other, "group", [(i, i ^ (2 * d + 2)) for i in range(group_size)])
            for d, other in enumerate(others)
        ]
        group_sum.append(sum((f.astype(jnp.float32) for f in far), mine).astype(jnp.bfloat16))
        projected = projected + lax.dot_general(
            rows.reshape(slot_count * held_rows, -1),
            down_weight[0, :, span[0] : span[1]],
            (((1,), (1,)), ((), ())),
            preferred_element_type=jnp.float32,
        )
        early = far[:1] + [projected]

    route_score = jnp.sum(projected * held_hidden.astype(jnp.float32), axis=1)
    returned = lax.all_to_all(
        hold(route_score.reshape(slot_count, held_rows), others[:1]),
        "expert",
        split_axis=0,
        concat_axis=0,
        tiled=True,
    )
    route_grad = pl.pallas_call(
        return_kernel, out_shape=jax.ShapeDtypeStruct(gates.T.shape, jnp.float32)
    )(returned, rank, slot_of, gates.T).T
    hidden_grad = projected.astype(jnp.bfloat16).reshape(slot_count, held_rows, hidden_units)[:, :cap_rows]

    group_sum = jnp.concatenate(group_sum, axis=1)
    if pairs:
        other = lax.switch(
            pairing,
            [functools.partial(lax.ppermute, axis_name="expert", perm=perm) for perm in perms],
            group_sum,
        )
        copy_grad = (group_sum.astype(jnp.float32) + other.astype(jnp.float32)).astype(jnp.bfloat16)
    else:
        copy_grad = sum_copies_any(group_sum, replica_plan)
    return (route_grad, hidden_grad[None, None], copy_grad.reshape(1, shard_rows, model_width))


def solution(mesh):
    placed = (
        P(("group", "expert"), None),
        P(("group", "expert"), None),
        P(("group", "expert"), None),
        P(("group", "expert"), None),
        P(),
        P("expert", None, None),
        P("group", "expert", None, None, None),
    )
    return jax.shard_map(
        local,
        mesh=mesh,
        in_specs=placed,
        out_specs=(
            P(("group", "expert"), None),
            P("group", "expert", None, None, None),
            P("expert", "group", None),
        ),
        check_vma=False,
    )
```

```python
import functools
import itertools

import jax
import jax.numpy as jnp
import numpy as np
from jax import lax
from jax.experimental import pallas as pl
from jax.experimental.pallas import tpu as pltpu
from jax.sharding import PartitionSpec as P

HOT = 2
TILE = 512


def cost(flops):
    return pl.CostEstimate(flops=flops, bytes_accessed=flops // 300, transcendentals=0)
CHUNKS = (2048, 1024, 512)


def slot_layout(replica_plan):
    slot_count = replica_plan.shape[0]
    slot_ids = jnp.arange(slot_count, dtype=jnp.int32)
    same_expert = replica_plan[:, None] == replica_plan[None, :]
    earlier_slot = slot_ids[None, :] < slot_ids[:, None]
    ordinal = jnp.sum(same_expert & earlier_slot, axis=1)
    return (slot_ids, same_expert, ordinal)


def route_kernel(
    expert_count, cap_rows, seat, slot_plan, plan_row, routes, picks, gates, spread, rank_out, slot_out
):
    slot_count = plan_row.shape[1]
    top_count, tokens = routes.shape
    column = lax.broadcasted_iota(jnp.int32, (slot_count, 1), 0)
    plan = jnp.zeros((slot_count, 1), jnp.int32)
    for s in range(slot_count):
        plan = jnp.where(column == s, slot_plan[s], plan)
    same = plan == plan_row[...]
    slot_r = lax.broadcasted_iota(jnp.int32, (slot_count, slot_count), 0)
    slot_c = lax.broadcasted_iota(jnp.int32, (slot_count, slot_count), 1)
    copies = jnp.sum(jnp.where(same, 1.0, 0.0), axis=1, keepdims=True)
    ordinal = jnp.sum(jnp.where(same & (slot_c < slot_r), 1.0, 0.0), axis=1, keepdims=True)
    slot_ids = lax.broadcasted_iota(jnp.int32, (slot_count, tokens), 0)
    reach = jnp.zeros((slot_count, tokens), jnp.float32)
    gate_of = jnp.zeros((slot_count, tokens), jnp.float32)
    matches = []
    for k in range(top_count):
        route = routes[k : k + 1, :]
        pick = picks[k : k + 1, :].astype(jnp.float32)
        chosen = pick - copies * jnp.floor((pick + 0.5) / copies)
        match = (route == plan) & (chosen == ordinal) & (route < expert_count)
        matches.append(match)
        reach = jnp.where(match, 1.0, reach)
        gate_of = jnp.where(match, gates[k : k + 1, :], gate_of)
    before = lax.broadcasted_iota(jnp.int32, (tokens, tokens), 0) < lax.broadcasted_iota(
        jnp.int32, (tokens, tokens), 1
    )
    rank = lax.dot_general(
        reach.astype(jnp.bfloat16),
        jnp.where(before, 1.0, 0.0).astype(jnp.bfloat16),
        (((1,), (0,)), ((), ())),
        preferred_element_type=jnp.float32,
    ).astype(jnp.int32)
    kept = (reach > 0.0) & (rank < cap_rows)
    rank = jnp.where(kept, rank, -1)
    rank_out[...] = rank
    for k in range(top_count):
        slot_out[k : k + 1, :] = (
            jnp.sum(jnp.where(matches[k] & kept, slot_ids + 1, 0), axis=0, keepdims=True) - 1
        )
    row_ids = lax.broadcasted_iota(jnp.int32, spread.shape[1:], 0)
    for s in range(slot_count):
        placed = jnp.where(row_ids == rank[s : s + 1, :], gate_of[s : s + 1, :], 0.0)
        spread[seat[0] ^ s] = placed.astype(jnp.bfloat16)


def place_routes(routes, picks, gates, replica_plan, seat, expert_count, cap_rows, held_rows):
    slot_count = replica_plan.shape[0]
    top_count, tokens = routes.shape
    vmem = pl.BlockSpec(memory_space=pltpu.VMEM)
    return pl.pallas_call(
        functools.partial(route_kernel, expert_count, cap_rows),
        out_shape=(
            jax.ShapeDtypeStruct((slot_count, held_rows, tokens), jnp.bfloat16),
            jax.ShapeDtypeStruct((slot_count, tokens), jnp.int32),
            jax.ShapeDtypeStruct((top_count, tokens), jnp.int32),
        ),
        in_specs=[pl.BlockSpec(memory_space=pltpu.SMEM)] * 2 + [vmem] * 4,
        out_specs=(vmem, vmem, vmem),
    )(seat, replica_plan, replica_plan.reshape(1, slot_count), routes, picks, gates)


def send_all_kernel(seat, spread, rows, *rest):
    out = rest[-1]
    held_rows, tokens = spread.shape[1:]
    total = jnp.dot(spread[...].reshape(-1, tokens), rows[...], preferred_element_type=jnp.float32)
    for d in range(spread.shape[0]):
        out[seat[0] ^ d] = total[d * held_rows : (d + 1) * held_rows].astype(jnp.bfloat16)


def all_rows_to_send(spread, out_grad, seat, span, after):
    slot_count, held_rows, tokens = spread.shape
    start, stop = span
    return pl.pallas_call(
        send_all_kernel,
        grid=((stop - start) // TILE,),
        in_specs=[
            pl.BlockSpec(memory_space=pltpu.SMEM),
            pl.BlockSpec((slot_count, held_rows, tokens), lambda j: (0, 0, 0)),
            pl.BlockSpec((tokens, TILE), lambda j: (0, start // TILE + j)),
        ]
        + [pl.BlockSpec(memory_space=pl.ANY)] * len(after),
        out_specs=pl.BlockSpec((slot_count, held_rows, TILE), lambda j: (0, 0, j)),
        out_shape=jax.ShapeDtypeStruct((slot_count, held_rows, stop - start), jnp.bfloat16),
        cost_estimate=cost(2 * slot_count * held_rows * tokens * (stop - start)),
    )(seat, spread, out_grad, *after)


def part_kernel(leave, rows, *rest):
    flat = rows[...].reshape(-1, rows.shape[-1])
    rest[-1][...] = jnp.dot(leave[...], flat, preferred_element_type=jnp.float32).astype(jnp.bfloat16)


def other_core_part(leave, rows, after):
    slot_count, held_rows, width = rows.shape
    units, held = leave.shape
    return pl.pallas_call(
        part_kernel,
        grid=(width // TILE,),
        in_specs=[
            pl.BlockSpec((units, held), lambda j: (0, 0)),
            pl.BlockSpec((slot_count, held_rows, TILE), lambda j: (0, 0, j)),
        ]
        + [pl.BlockSpec(memory_space=pl.ANY)] * len(after),
        out_specs=pl.BlockSpec((units, TILE), lambda j: (0, j)),
        out_shape=jax.ShapeDtypeStruct((units, width), jnp.bfloat16),
        cost_estimate=cost(2 * units * held * width),
    )(leave, rows, *after)


def near_kernel(chips, stay, rows, near, *rest):
    mine, *others = rest[-chips:]
    flat = rows[...].reshape(-1, rows.shape[-1])
    shard = mine.shape[0]
    total = jnp.dot(stay[...], flat, preferred_element_type=jnp.float32) + near[...].astype(jnp.float32)
    mine[...] = total[:shard]
    for d, other in enumerate(others):
        other[...] = total[(d + 1) * shard : (d + 2) * shard].astype(jnp.bfloat16)


def add_near(stay, rows, near, chips, after):
    units, held = stay.shape
    width = rows.shape[-1]
    shard = units // chips
    return pl.pallas_call(
        functools.partial(near_kernel, chips),
        grid=(width // TILE,),
        in_specs=[
            pl.BlockSpec((units, held), lambda j: (0, 0)),
            pl.BlockSpec(rows.shape[:2] + (TILE,), lambda j: (0, 0, j)),
            pl.BlockSpec((units, TILE), lambda j: (0, j)),
        ]
        + [pl.BlockSpec(memory_space=pl.ANY)] * len(after),
        out_specs=(pl.BlockSpec((shard, TILE), lambda j: (0, j)),) * chips,
        out_shape=(jax.ShapeDtypeStruct((shard, width), jnp.float32),)
        + (jax.ShapeDtypeStruct((shard, width), jnp.bfloat16),) * (chips - 1),
        cost_estimate=cost(2 * units * held * width),
    )(stay, rows, near, *after)


def few_part(leave, rows, after):
    vmem = pl.BlockSpec(memory_space=pltpu.VMEM)
    return pl.pallas_call(
        part_kernel,
        in_specs=[vmem] * 2 + [pl.BlockSpec(memory_space=pl.ANY)] * len(after),
        out_specs=vmem,
        out_shape=jax.ShapeDtypeStruct((leave.shape[0], rows.shape[-1]), jnp.bfloat16),
        compiler_params=pltpu.CompilerParams(vmem_limit_bytes=32 * 1024 * 1024),
        cost_estimate=cost(2 * leave.size * rows.shape[-1]),
    )(leave, rows, *after)


def few_near(stay, rows, near, chips, after):
    shape = (stay.shape[0] // chips, rows.shape[-1])
    vmem = pl.BlockSpec(memory_space=pltpu.VMEM)
    return pl.pallas_call(
        functools.partial(near_kernel, chips),
        in_specs=[vmem] * 3 + [pl.BlockSpec(memory_space=pl.ANY)] * len(after),
        out_specs=(vmem,) * chips,
        out_shape=(jax.ShapeDtypeStruct(shape, jnp.float32),)
        + (jax.ShapeDtypeStruct(shape, jnp.bfloat16),) * (chips - 1),
        compiler_params=pltpu.CompilerParams(vmem_limit_bytes=32 * 1024 * 1024),
        cost_estimate=cost(2 * stay.size * rows.shape[-1]),
    )(stay, rows, near, *after)


def hold_kernel(*refs):
    pass


def hold(array, after):
    return pl.pallas_call(
        hold_kernel,
        in_specs=[pl.BlockSpec(memory_space=pl.ANY)] * (1 + len(after)),
        out_specs=pl.BlockSpec(memory_space=pl.ANY),
        out_shape=jax.ShapeDtypeStruct(array.shape, array.dtype),
        input_output_aliases={0: 0},
        cost_estimate=cost(1),
    )(array, *after)


def return_kernel(score, rank, slot_of, gates, out):
    slot_count, cap_rows = score.shape
    top_count, tokens = slot_of.shape
    row_ids = lax.broadcasted_iota(jnp.int32, (cap_rows, tokens), 0)
    total = jnp.zeros((top_count, tokens), jnp.float32)
    for s in range(slot_count):
        onehot = jnp.where(row_ids == rank[s : s + 1, :], 1.0, 0.0)
        value = lax.dot_general(
            score[s : s + 1, :],
            onehot,
            (((1,), (0,)), ((), ())),
            precision=lax.Precision.HIGHEST,
            preferred_element_type=jnp.float32,
        )
        total = jnp.where(slot_of[...] == s, value, total)
    held_gate = gates[...].astype(jnp.bfloat16).astype(jnp.float32)
    out[...] = jnp.where(slot_of[...] >= 0, total / held_gate, 0.0)


def matchings(slot_count):
    first = np.zeros((1 << slot_count,), np.int32)
    perms = []
    for four in itertools.combinations(range(slot_count), 4):
        first[sum(1 << s for s in four)] = len(perms)
        for other in range(3):
            rest = [four[1 + i] for i in range(3) if i != other]
            pairs = ((four[0], four[1 + other]), tuple(rest))
            perms.append([(a, b) for a, b in pairs] + [(b, a) for a, b in pairs])
    return first, perms


def matching_index(replica_plan, first):
    slot_ids, same_expert, ordinal = slot_layout(replica_plan)
    hot = jnp.sum(same_expert, axis=1) > 1
    mask = jnp.sum(jnp.where(hot, 1 << slot_ids, 0))
    least = jnp.min(jnp.where(hot, slot_ids, slot_ids.shape[0]))
    expert = jnp.sum(jnp.where(slot_ids == least, replica_plan, 0))
    partner = jnp.max(jnp.where(replica_plan == expert, slot_ids, 0))
    between = jnp.sum(hot & (slot_ids > least) & (slot_ids < partner))
    base = jnp.sum(jnp.where(jnp.arange(first.shape[0]) == mask, jnp.asarray(first), 0))
    return base + between


def sum_copies_any(group_sum, replica_plan):
    slot_ids, same_expert, ordinal = slot_layout(replica_plan)
    copies = jnp.sum(same_expert, axis=1)
    hot_first = (copies > 1) & (ordinal == 0)
    hot_rank = jnp.sum(hot_first[None, :] & (replica_plan[None, :] < replica_plan[:, None]), axis=1)
    my_slot = slot_ids == lax.axis_index("expert")
    my_rank = jnp.sum(jnp.where(my_slot, hot_rank, 0))
    my_hot = jnp.any(my_slot & (copies > 1))
    place_hot = (jnp.arange(HOT, dtype=jnp.int32) == my_rank) & my_hot
    group_f = group_sum.astype(jnp.float32)
    table = jnp.where(place_hot[:, None, None], group_f[None], 0.0)
    summed = lax.psum(table.astype(jnp.bfloat16), "expert").astype(jnp.float32)
    picked = jnp.sum(jnp.where(place_hot[:, None, None], summed, 0.0), axis=0)
    return jnp.where(my_hot, picked, group_f).astype(jnp.bfloat16)


def local(out_grad, gates, routes, copy_pick, replica_plan, down_weight, saved_hidden):
    slot_count = replica_plan.shape[0]
    cap_rows = saved_hidden.shape[3]
    expert_count = slot_count - slot_count // 4
    model_width = out_grad.shape[1]
    hidden_units = down_weight.shape[1]
    group_size = lax.axis_size("group")
    chips = group_size // 2
    shard_rows = hidden_units // group_size
    me = lax.axis_index("group")
    chip, core = me // 2, me % 2

    seat = lax.axis_index("expert").astype(jnp.int32).reshape(1)
    held_rows = -(-cap_rows // 16) * 16
    pad = ((0, 0), (0, held_rows - cap_rows), (0, 0))
    held_hidden = jnp.pad(saved_hidden[0, 0], pad).reshape(slot_count * held_rows, hidden_units)

    spread, rank, slot_of = place_routes(
        routes.T, copy_pick.T, gates.T, replica_plan, seat, expert_count, cap_rows, held_rows
    )

    by_owner = held_hidden.T.reshape(chips, 2, shard_rows, -1)
    by_owner = jnp.stack([by_owner[chip ^ d] for d in range(chips)])
    stay = by_owner[:, core].reshape(hidden_units // 2, -1)
    leave = by_owner[:, 1 - core].reshape(hidden_units // 2, -1)

    edges = np.cumsum((0,) + CHUNKS)
    spans = [(int(a), int(b)) for a, b in zip(edges[:-1], edges[1:])]
    ready = [all_rows_to_send(spread, out_grad, seat, span, []) for span in spans]
    pairs = slot_count - expert_count == HOT
    if pairs:
        first, perms = matchings(slot_count)
        pairing = matching_index(replica_plan, first)
    group_sum, projected = [], jnp.zeros((slot_count * held_rows, hidden_units), jnp.float32)
    rows, far, others = None, [], []
    early = ready[2:] + ([pairing.reshape(1)] if pairs else [])
    for span, sent in zip(spans, ready):
        if rows is not None:
            sent = hold(sent, [rows] + early)
            early = others[:1] + [projected]
        rows = lax.all_to_all(sent, "expert", split_axis=0, concat_axis=0, tiled=True)
        few = span != spans[0]
        away = (few_part if few else other_core_part)(leave, rows, others[:1])
        near = lax.ppermute(away, "group", [(i, i ^ 1) for i in range(group_size)])
        mine, *others = (few_near if few else add_near)(stay, rows, near, chips, far[:1])
        far = [
            lax.ppermute(other, "group", [(i, i ^ (2 * d + 2)) for i in range(group_size)])
            for d, other in enumerate(others)
        ]
        group_sum.append(sum((f.astype(jnp.float32) for f in far), mine).astype(jnp.bfloat16))
        projected = projected + lax.dot_general(
            rows.reshape(slot_count * held_rows, -1),
            down_weight[0, :, span[0] : span[1]],
            (((1,), (1,)), ((), ())),
            preferred_element_type=jnp.float32,
        )

    route_score = jnp.sum(projected * held_hidden.astype(jnp.float32), axis=1)
    returned = lax.all_to_all(
        hold(route_score.reshape(slot_count, held_rows), others[:1]),
        "expert",
        split_axis=0,
        concat_axis=0,
        tiled=True,
    )
    route_grad = pl.pallas_call(
        return_kernel, out_shape=jax.ShapeDtypeStruct(gates.T.shape, jnp.float32)
    )(returned, rank, slot_of, gates.T).T
    hidden_grad = projected.astype(jnp.bfloat16).reshape(slot_count, held_rows, hidden_units)[:, :cap_rows]

    group_sum = jnp.concatenate(group_sum, axis=1)
    if pairs:
        other = lax.switch(
            pairing,
            [functools.partial(lax.ppermute, axis_name="expert", perm=perm) for perm in perms],
            group_sum,
        )
        copy_grad = (group_sum.astype(jnp.float32) + other.astype(jnp.float32)).astype(jnp.bfloat16)
    else:
        copy_grad = sum_copies_any(group_sum, replica_plan)
    return (route_grad, hidden_grad[None, None], copy_grad.reshape(1, shard_rows, model_width))


def solution(mesh):
    placed = (
        P(("group", "expert"), None),
        P(("group", "expert"), None),
        P(("group", "expert"), None),
        P(("group", "expert"), None),
        P(),
        P("expert", None, None),
        P("group", "expert", None, None, None),
    )
    return jax.shard_map(
        local,
        mesh=mesh,
        in_specs=placed,
        out_specs=(
            P(("group", "expert"), None),
            P("group", "expert", None, None, None),
            P("expert", "group", None),
        ),
        check_vma=False,
    )
```

```python
import functools
import itertools

import jax
import jax.numpy as jnp
import numpy as np
from jax import lax
from jax.experimental import pallas as pl
from jax.experimental.pallas import tpu as pltpu
from jax.sharding import PartitionSpec as P

HOT = 2
TILE = 512


def cost(flops):
    return pl.CostEstimate(flops=flops, bytes_accessed=flops // 300, transcendentals=0)
CHUNKS = (2048, 1024, 512)


def slot_layout(replica_plan):
    slot_count = replica_plan.shape[0]
    slot_ids = jnp.arange(slot_count, dtype=jnp.int32)
    same_expert = replica_plan[:, None] == replica_plan[None, :]
    earlier_slot = slot_ids[None, :] < slot_ids[:, None]
    ordinal = jnp.sum(same_expert & earlier_slot, axis=1)
    return (slot_ids, same_expert, ordinal)


def route_kernel(
    expert_count, cap_rows, seat, slot_plan, plan_row, routes, picks, gates, spread, rank_out, slot_out
):
    slot_count = plan_row.shape[1]
    top_count, tokens = routes.shape
    column = lax.broadcasted_iota(jnp.int32, (slot_count, 1), 0)
    plan = jnp.zeros((slot_count, 1), jnp.int32)
    for s in range(slot_count):
        plan = jnp.where(column == s, slot_plan[s], plan)
    same = plan == plan_row[...]
    slot_r = lax.broadcasted_iota(jnp.int32, (slot_count, slot_count), 0)
    slot_c = lax.broadcasted_iota(jnp.int32, (slot_count, slot_count), 1)
    copies = jnp.sum(jnp.where(same, 1.0, 0.0), axis=1, keepdims=True)
    ordinal = jnp.sum(jnp.where(same & (slot_c < slot_r), 1.0, 0.0), axis=1, keepdims=True)
    slot_ids = lax.broadcasted_iota(jnp.int32, (slot_count, tokens), 0)
    reach = jnp.zeros((slot_count, tokens), jnp.float32)
    gate_of = jnp.zeros((slot_count, tokens), jnp.float32)
    matches = []
    for k in range(top_count):
        route = routes[k : k + 1, :]
        pick = picks[k : k + 1, :].astype(jnp.float32)
        chosen = pick - copies * jnp.floor((pick + 0.5) / copies)
        match = (route == plan) & (chosen == ordinal) & (route < expert_count)
        matches.append(match)
        reach = jnp.where(match, 1.0, reach)
        gate_of = jnp.where(match, gates[k : k + 1, :], gate_of)
    before = lax.broadcasted_iota(jnp.int32, (tokens, tokens), 0) < lax.broadcasted_iota(
        jnp.int32, (tokens, tokens), 1
    )
    rank = lax.dot_general(
        reach.astype(jnp.bfloat16),
        jnp.where(before, 1.0, 0.0).astype(jnp.bfloat16),
        (((1,), (0,)), ((), ())),
        preferred_element_type=jnp.float32,
    ).astype(jnp.int32)
    kept = (reach > 0.0) & (rank < cap_rows)
    rank = jnp.where(kept, rank, -1)
    rank_out[...] = rank
    for k in range(top_count):
        slot_out[k : k + 1, :] = (
            jnp.sum(jnp.where(matches[k] & kept, slot_ids + 1, 0), axis=0, keepdims=True) - 1
        )
    row_ids = lax.broadcasted_iota(jnp.int32, spread.shape[1:], 0)
    for s in range(slot_count):
        placed = jnp.where(row_ids == rank[s : s + 1, :], gate_of[s : s + 1, :], 0.0)
        spread[seat[0] ^ s] = placed.astype(jnp.bfloat16)


def place_routes(routes, picks, gates, replica_plan, seat, expert_count, cap_rows, held_rows):
    slot_count = replica_plan.shape[0]
    top_count, tokens = routes.shape
    vmem = pl.BlockSpec(memory_space=pltpu.VMEM)
    return pl.pallas_call(
        functools.partial(route_kernel, expert_count, cap_rows),
        out_shape=(
            jax.ShapeDtypeStruct((slot_count, held_rows, tokens), jnp.bfloat16),
            jax.ShapeDtypeStruct((slot_count, tokens), jnp.int32),
            jax.ShapeDtypeStruct((top_count, tokens), jnp.int32),
        ),
        in_specs=[pl.BlockSpec(memory_space=pltpu.SMEM)] * 2 + [vmem] * 4,
        out_specs=(vmem, vmem, vmem),
    )(seat, replica_plan, replica_plan.reshape(1, slot_count), routes, picks, gates)


def send_all_kernel(seat, spread, rows, *rest):
    out = rest[-1]
    held_rows, tokens = spread.shape[1:]
    total = jnp.dot(spread[...].reshape(-1, tokens), rows[...], preferred_element_type=jnp.float32)
    for d in range(spread.shape[0]):
        out[seat[0] ^ d] = total[d * held_rows : (d + 1) * held_rows].astype(jnp.bfloat16)


def all_rows_to_send(spread, out_grad, seat, span, after):
    slot_count, held_rows, tokens = spread.shape
    start, stop = span
    return pl.pallas_call(
        send_all_kernel,
        grid=((stop - start) // TILE,),
        in_specs=[
            pl.BlockSpec(memory_space=pltpu.SMEM),
            pl.BlockSpec((slot_count, held_rows, tokens), lambda j: (0, 0, 0)),
            pl.BlockSpec((tokens, TILE), lambda j: (0, start // TILE + j)),
        ]
        + [pl.BlockSpec(memory_space=pl.ANY)] * len(after),
        out_specs=pl.BlockSpec((slot_count, held_rows, TILE), lambda j: (0, 0, j)),
        out_shape=jax.ShapeDtypeStruct((slot_count, held_rows, stop - start), jnp.bfloat16),
        cost_estimate=cost(2 * slot_count * held_rows * tokens * (stop - start)),
    )(seat, spread, out_grad, *after)


def part_kernel(leave, rows, *rest):
    flat = rows[...].reshape(-1, rows.shape[-1])
    rest[-1][...] = jnp.dot(leave[...], flat, preferred_element_type=jnp.float32).astype(jnp.bfloat16)


def other_core_part(leave, rows, after):
    slot_count, held_rows, width = rows.shape
    units, held = leave.shape
    return pl.pallas_call(
        part_kernel,
        grid=(width // TILE,),
        in_specs=[
            pl.BlockSpec((units, held), lambda j: (0, 0)),
            pl.BlockSpec((slot_count, held_rows, TILE), lambda j: (0, 0, j)),
        ]
        + [pl.BlockSpec(memory_space=pl.ANY)] * len(after),
        out_specs=pl.BlockSpec((units, TILE), lambda j: (0, j)),
        out_shape=jax.ShapeDtypeStruct((units, width), jnp.bfloat16),
        cost_estimate=cost(2 * units * held * width),
    )(leave, rows, *after)


def near_kernel(chips, stay, rows, near, *rest):
    mine, *others = rest[-chips:]
    flat = rows[...].reshape(-1, rows.shape[-1])
    shard = mine.shape[0]
    total = jnp.dot(stay[...], flat, preferred_element_type=jnp.float32) + near[...].astype(jnp.float32)
    mine[...] = total[:shard]
    for d, other in enumerate(others):
        other[...] = total[(d + 1) * shard : (d + 2) * shard].astype(jnp.bfloat16)


def add_near(stay, rows, near, chips, after):
    units, held = stay.shape
    width = rows.shape[-1]
    shard = units // chips
    return pl.pallas_call(
        functools.partial(near_kernel, chips),
        grid=(width // TILE,),
        in_specs=[
            pl.BlockSpec((units, held), lambda j: (0, 0)),
            pl.BlockSpec(rows.shape[:2] + (TILE,), lambda j: (0, 0, j)),
            pl.BlockSpec((units, TILE), lambda j: (0, j)),
        ]
        + [pl.BlockSpec(memory_space=pl.ANY)] * len(after),
        out_specs=(pl.BlockSpec((shard, TILE), lambda j: (0, j)),) * chips,
        out_shape=(jax.ShapeDtypeStruct((shard, width), jnp.float32),)
        + (jax.ShapeDtypeStruct((shard, width), jnp.bfloat16),) * (chips - 1),
        cost_estimate=cost(2 * units * held * width),
    )(stay, rows, near, *after)


def few_part(leave, rows, after):
    vmem = pl.BlockSpec(memory_space=pltpu.VMEM)
    return pl.pallas_call(
        part_kernel,
        in_specs=[vmem] * 2 + [pl.BlockSpec(memory_space=pl.ANY)] * len(after),
        out_specs=vmem,
        out_shape=jax.ShapeDtypeStruct((leave.shape[0], rows.shape[-1]), jnp.bfloat16),
        compiler_params=pltpu.CompilerParams(vmem_limit_bytes=32 * 1024 * 1024),
        cost_estimate=cost(2 * leave.size * rows.shape[-1]),
    )(leave, rows, *after)


def few_near(stay, rows, near, chips, after):
    shape = (stay.shape[0] // chips, rows.shape[-1])
    vmem = pl.BlockSpec(memory_space=pltpu.VMEM)
    return pl.pallas_call(
        functools.partial(near_kernel, chips),
        in_specs=[vmem] * 3 + [pl.BlockSpec(memory_space=pl.ANY)] * len(after),
        out_specs=(vmem,) * chips,
        out_shape=(jax.ShapeDtypeStruct(shape, jnp.float32),)
        + (jax.ShapeDtypeStruct(shape, jnp.bfloat16),) * (chips - 1),
        compiler_params=pltpu.CompilerParams(vmem_limit_bytes=32 * 1024 * 1024),
        cost_estimate=cost(2 * stay.size * rows.shape[-1]),
    )(stay, rows, near, *after)


def hold_kernel(*refs):
    pass


def hold(array, after):
    return pl.pallas_call(
        hold_kernel,
        in_specs=[pl.BlockSpec(memory_space=pl.ANY)] * (1 + len(after)),
        out_specs=pl.BlockSpec(memory_space=pl.ANY),
        out_shape=jax.ShapeDtypeStruct(array.shape, array.dtype),
        input_output_aliases={0: 0},
        cost_estimate=cost(1),
    )(array, *after)


def return_kernel(score, rank, slot_of, gates, out):
    slot_count, cap_rows = score.shape
    top_count, tokens = slot_of.shape
    row_ids = lax.broadcasted_iota(jnp.int32, (cap_rows, tokens), 0)
    total = jnp.zeros((top_count, tokens), jnp.float32)
    for s in range(slot_count):
        onehot = jnp.where(row_ids == rank[s : s + 1, :], 1.0, 0.0)
        value = lax.dot_general(
            score[s : s + 1, :],
            onehot,
            (((1,), (0,)), ((), ())),
            precision=lax.Precision.HIGHEST,
            preferred_element_type=jnp.float32,
        )
        total = jnp.where(slot_of[...] == s, value, total)
    held_gate = gates[...].astype(jnp.bfloat16).astype(jnp.float32)
    out[...] = jnp.where(slot_of[...] >= 0, total / held_gate, 0.0)


def matchings(slot_count):
    first = np.zeros((1 << slot_count,), np.int32)
    perms = []
    for four in itertools.combinations(range(slot_count), 4):
        first[sum(1 << s for s in four)] = len(perms)
        for other in range(3):
            rest = [four[1 + i] for i in range(3) if i != other]
            pairs = ((four[0], four[1 + other]), tuple(rest))
            perms.append([(a, b) for a, b in pairs] + [(b, a) for a, b in pairs])
    return first, perms


def matching_index(replica_plan, first):
    slot_ids, same_expert, ordinal = slot_layout(replica_plan)
    hot = jnp.sum(same_expert, axis=1) > 1
    mask = jnp.sum(jnp.where(hot, 1 << slot_ids, 0))
    least = jnp.min(jnp.where(hot, slot_ids, slot_ids.shape[0]))
    expert = jnp.sum(jnp.where(slot_ids == least, replica_plan, 0))
    partner = jnp.max(jnp.where(replica_plan == expert, slot_ids, 0))
    between = jnp.sum(hot & (slot_ids > least) & (slot_ids < partner))
    base = jnp.sum(jnp.where(jnp.arange(first.shape[0]) == mask, jnp.asarray(first), 0))
    return base + between


def sum_copies_any(group_sum, replica_plan):
    slot_ids, same_expert, ordinal = slot_layout(replica_plan)
    copies = jnp.sum(same_expert, axis=1)
    hot_first = (copies > 1) & (ordinal == 0)
    hot_rank = jnp.sum(hot_first[None, :] & (replica_plan[None, :] < replica_plan[:, None]), axis=1)
    my_slot = slot_ids == lax.axis_index("expert")
    my_rank = jnp.sum(jnp.where(my_slot, hot_rank, 0))
    my_hot = jnp.any(my_slot & (copies > 1))
    place_hot = (jnp.arange(HOT, dtype=jnp.int32) == my_rank) & my_hot
    group_f = group_sum.astype(jnp.float32)
    table = jnp.where(place_hot[:, None, None], group_f[None], 0.0)
    summed = lax.psum(table.astype(jnp.bfloat16), "expert").astype(jnp.float32)
    picked = jnp.sum(jnp.where(place_hot[:, None, None], summed, 0.0), axis=0)
    return jnp.where(my_hot, picked, group_f).astype(jnp.bfloat16)


def local(out_grad, gates, routes, copy_pick, replica_plan, down_weight, saved_hidden):
    slot_count = replica_plan.shape[0]
    cap_rows = saved_hidden.shape[3]
    expert_count = slot_count - slot_count // 4
    model_width = out_grad.shape[1]
    hidden_units = down_weight.shape[1]
    group_size = lax.axis_size("group")
    chips = group_size // 2
    shard_rows = hidden_units // group_size
    me = lax.axis_index("group")
    chip, core = me // 2, me % 2

    seat = lax.axis_index("expert").astype(jnp.int32).reshape(1)
    held_rows = -(-cap_rows // 16) * 16
    pad = ((0, 0), (0, held_rows - cap_rows), (0, 0))
    held_hidden = jnp.pad(saved_hidden[0, 0], pad).reshape(slot_count * held_rows, hidden_units)

    spread, rank, slot_of = place_routes(
        routes.T, copy_pick.T, gates.T, replica_plan, seat, expert_count, cap_rows, held_rows
    )

    by_owner = held_hidden.T.reshape(chips, 2, shard_rows, -1)
    by_owner = jnp.stack([by_owner[chip ^ d] for d in range(chips)])
    stay = by_owner[:, core].reshape(hidden_units // 2, -1)
    leave = by_owner[:, 1 - core].reshape(hidden_units // 2, -1)

    edges = np.cumsum((0,) + CHUNKS)
    spans = [(int(a), int(b)) for a, b in zip(edges[:-1], edges[1:])]
    ready = [all_rows_to_send(spread, out_grad, seat, span, []) for span in spans]
    pairs = slot_count - expert_count == HOT
    if pairs:
        first, perms = matchings(slot_count)
        pairing = matching_index(replica_plan, first)
    group_sum, projected = [], jnp.zeros((slot_count * held_rows, hidden_units), jnp.float32)
    rows, far, others = None, [], []
    early = ready[2:] + ([pairing.reshape(1)] if pairs else [])
    for span, sent in zip(spans, ready):
        if rows is not None:
            sent = hold(sent, [rows] + early)
            early = others[:1] + [projected]
        rows = lax.all_to_all(sent, "expert", split_axis=0, concat_axis=0, tiled=True)
        few = span != spans[0]
        away = (few_part if few else other_core_part)(leave, rows, others[:1])
        near = lax.ppermute(away, "group", [(i, i ^ 1) for i in range(group_size)])
        mine, *others = (few_near if few else add_near)(stay, rows, near, chips, far[:1])
        far = [
            lax.ppermute(other, "group", [(i, i ^ (2 * d + 2)) for i in range(group_size)])
            for d, other in enumerate(others)
        ]
        group_sum.append(sum((f.astype(jnp.float32) for f in far), mine).astype(jnp.bfloat16))
        projected = projected + lax.dot_general(
            rows.reshape(slot_count * held_rows, -1),
            down_weight[0, :, span[0] : span[1]],
            (((1,), (1,)), ((), ())),
            preferred_element_type=jnp.float32,
        )

    route_score = jnp.sum(projected * held_hidden.astype(jnp.float32), axis=1)
    returned = lax.all_to_all(
        route_score.reshape(slot_count, held_rows),
        "expert",
        split_axis=0,
        concat_axis=0,
        tiled=True,
    )
    route_grad = pl.pallas_call(
        return_kernel, out_shape=jax.ShapeDtypeStruct(gates.T.shape, jnp.float32)
    )(returned, rank, slot_of, gates.T).T
    hidden_grad = projected.astype(jnp.bfloat16).reshape(slot_count, held_rows, hidden_units)[:, :cap_rows]

    group_sum = jnp.concatenate(group_sum, axis=1)
    if pairs:
        other = lax.switch(
            pairing,
            [functools.partial(lax.ppermute, axis_name="expert", perm=perm) for perm in perms],
            group_sum,
        )
        copy_grad = (group_sum.astype(jnp.float32) + other.astype(jnp.float32)).astype(jnp.bfloat16)
    else:
        copy_grad = sum_copies_any(group_sum, replica_plan)
    return (route_grad, hidden_grad[None, None], copy_grad.reshape(1, shard_rows, model_width))


def solution(mesh):
    placed = (
        P(("group", "expert"), None),
        P(("group", "expert"), None),
        P(("group", "expert"), None),
        P(("group", "expert"), None),
        P(),
        P("expert", None, None),
        P("group", "expert", None, None, None),
    )
    return jax.shard_map(
        local,
        mesh=mesh,
        in_specs=placed,
        out_specs=(
            P(("group", "expert"), None),
            P("group", "expert", None, None, None),
            P("expert", "group", None),
        ),
        check_vma=False,
    )
```

```python
import functools
import itertools

import jax
import jax.numpy as jnp
import numpy as np
from jax import lax
from jax.experimental import pallas as pl
from jax.experimental.pallas import tpu as pltpu
from jax.sharding import PartitionSpec as P

HOT = 2
TILE = 512


def cost(flops):
    return pl.CostEstimate(flops=flops, bytes_accessed=flops // 300, transcendentals=0)
CHUNKS = (2048, 1024, 512)


def slot_layout(replica_plan):
    slot_count = replica_plan.shape[0]
    slot_ids = jnp.arange(slot_count, dtype=jnp.int32)
    same_expert = replica_plan[:, None] == replica_plan[None, :]
    earlier_slot = slot_ids[None, :] < slot_ids[:, None]
    ordinal = jnp.sum(same_expert & earlier_slot, axis=1)
    return (slot_ids, same_expert, ordinal)


def route_kernel(
    expert_count, cap_rows, seat, slot_plan, plan_row, routes, picks, gates, spread, rank_out, slot_out
):
    slot_count = plan_row.shape[1]
    top_count, tokens = routes.shape
    column = lax.broadcasted_iota(jnp.int32, (slot_count, 1), 0)
    plan = jnp.zeros((slot_count, 1), jnp.int32)
    for s in range(slot_count):
        plan = jnp.where(column == s, slot_plan[s], plan)
    same = plan == plan_row[...]
    slot_r = lax.broadcasted_iota(jnp.int32, (slot_count, slot_count), 0)
    slot_c = lax.broadcasted_iota(jnp.int32, (slot_count, slot_count), 1)
    copies = jnp.sum(jnp.where(same, 1.0, 0.0), axis=1, keepdims=True)
    ordinal = jnp.sum(jnp.where(same & (slot_c < slot_r), 1.0, 0.0), axis=1, keepdims=True)
    slot_ids = lax.broadcasted_iota(jnp.int32, (slot_count, tokens), 0)
    reach = jnp.zeros((slot_count, tokens), jnp.float32)
    gate_of = jnp.zeros((slot_count, tokens), jnp.float32)
    matches = []
    for k in range(top_count):
        route = routes[k : k + 1, :]
        pick = picks[k : k + 1, :].astype(jnp.float32)
        chosen = pick - copies * jnp.floor((pick + 0.5) / copies)
        match = (route == plan) & (chosen == ordinal) & (route < expert_count)
        matches.append(match)
        reach = jnp.where(match, 1.0, reach)
        gate_of = jnp.where(match, gates[k : k + 1, :], gate_of)
    before = lax.broadcasted_iota(jnp.int32, (tokens, tokens), 0) < lax.broadcasted_iota(
        jnp.int32, (tokens, tokens), 1
    )
    rank = lax.dot_general(
        reach.astype(jnp.bfloat16),
        jnp.where(before, 1.0, 0.0).astype(jnp.bfloat16),
        (((1,), (0,)), ((), ())),
        preferred_element_type=jnp.float32,
    ).astype(jnp.int32)
    kept = (reach > 0.0) & (rank < cap_rows)
    rank = jnp.where(kept, rank, -1)
    rank_out[...] = rank
    for k in range(top_count):
        slot_out[k : k + 1, :] = (
            jnp.sum(jnp.where(matches[k] & kept, slot_ids + 1, 0), axis=0, keepdims=True) - 1
        )
    row_ids = lax.broadcasted_iota(jnp.int32, spread.shape[1:], 0)
    for s in range(slot_count):
        placed = jnp.where(row_ids == rank[s : s + 1, :], gate_of[s : s + 1, :], 0.0)
        spread[seat[0] ^ s] = placed.astype(jnp.bfloat16)


def place_routes(routes, picks, gates, replica_plan, seat, expert_count, cap_rows, held_rows):
    slot_count = replica_plan.shape[0]
    top_count, tokens = routes.shape
    vmem = pl.BlockSpec(memory_space=pltpu.VMEM)
    return pl.pallas_call(
        functools.partial(route_kernel, expert_count, cap_rows),
        out_shape=(
            jax.ShapeDtypeStruct((slot_count, held_rows, tokens), jnp.bfloat16),
            jax.ShapeDtypeStruct((slot_count, tokens), jnp.int32),
            jax.ShapeDtypeStruct((top_count, tokens), jnp.int32),
        ),
        in_specs=[pl.BlockSpec(memory_space=pltpu.SMEM)] * 2 + [vmem] * 4,
        out_specs=(vmem, vmem, vmem),
    )(seat, replica_plan, replica_plan.reshape(1, slot_count), routes, picks, gates)


def send_all_kernel(seat, spread, rows, *rest):
    out = rest[-1]
    held_rows, tokens = spread.shape[1:]
    total = jnp.dot(spread[...].reshape(-1, tokens), rows[...], preferred_element_type=jnp.float32)
    for d in range(spread.shape[0]):
        out[seat[0] ^ d] = total[d * held_rows : (d + 1) * held_rows].astype(jnp.bfloat16)


def all_rows_to_send(spread, out_grad, seat, span, after):
    slot_count, held_rows, tokens = spread.shape
    start, stop = span
    return pl.pallas_call(
        send_all_kernel,
        grid=((stop - start) // TILE,),
        in_specs=[
            pl.BlockSpec(memory_space=pltpu.SMEM),
            pl.BlockSpec((slot_count, held_rows, tokens), lambda j: (0, 0, 0)),
            pl.BlockSpec((tokens, TILE), lambda j: (0, start // TILE + j)),
        ]
        + [pl.BlockSpec(memory_space=pl.ANY)] * len(after),
        out_specs=pl.BlockSpec((slot_count, held_rows, TILE), lambda j: (0, 0, j)),
        out_shape=jax.ShapeDtypeStruct((slot_count, held_rows, stop - start), jnp.bfloat16),
        cost_estimate=cost(2 * slot_count * held_rows * tokens * (stop - start)),
    )(seat, spread, out_grad, *after)


def part_kernel(leave, rows, *rest):
    flat = rows[...].reshape(-1, rows.shape[-1])
    rest[-1][...] = jnp.dot(leave[...], flat, preferred_element_type=jnp.float32).astype(jnp.bfloat16)


def other_core_part(leave, rows, after):
    slot_count, held_rows, width = rows.shape
    units, held = leave.shape
    return pl.pallas_call(
        part_kernel,
        grid=(width // TILE,),
        in_specs=[
            pl.BlockSpec((units, held), lambda j: (0, 0)),
            pl.BlockSpec((slot_count, held_rows, TILE), lambda j: (0, 0, j)),
        ]
        + [pl.BlockSpec(memory_space=pl.ANY)] * len(after),
        out_specs=pl.BlockSpec((units, TILE), lambda j: (0, j)),
        out_shape=jax.ShapeDtypeStruct((units, width), jnp.bfloat16),
        cost_estimate=cost(2 * units * held * width),
    )(leave, rows, *after)


def near_kernel(chips, stay, rows, near, *rest):
    mine, *others = rest[-chips:]
    flat = rows[...].reshape(-1, rows.shape[-1])
    shard = mine.shape[0]
    total = jnp.dot(stay[...], flat, preferred_element_type=jnp.float32) + near[...].astype(jnp.float32)
    mine[...] = total[:shard]
    for d, other in enumerate(others):
        other[...] = total[(d + 1) * shard : (d + 2) * shard].astype(jnp.bfloat16)


def add_near(stay, rows, near, chips, after):
    units, held = stay.shape
    width = rows.shape[-1]
    shard = units // chips
    return pl.pallas_call(
        functools.partial(near_kernel, chips),
        grid=(width // TILE,),
        in_specs=[
            pl.BlockSpec((units, held), lambda j: (0, 0)),
            pl.BlockSpec(rows.shape[:2] + (TILE,), lambda j: (0, 0, j)),
            pl.BlockSpec((units, TILE), lambda j: (0, j)),
        ]
        + [pl.BlockSpec(memory_space=pl.ANY)] * len(after),
        out_specs=(pl.BlockSpec((shard, TILE), lambda j: (0, j)),) * chips,
        out_shape=(jax.ShapeDtypeStruct((shard, width), jnp.float32),)
        + (jax.ShapeDtypeStruct((shard, width), jnp.bfloat16),) * (chips - 1),
        cost_estimate=cost(2 * units * held * width),
    )(stay, rows, near, *after)


def few_part(leave, rows, after):
    vmem = pl.BlockSpec(memory_space=pltpu.VMEM)
    return pl.pallas_call(
        part_kernel,
        in_specs=[vmem] * 2 + [pl.BlockSpec(memory_space=pl.ANY)] * len(after),
        out_specs=vmem,
        out_shape=jax.ShapeDtypeStruct((leave.shape[0], rows.shape[-1]), jnp.bfloat16),
        compiler_params=pltpu.CompilerParams(vmem_limit_bytes=32 * 1024 * 1024),
        cost_estimate=cost(2 * leave.size * rows.shape[-1]),
    )(leave, rows, *after)


def few_near(stay, rows, near, chips, after):
    shape = (stay.shape[0] // chips, rows.shape[-1])
    vmem = pl.BlockSpec(memory_space=pltpu.VMEM)
    return pl.pallas_call(
        functools.partial(near_kernel, chips),
        in_specs=[vmem] * 3 + [pl.BlockSpec(memory_space=pl.ANY)] * len(after),
        out_specs=(vmem,) * chips,
        out_shape=(jax.ShapeDtypeStruct(shape, jnp.float32),)
        + (jax.ShapeDtypeStruct(shape, jnp.bfloat16),) * (chips - 1),
        compiler_params=pltpu.CompilerParams(vmem_limit_bytes=32 * 1024 * 1024),
        cost_estimate=cost(2 * stay.size * rows.shape[-1]),
    )(stay, rows, near, *after)


def hold_kernel(*refs):
    pass


def hold(array, after):
    return pl.pallas_call(
        hold_kernel,
        in_specs=[pl.BlockSpec(memory_space=pl.ANY)] * (1 + len(after)),
        out_specs=pl.BlockSpec(memory_space=pl.ANY),
        out_shape=jax.ShapeDtypeStruct(array.shape, array.dtype),
        input_output_aliases={0: 0},
        cost_estimate=cost(1),
    )(array, *after)


def return_kernel(score, rank, slot_of, gates, out):
    slot_count, cap_rows = score.shape
    top_count, tokens = slot_of.shape
    row_ids = lax.broadcasted_iota(jnp.int32, (cap_rows, tokens), 0)
    total = jnp.zeros((top_count, tokens), jnp.float32)
    for s in range(slot_count):
        onehot = jnp.where(row_ids == rank[s : s + 1, :], 1.0, 0.0)
        value = lax.dot_general(
            score[s : s + 1, :],
            onehot,
            (((1,), (0,)), ((), ())),
            precision=lax.Precision.HIGHEST,
            preferred_element_type=jnp.float32,
        )
        total = jnp.where(slot_of[...] == s, value, total)
    held_gate = gates[...].astype(jnp.bfloat16).astype(jnp.float32)
    out[...] = jnp.where(slot_of[...] >= 0, total / held_gate, 0.0)


def matchings(slot_count):
    first = np.zeros((1 << slot_count,), np.int32)
    perms = []
    for four in itertools.combinations(range(slot_count), 4):
        first[sum(1 << s for s in four)] = len(perms)
        for other in range(3):
            rest = [four[1 + i] for i in range(3) if i != other]
            pairs = ((four[0], four[1 + other]), tuple(rest))
            perms.append([(a, b) for a, b in pairs] + [(b, a) for a, b in pairs])
    return first, perms


def matching_index(replica_plan, first):
    slot_ids, same_expert, ordinal = slot_layout(replica_plan)
    hot = jnp.sum(same_expert, axis=1) > 1
    mask = jnp.sum(jnp.where(hot, 1 << slot_ids, 0))
    least = jnp.min(jnp.where(hot, slot_ids, slot_ids.shape[0]))
    expert = jnp.sum(jnp.where(slot_ids == least, replica_plan, 0))
    partner = jnp.max(jnp.where(replica_plan == expert, slot_ids, 0))
    between = jnp.sum(hot & (slot_ids > least) & (slot_ids < partner))
    base = jnp.sum(jnp.where(jnp.arange(first.shape[0]) == mask, jnp.asarray(first), 0))
    return base + between


def sum_copies_any(group_sum, replica_plan):
    slot_ids, same_expert, ordinal = slot_layout(replica_plan)
    copies = jnp.sum(same_expert, axis=1)
    hot_first = (copies > 1) & (ordinal == 0)
    hot_rank = jnp.sum(hot_first[None, :] & (replica_plan[None, :] < replica_plan[:, None]), axis=1)
    my_slot = slot_ids == lax.axis_index("expert")
    my_rank = jnp.sum(jnp.where(my_slot, hot_rank, 0))
    my_hot = jnp.any(my_slot & (copies > 1))
    place_hot = (jnp.arange(HOT, dtype=jnp.int32) == my_rank) & my_hot
    group_f = group_sum.astype(jnp.float32)
    table = jnp.where(place_hot[:, None, None], group_f[None], 0.0)
    summed = lax.psum(table.astype(jnp.bfloat16), "expert").astype(jnp.float32)
    picked = jnp.sum(jnp.where(place_hot[:, None, None], summed, 0.0), axis=0)
    return jnp.where(my_hot, picked, group_f).astype(jnp.bfloat16)


def local(out_grad, gates, routes, copy_pick, replica_plan, down_weight, saved_hidden):
    slot_count = replica_plan.shape[0]
    cap_rows = saved_hidden.shape[3]
    expert_count = slot_count - slot_count // 4
    model_width = out_grad.shape[1]
    hidden_units = down_weight.shape[1]
    group_size = lax.axis_size("group")
    chips = group_size // 2
    shard_rows = hidden_units // group_size
    me = lax.axis_index("group")
    chip, core = me // 2, me % 2

    seat = lax.axis_index("expert").astype(jnp.int32).reshape(1)
    held_rows = -(-cap_rows // 16) * 16
    pad = ((0, 0), (0, held_rows - cap_rows), (0, 0))
    held_hidden = jnp.pad(saved_hidden[0, 0], pad).reshape(slot_count * held_rows, hidden_units)

    spread, rank, slot_of = place_routes(
        routes.T, copy_pick.T, gates.T, replica_plan, seat, expert_count, cap_rows, held_rows
    )

    by_owner = held_hidden.T.reshape(chips, 2, shard_rows, -1)
    by_owner = jnp.stack([by_owner[chip ^ d] for d in range(chips)])
    stay = by_owner[:, core].reshape(hidden_units // 2, -1)
    leave = by_owner[:, 1 - core].reshape(hidden_units // 2, -1)

    edges = np.cumsum((0,) + CHUNKS)
    spans = [(int(a), int(b)) for a, b in zip(edges[:-1], edges[1:])]
    ready = [all_rows_to_send(spread, out_grad, seat, span, []) for span in spans]
    pairs = slot_count - expert_count == HOT
    if pairs:
        first, perms = matchings(slot_count)
        pairing = matching_index(replica_plan, first)
    group_sum, projected = [], jnp.zeros((slot_count * held_rows, hidden_units), jnp.float32)
    rows, far, others = None, [], []
    early = ready[2:] + ([pairing.reshape(1)] if pairs else [])
    for span, sent in zip(spans, ready):
        if rows is not None:
            sent = hold(sent, early if others else [rows] + early)
            early = others[:1] + [projected]
        rows = lax.all_to_all(sent, "expert", split_axis=0, concat_axis=0, tiled=True)
        few = span != spans[0]
        away = (few_part if few else other_core_part)(leave, rows, others[:1])
        near = lax.ppermute(away, "group", [(i, i ^ 1) for i in range(group_size)])
        mine, *others = (few_near if few else add_near)(stay, rows, near, chips, far[:1])
        far = [
            lax.ppermute(other, "group", [(i, i ^ (2 * d + 2)) for i in range(group_size)])
            for d, other in enumerate(others)
        ]
        group_sum.append(sum((f.astype(jnp.float32) for f in far), mine).astype(jnp.bfloat16))
        projected = projected + lax.dot_general(
            rows.reshape(slot_count * held_rows, -1),
            down_weight[0, :, span[0] : span[1]],
            (((1,), (1,)), ((), ())),
            preferred_element_type=jnp.float32,
        )

    route_score = jnp.sum(projected * held_hidden.astype(jnp.float32), axis=1)
    returned = lax.all_to_all(
        hold(route_score.reshape(slot_count, held_rows), others[:1]),
        "expert",
        split_axis=0,
        concat_axis=0,
        tiled=True,
    )
    route_grad = pl.pallas_call(
        return_kernel, out_shape=jax.ShapeDtypeStruct(gates.T.shape, jnp.float32)
    )(returned, rank, slot_of, gates.T).T
    hidden_grad = projected.astype(jnp.bfloat16).reshape(slot_count, held_rows, hidden_units)[:, :cap_rows]

    group_sum = jnp.concatenate(group_sum, axis=1)
    if pairs:
        other = lax.switch(
            pairing,
            [functools.partial(lax.ppermute, axis_name="expert", perm=perm) for perm in perms],
            group_sum,
        )
        copy_grad = (group_sum.astype(jnp.float32) + other.astype(jnp.float32)).astype(jnp.bfloat16)
    else:
        copy_grad = sum_copies_any(group_sum, replica_plan)
    return (route_grad, hidden_grad[None, None], copy_grad.reshape(1, shard_rows, model_width))


def solution(mesh):
    placed = (
        P(("group", "expert"), None),
        P(("group", "expert"), None),
        P(("group", "expert"), None),
        P(("group", "expert"), None),
        P(),
        P("expert", None, None),
        P("group", "expert", None, None, None),
    )
    return jax.shard_map(
        local,
        mesh=mesh,
        in_specs=placed,
        out_specs=(
            P(("group", "expert"), None),
            P("group", "expert", None, None, None),
            P("expert", "group", None),
        ),
        check_vma=False,
    )
```
